256 devices in a mesh: gx: 8 (over z), gy: 16 (over y, x), gz: 2 (over core).
Axes of the slice: x: 4, y: 4, z: 8, core: 2. Of those that a mesh axis runs over, the one named last changes fastest.
Arguments:
- forcing: float32 [3, 128, 256, 256], P(None, 'gx', 'gy', 'gz'), may hold values from -6 to 6
- start_field: float32 [3, 128, 256, 256], P(None, 'gx', 'gy', 'gz'), may hold values from -6 to 6
- modulus: float32 [128, 256, 256], P('gx', 'gy', 'gz'), may hold values from 1 to 4
- corners: int32 [256, 3], P(('gx', 'gy', 'gz')), may hold values from 0 to 236, as said below
Outputs:
- displacement: float32 [3, 128, 256, 256], P(None, 'gx', 'gy', 'gz')
- new_modulus: float32 [128, 256, 256], P('gx', 'gy', 'gz')
The draws below stay inside these ranges and needn't reach their ends.
Inputs may be any that keep to these rules, and one draw needn't show every extreme that they name: `corners`: subzone i is handled by device i // 1 in row-major order over (gx, gy, gz). In each dimension its corner lies within lo - 5 to lo + B + 5 - 2 * 10, where lo and B are that device's first voxel and voxel count in that dimension, and the subzone lies inside the grid.
All inputs are finite; a program needn't handle non-finite values.
Results may differ from the reference program's by a relative error of at most 0.0003.
Values sent between devices are 32-bit elements; how exact they have to be, the bound alone decides.
No kernel may reach another device: no remote copies, remote signals or barrier semaphores. Data moves between devices by JAX's collectives and lax.ppermute only.
A program may use at most 192 MiB of HBM per device.

```python
import math
import jax
import jax.numpy as jnp
from jax import lax

BX = 16
BY = 16
BZ = 128
SUB_DEV = 1
PC = 10
HALO = 6
FSWEEPS = 4
NX = 128
NY = 256
NZ = 256
NSUB = 256
N_GY = 16
N_GZ = 2


def draw_corners(key, part):
    number = jnp.arange(NSUB, dtype=jnp.int32)
    device = number // SUB_DEV
    brick_x = device // (N_GY * N_GZ)
    brick_y = device // N_GZ % N_GY
    brick_z = device % N_GZ
    lower = jnp.stack([brick_x * BX, brick_y * BY, brick_z * BZ], axis=1)
    counts = jnp.array([BX + 2 * HALO - 1 - 2 * PC, BY + 2 * HALO - 1 - 2 * PC, BZ + 2 * HALO - 1 - 2 * PC], jnp.int32)
    offsets = jax.random.randint(key, (NSUB, 3), jnp.zeros((1, 3), jnp.int32), counts[None, :])
    corner_raw = lower - HALO + 1 + offsets
    upper_limit = jnp.array([NX, NY, NZ], jnp.int32) - 2 * PC
    return jnp.clip(corner_raw, 0, upper_limit[None, :]).astype(jnp.int32)


def block_amplitude(key):
    cell_x = (NX + 3) // 4
    cell_y = (NY + 3) // 4
    cell_z = (NZ + 3) // 4
    exponent = jax.random.uniform(jax.random.fold_in(key, 11), (cell_x, cell_y, cell_z), jnp.float32, -4.0, 0.0)
    amplitude = jnp.exp(exponent)
    amplitude = jnp.repeat(jnp.repeat(jnp.repeat(amplitude, 4, axis=0), 4, axis=1), 4, axis=2)
    return amplitude[:NX, :NY, :NZ]


def modulated_field(key, draw_tag):
    amplitude = block_amplitude(key)
    inner_key = jax.random.fold_in(key, draw_tag)
    samples = jax.random.normal(inner_key, (3, NX, NY, NZ), jnp.float32)
    return jnp.clip(samples * amplitude[None], -6.0, 6.0).astype(jnp.float32)


def draw_forcing(key, part):
    return modulated_field(key, 21)


def draw_start_field(key, part):
    return modulated_field(key, 37)


def shard_levels(stream_key, extent, split, low, largest):
    factor_of, own = 1.0, jax.random.fold_in(stream_key, 6)
    for dim, shards_of in split:
        steps = jnp.exp(jax.random.uniform(jax.random.fold_in(own, dim), (shards_of,), jnp.float32, low / len(split), largest / len(split)))
        factor_of = factor_of * jnp.repeat(steps, extent[dim] // shards_of).reshape([-1 if axis == dim else 1 for axis in range(len(extent))])
    return factor_of


def setup_inputs(seed: int = 0) -> dict:
    arg_keys = jax.random.split(jax.random.key(seed), 5)
    forcing = draw_forcing(jax.random.fold_in(arg_keys[4], 71), 0)
    start_field = draw_start_field(jax.random.fold_in(arg_keys[4], 71), 0)
    modulus = jnp.clip(jnp.exp(math.log(4.0) - 1.3862944 * jax.random.uniform(arg_keys[2], (NX, NY, NZ), jnp.float32) ** shard_levels(arg_keys[2], (NX, NY, NZ), ((0, 8), (1, 16), (2, 2)), -0.2, 0.2)), 1.0, 4.0)
    corners = draw_corners(jax.random.fold_in(arg_keys[4], 71), 0)
    return dict(forcing=forcing, start_field=start_field, modulus=modulus, corners=corners)


MASS_TERM = 0.5
DAMPING = 0.1
EPSILON = 1e-06
DIRECTIONS = ((0, True), (0, False), (1, True), (1, False), (2, True), (2, False))

def neighbor(values, which_axis, upward):
    index_list = [slice(1, -1), slice(1, -1), slice(1, -1)]
    index_list[which_axis] = slice(2, None) if upward else slice(0, -2)
    return values[tuple([slice(None)] * (values.ndim - 3) + index_list)]

def center(values):
    return values[tuple([slice(None)] * (values.ndim - 3) + [slice(1, -1)] * 3)]

def relax_sweep(field_pad, modulus_pad, forcing_mid):
    middle = center(modulus_pad)
    numerator = forcing_mid
    denominator = MASS_TERM
    for which_axis, upward in DIRECTIONS:
        coupling = 0.5 * (middle + neighbor(modulus_pad, which_axis, upward))
        numerator = numerator + coupling * neighbor(field_pad, which_axis, upward)
        denominator = denominator + coupling
    return numerator / denominator

def block_sum(values, coarse):
    return values.reshape(values.shape[0], coarse, 2, coarse, 2, coarse, 2).sum(axis=(2, 4, 6))

def shift_coarse(values, offset):
    padded = jnp.pad(values, 1)
    coarse = values.shape[0]
    begin = (1 - offset[0], 1 - offset[1], 1 - offset[2])
    return lax.slice(padded, begin, (begin[0] + coarse, begin[1] + coarse, begin[2] + coarse))

def zone_update(field_rim, forcing_zone, modulus_rim):
    zone_span = forcing_zone.shape[-1]
    coarse = zone_span // 2
    params = coarse ** 3
    field_mid = center(field_rim)
    modulus_mid = center(modulus_rim)
    applied = MASS_TERM * field_mid
    laplace = jnp.zeros_like(field_mid)
    face_flows = []
    for which_axis, upward in DIRECTIONS:
        field_next = neighbor(field_rim, which_axis, upward)
        modulus_next = neighbor(modulus_rim, which_axis, upward)
        change = field_mid - field_next
        applied = applied + 0.5 * (modulus_mid + modulus_next) * change
        laplace = laplace + change
        face_flows.append(-0.5 * modulus_next * change)
    coarse_resid = block_sum(forcing_zone - applied, coarse)
    diagonal = block_sum(-0.5 * modulus_mid * laplace, coarse)
    position = jnp.arange(coarse)
    columns = {}
    for (which_axis, upward), face_flow in zip(DIRECTIONS, face_flows):
        blocks = face_flow.reshape(3, coarse, 2, coarse, 2, coarse, 2)
        inner_pos = 0 if upward else 1
        same_part = lax.index_in_dim(blocks, inner_pos, 2 + 2 * which_axis, keepdims=True).sum(axis=(2, 4, 6))
        cross_part = lax.index_in_dim(blocks, 1 - inner_pos, 2 + 2 * which_axis, keepdims=True).sum(axis=(2, 4, 6))
        diagonal = diagonal + same_part
        in_range = position < coarse - 1 if upward else position > 0
        shape_list = [1, 1, 1]
        shape_list[which_axis] = coarse
        in_range = in_range.reshape(shape_list)
        step_list = [0, 0, 0]
        step_list[which_axis] = 1 if upward else -1
        columns[tuple(step_list)] = jnp.where(in_range, cross_part, 0.0)
    columns[0, 0, 0] = diagonal
    offset_list = list(columns.keys())
    gradient = jnp.zeros((coarse, coarse, coarse), jnp.float32)
    band_sums = {}
    for offset_one in offset_list:
        gradient = gradient + shift_coarse(jnp.sum(columns[offset_one] * coarse_resid, axis=0), offset_one)
        for offset_two in offset_list:
            band_key = (offset_two[0] - offset_one[0], offset_two[1] - offset_one[1], offset_two[2] - offset_one[2])
            term_value = shift_coarse(jnp.sum(columns[offset_one] * columns[offset_two], axis=0), offset_one)
            if band_key in band_sums:
                band_sums[band_key] = band_sums[band_key] + term_value
            else:
                band_sums[band_key] = term_value
    base_rows = jnp.arange(params, dtype=jnp.int32)
    row_parts = []
    col_parts = []
    value_parts = []
    for band_key, band_value in band_sums.items():
        linear = band_key[0] * coarse * coarse + band_key[1] * coarse + band_key[2]
        target = base_rows + linear
        target = jnp.where((target >= 0) & (target < params), target, params).astype(jnp.int32)
        row_parts.append(base_rows)
        col_parts.append(target)
        value_parts.append(band_value.reshape(params))
    hessian = jnp.zeros((params, params), jnp.float32).at[jnp.concatenate(row_parts), jnp.concatenate(col_parts)].add(jnp.concatenate(value_parts), mode='drop')
    ridge = DAMPING * jnp.sum(band_sums[0, 0, 0]) / params + EPSILON
    hessian = hessian + ridge * jnp.eye(params, dtype=jnp.float32)
    factor = jnp.linalg.cholesky(hessian)
    right_hand = gradient.reshape(params, 1)
    middle_sol = lax.linalg.triangular_solve(factor, right_hand, left_side=True, lower=True)
    solution = lax.linalg.triangular_solve(factor, middle_sol, left_side=True, lower=True, transpose_a=True)
    update = -solution.reshape(coarse, coarse, coarse)
    update = jnp.repeat(jnp.repeat(jnp.repeat(update, 2, axis=0), 2, axis=1), 2, axis=2)
    ramp_curve = jnp.sin(math.pi * (jnp.arange(zone_span, dtype=jnp.float32) + 0.5) / zone_span)
    taper_weight = ramp_curve[:, None, None] * ramp_curve[None, :, None] * ramp_curve[None, None, :]
    return taper_weight * modulus_mid * update

def reference(forcing, start_field, modulus, corners):
    zone_span = 2 * PC
    field = start_field
    modulus_pad = jnp.pad(modulus, 1)
    for sweep_count in range(FSWEEPS):
        field = relax_sweep(jnp.pad(field, ((0, 0), (1, 1), (1, 1), (1, 1))), modulus_pad, forcing)
    field_pad = jnp.pad(field, ((0, 0), (1, 1), (1, 1), (1, 1)))
    anchor = jnp.zeros((), jnp.int32)

    def one_zone(corner):
        corner = corner.astype(jnp.int32)
        field_rim = lax.dynamic_slice(field_pad, (anchor, corner[0], corner[1], corner[2]), (3, zone_span + 2, zone_span + 2, zone_span + 2))
        modulus_rim = lax.dynamic_slice(modulus_pad, (corner[0], corner[1], corner[2]), (zone_span + 2, zone_span + 2, zone_span + 2))
        forcing_zone = lax.dynamic_slice(forcing, (anchor, corner[0], corner[1], corner[2]), (3, zone_span, zone_span, zone_span))
        return zone_update(field_rim, forcing_zone, modulus_rim)
    pieces = lax.map(one_zone, corners)

    def add_piece(number, total):
        corner = corners[number].astype(jnp.int32)
        begin = (corner[0], corner[1], corner[2])
        current = lax.dynamic_slice(total, begin, (zone_span, zone_span, zone_span))
        return lax.dynamic_update_slice(total, current + pieces[number], begin)
    total = lax.fori_loop(0, corners.shape[0], add_piece, jnp.zeros(modulus.shape, jnp.float32))
    return (field, modulus + total)
```

```python
import functools
import math

import jax
import jax.numpy as jnp
from jax import lax
from jax.experimental import pallas as pl
from jax.experimental.pallas import tpu as pltpu
from jax.sharding import PartitionSpec as P

PC = 10
SPAN = 2 * PC
FSWEEPS = 4
MASS_TERM = 0.5
DAMPING = 0.1
EPSILON = 1e-06
BX, BY, BZ = 16, 16, 128
DEEP = 10
WIN = 30
WY = 32
AX = 24
ROWS = 104
TILES = ROWS // 8
PLANES = 3 * DEEP + 3 * (DEEP - 1) + DEEP
AXES = ("gx", "gy", "gz")
F32 = jnp.float32
BF16 = jnp.bfloat16
HIGH = lax.Precision.HIGHEST
VMEM_LIMIT = 48 * 1024 * 1024


def iota(shape, dim):
    return lax.broadcasted_iota(jnp.int32, shape, dim)


def lane_roll(values, shift):
    if isinstance(shift, int):
        shift = shift % values.shape[-1]
        return values if shift == 0 else pltpu.roll(values, shift, values.ndim - 1)
    size = values.shape[-1]
    return pltpu.roll(values, lax.rem(shift + 8 * size, size), values.ndim - 1)


def row_roll(values, shift):
    if isinstance(shift, int):
        shift = shift % values.shape[-2]
        return values if shift == 0 else pltpu.roll(values, shift, values.ndim - 2)
    size = values.shape[-2]
    return pltpu.roll(values, lax.rem(shift + 8 * size, size), values.ndim - 2)


def three_parts(values):
    first = values.astype(BF16)
    rest = values - first.astype(F32)
    second = rest.astype(BF16)
    third = (rest - second.astype(F32)).astype(BF16)
    return first, second, third


def dot(a, b):
    return lax.dot_general(a, b, (((1,), (0,)), ((), ())), precision=HIGH, preferred_element_type=F32)


def dot_exact(values, selector):
    parts = [
        lax.dot_general(part, selector, (((1,), (0,)), ((), ())), preferred_element_type=F32)
        for part in three_parts(values)
    ]
    return parts[0] + parts[1] + parts[2]


def div10(value):
    return lax.shift_right_arithmetic(value * 205, 11)


def edge_kernel(sc, u, f, m, msg1, msg2, strip, strip1, strip2):
    gz = sc[0]
    low_first = gz == 0
    s1 = jnp.where(low_first, BX - DEEP, 0)
    s2 = BX - DEEP - s1
    f1 = jnp.where(low_first, BX - DEEP + 1, 0)
    f2 = BX - DEEP + 1 - f1
    for out, s, fs in ((msg1, s1, f1), (msg2, s2, f2)):
        for k in range(3):
            out[k * DEEP : (k + 1) * DEEP] = u[k, pl.ds(s, DEEP)]
            base = 3 * DEEP + k * (DEEP - 1)
            out[base : base + DEEP - 1] = f[k, pl.ds(fs, DEEP - 1)]
        out[PLANES - DEEP : PLANES] = m[pl.ds(s, DEEP)]
    lane = iota((BY, 128), 1)
    extra = jnp.where(low_first, DEEP, 0)

    def one(x, carry):
        total = jnp.zeros((BY, 128), F32)
        for c in range(7):
            source = u[c, x] if c < 3 else (f[c - 3, x] if c < 6 else m[x])
            moved = lane_roll(source, extra + DEEP * c)
            total = jnp.where((lane >= DEEP * c) & (lane < DEEP * (c + 1)), moved, total)
        strip[x] = total
        return carry

    lax.fori_loop(0, BX, one, 0)
    strip1[...] = strip[pl.ds(s1, DEEP)]
    strip2[...] = strip[pl.ds(s2, DEEP)]


def pack_kernel(sc, u, f, m, x1, x2, strip, strip1, strip2, own_u, own_f, msg1, msg2, side1, side2, eu, ef, em, es):
    gz = sc[0]
    low_first = gz == 0
    p1 = jnp.where(low_first, 0, BX + DEEP)
    p2 = BX + DEEP - p1
    q1 = jnp.where(low_first, 1, BX + DEEP)
    q2 = BX + DEEP + 1 - q1
    for k in range(3):
        eu[k, DEEP : DEEP + BX] = u[k]
        ef[k, DEEP : DEEP + BX] = f[k]
        ef[k, 0] = jnp.zeros((BY, 128), F32)
        ef[k, 2 * DEEP + BX - 1] = jnp.zeros((BY, 128), F32)
        for msg, p, q in ((x1, p1, q1), (x2, p2, q2)):
            eu[k, pl.ds(p, DEEP)] = msg[k * DEEP : (k + 1) * DEEP]
            base = 3 * DEEP + k * (DEEP - 1)
            ef[k, pl.ds(q, DEEP - 1)] = msg[base : base + DEEP - 1]
    em[DEEP : DEEP + BX] = m[...]
    es[DEEP : DEEP + BX] = strip[...]
    em[pl.ds(p1, DEEP)] = x1[PLANES - DEEP : PLANES]
    em[pl.ds(p2, DEEP)] = x2[PLANES - DEEP : PLANES]
    es[pl.ds(p2, DEEP)] = strip1[...]
    es[pl.ds(p1, DEEP)] = strip2[...]

    lane = iota((BY, 128), 1)
    group = lax.shift_right_arithmetic(lane, 5)
    inner = lane & 31
    zoff = jnp.where(low_first, BZ, -DEEP)

    def window(relz):
        w0 = relz - (DEEP - 5)
        z = inner + w0
        main_ok = (z >= 0) & (z < BZ)
        strip_ok = (z >= zoff) & (z < zoff + DEEP)

        def take(x):
            side = es[x]
            values = []
            for sources in ((eu, 0), (ef, 3)):
                ref, first = sources
                main = jnp.zeros((BY, 128), F32)
                far = jnp.zeros((BY, 128), F32)
                for k in range(4 if first == 0 else 3):
                    source, c = (ref[k, x], first + k) if k < 3 else (em[x], 6)
                    main = jnp.where(group == k, lane_roll(source, 32 * k - w0), main)
                    far = jnp.where(group == k, lane_roll(side, 32 * k + zoff - w0 - DEEP * c), far)
                values.append(jnp.where(main_ok, main, jnp.where(strip_ok, far, 0.0)))
            return values

        return take

    take_own = window(sc[3])
    x0 = sc[1] + 5

    def own(i, carry):
        field, force = take_own(x0 + i)
        own_u[i] = field
        own_f[i] = force
        return carry

    lax.fori_loop(0, WIN, own, 0)

    sub = iota((8, 128), 0)
    for msg, side, base, upward in ((msg1, side1, 4, low_first), (msg2, side2, 7, gz != 0)):
        take = window(sc[base + 2])
        start = sc[base] + 5

        def pair(i, carry, msg=msg, take=take, start=start, upward=upward):
            mixed = jnp.zeros((8, 128), F32)
            number = 0
            for step in range(2):
                for values in take(start + 2 * i + step):
                    top, bottom = values[0:8], values[8:16]
                    msg[i, 8 * number : 8 * number + 8] = jnp.where(upward, bottom, top)
                    edge = jnp.where(upward, row_roll(top, 2), bottom)
                    mixed = jnp.where((sub >= 2 * number) & (sub < 2 * number + 2), row_roll(edge, 2 * number), mixed)
                    number += 1
            msg[i, 32:40] = mixed
            return carry

        lax.fori_loop(0, WIN // 2, pair, 0)

        def plane(i, carry, side=side, upward=upward):
            x = i + DEEP - FSWEEPS

            def edge(values):
                return jnp.where(upward, row_roll(values[8:16], 4), values[0:8])

            every = [edge(eu[k, x]) for k in range(3)] + [edge(ef[k, x]) for k in range(3)] + [edge(em[x]), edge(es[x])]
            for j in range(4):
                side[i, 8 * j : 8 * j + 8] = jnp.where(sub < 4, every[2 * j], row_roll(every[2 * j + 1], 4))
            return carry

        lax.fori_loop(0, AX, plane, 0)


def invert(chains):
    sub = iota((8, 128), 0)
    lane = iota((8, 128), 1)

    def row_of(values, j):
        return jnp.broadcast_to(values[j : j + 1, :], (8, 128))

    def column_of(values, j):
        return jnp.broadcast_to(values[:, j : j + 1], (8, 128))

    for b in range(TILES):
        in_block = (lane >= 8 * b) & (lane < 8 * b + 8)
        for chain in chains:
            columns = [[column_of(tile, 8 * b + j) for j in range(8)] for tile in chain]
            pivot = chain[b]
            own = columns[b]
            for j in range(8):
                at = lane == 8 * b + j
                scale = 1.0 / row_of(own[j], j)
                line = jnp.where(at, 1.0, row_of(pivot, j)) * scale
                pivot = jnp.where(sub == j, line, jnp.where(at, 0.0, pivot) - own[j] * line)
                for n in range(j + 1, 8):
                    other = row_of(own[n], j) * scale
                    own[n] = jnp.where(sub == j, other, own[n] - own[j] * other)
            lines = [row_of(pivot, j) for j in range(8)]
            for i in range(TILES):
                if i != b:
                    tile = jnp.where(in_block, 0.0, chain[i])
                    for j in range(8):
                        tile = tile - columns[i][j] * lines[j]
                    chain[i] = tile
            chain[b] = pivot
    return chains


OFFSETS = (0, PC, -PC, 1, -1)
BANDS = (0, 1, 2, 9, 10, 11, 20)


def zone_kernel(
    sizes, sc, own_u, own_f, r1, r2, out,
    ua, ub, fo, m3, cx, cy, cz, iv, rows, band, up, down, far, grad, hess, bl, br, yt, zs, dl, gs,
):
    nx, ny, nz = sizes
    low_first = sc[0] == 0
    rely = sc[2]
    lane32 = iota((WY, 128), 1)
    group = lax.shift_right_arithmetic(lane32, 5)
    inner = lane32 & 31
    row32 = iota((WY, 128), 0)
    shift = -(rely + 11)

    def unpack(i, carry):
        for step in range(2):
            for which in range(2):
                number = 2 * step + which
                first = r1[i, 8 * number : 8 * number + 8]
                second = r2[i, 8 * number : 8 * number + 8]
                mix1 = r1[i, 32:40]
                mix2 = r2[i, 32:40]
                low, high = jnp.where(low_first, first, second), jnp.where(low_first, second, first)
                low_mix, high_mix = jnp.where(low_first, mix1, mix2), jnp.where(low_first, mix2, mix1)
                middle = own_u[2 * i + step] if which == 0 else own_f[2 * i + step]
                tall = jnp.concatenate(
                    [row_roll(low_mix, 6 - 2 * number), low, middle, high, row_roll(high_mix, -2 * number)], axis=0
                )
                tall = row_roll(tall, shift)[0:WY]
                if which == 0:
                    ua[2 * i + step] = tall
                    moved = jnp.where(group == 0, lane_roll(tall, 32), 0.0)
                    moved = jnp.where(group == 1, lane_roll(tall, 64), moved)
                    m3[2 * i + step] = jnp.where(group == 2, lane_roll(tall, 96), moved)
                else:
                    fo[2 * i + step] = tall
        return carry

    lax.fori_loop(0, WIN // 2, unpack, 0)

    inside_y = sc[11] - 5 + row32
    inside_z = sc[12] - 5 + inner
    inside = (inside_y >= 0) & (inside_y < ny) & (inside_z >= 0) & (inside_z < nz)

    def faces(i, carry):
        here = m3[i]
        cx[i] = 0.5 * (here + m3[jnp.minimum(i + 1, WIN - 1)])
        cy[i] = 0.5 * (here + row_roll(here, -1))
        cz[i] = 0.5 * (here + lane_roll(here, -1))
        return carry

    lax.fori_loop(0, WIN, faces, 0)

    def scale(i, carry):
        total = MASS_TERM + cx[i] + cx[i - 1] + cy[i] + row_roll(cy[i], 1) + cz[i] + lane_roll(cz[i], 1)
        gx = sc[10] - 5 + i
        good = inside & (gx >= 0) & (gx < nx)
        iv[i] = jnp.where(good, 1.0 / total, 0.0)
        return carry

    lax.fori_loop(1, WIN - 1, scale, 0)

    for sweep in range(FSWEEPS):
        src, dst = (ua, ub) if sweep % 2 == 0 else (ub, ua)

        def relax(i, carry, src=src, dst=dst):
            here = src[i]
            total = fo[i] + cx[i] * src[i + 1] + cx[i - 1] * src[i - 1]
            total = total + cy[i] * row_roll(here, -1) + row_roll(cy[i] * here, 1)
            total = total + cz[i] * lane_roll(here, -1) + lane_roll(cz[i] * here, 1)
            dst[i] = total * iv[i]
            return carry

        lax.fori_loop(sweep + 1, WIN - 1 - sweep, relax, 0)

    line = iota((128, 384), 0)
    column = iota((128, 384), 1)
    part = lax.shift_right_arithmetic(column, 7)
    spot = column & 127
    spot_y = div10(spot)
    spot_z = spot - PC * spot_y
    inner_z = (line & 31) - 5
    hit = (lax.shift_right_arithmetic(line, 5) == part) & (inner_z >= 0) & (inner_z < SPAN) & (spot < PC * PC)
    hit = hit & (lax.shift_right_arithmetic(inner_z, 1) == spot_z)
    selector = jnp.where(hit, 1.0, 0.0).astype(BF16)
    zone_y = row32 - 5
    lane_y = div10(lane32)
    pick_y = (zone_y >= 0) & (zone_y < SPAN) & (lax.shift_right_arithmetic(zone_y, 1) == lane_y) & (lane32 < PC * PC)
    pick_y = jnp.where(pick_y, 1.0, 0.0)
    even_y = (zone_y & 1) == 0
    even_z = ((inner - 5) & 1) == 0
    rows[...] = jnp.zeros(rows.shape, F32)

    def layer(a, carry):
        sums = None
        for odd in range(2):
            i = 5 + 2 * a + odd
            here, m_here = ua[i], m3[i]
            ch_x, ch_b = here - ua[i + 1], ua[i - 1] - here
            ch_y = here - row_roll(here, -1)
            ch_z = here - lane_roll(here, -1)
            flow_y, flow_z = cy[i] * ch_y, cz[i] * ch_z
            applied = MASS_TERM * here + cx[i] * ch_x - cx[i - 1] * ch_b
            applied = applied + flow_y - row_roll(flow_y, 1) + flow_z - lane_roll(flow_z, 1)
            resid = fo[i] - applied
            back_y, back_z = row_roll(ch_y, 1), lane_roll(ch_z, 1)
            laplace = ch_x - ch_b + ch_y - back_y + ch_z - back_z
            xp = -0.5 * m3[i + 1] * ch_x
            xm = 0.5 * m3[i - 1] * ch_b
            yp = -0.5 * row_roll(m_here, -1) * ch_y
            ym = 0.5 * row_roll(m_here, 1) * back_y
            zp = -0.5 * lane_roll(m_here, -1) * ch_z
            zm = 0.5 * lane_roll(m_here, 1) * back_z
            diag = -0.5 * m_here * laplace + jnp.where(even_y, yp, ym) + jnp.where(even_z, zp, zm)
            diag = diag + (xm if odd else xp)
            now = [
                diag, xp if odd else None, None if odd else xm,
                jnp.where(even_y, 0.0, yp), jnp.where(even_y, ym, 0.0),
                jnp.where(even_z, 0.0, zp), jnp.where(even_z, zm, 0.0), resid,
            ]
            if sums is None:
                sums = now
            else:
                sums = [p if q is None else (q if p is None else p + q) for p, q in zip(sums, now)]
        tall = dot_exact(jnp.concatenate(sums, axis=0), selector)
        for n in range(8):
            for k in range(3):
                piece = tall[n * WY : (n + 1) * WY, 128 * k : 128 * k + 128] * pick_y
                rows[n, k, pl.ds(a, 1), :] = jnp.sum(piece, axis=0, keepdims=True)
        return carry

    lax.fori_loop(0, PC, layer, 0)

    lane16 = iota((16, 128), 1)
    row16 = iota((16, 128), 0)
    at_y = div10(lane16)
    at_z = lane16 - PC * at_y

    def masked(n, keep):
        return [jnp.where(keep, rows[n, k], 0.0) for k in range(3)]

    full = row16 < PC
    v = {
        0: masked(0, full),
        PC: masked(3, full & (at_y < PC - 1)),
        -PC: masked(4, full & (at_y > 0)),
        1: masked(5, full & (at_z < PC - 1)),
        -1: masked(6, full & (at_z > 0)),
    }
    vxp = masked(1, row16 < PC - 1)
    vxm = masked(2, full & (row16 > 0))
    res = masked(7, full)

    def mix(p, q):
        return p[0] * q[0] + p[1] * q[1] + p[2] * q[2]

    bands = {}
    for o1 in OFFSETS:
        for o2 in OFFSETS:
            key = o1 - o2
            if key >= 0:
                term = lane_roll(mix(v[o1], v[o2]), o2)
                bands[key] = bands[key] + term if key in bands else term
    bands[0] = bands[0] + row_roll(mix(vxp, vxp), 1) + row_roll(mix(vxm, vxm), -1)
    trace = jnp.sum(jnp.sum(bands[0], axis=1, keepdims=True), axis=0, keepdims=True)
    ridge = DAMPING * trace / PC**3 + EPSILON
    bands[0] = jnp.where(lane16 < PC * PC, bands[0] + ridge, jnp.where(lane16 < ROWS, 1.0, 0.0))
    slots = {}
    for n, key in enumerate(BANDS):
        band[n] = bands[key]
        slots[key] = n
    for n, key in enumerate(BANDS[1:]):
        band[len(BANDS) + n] = lane_roll(bands[key], key)
        slots[-key] = len(BANDS) + n
    for n, key in enumerate(OFFSETS):
        above = row_roll(mix(vxm, v[-key]), -1)
        below = row_roll(mix(vxp, v[-key]), 1)
        up[n] = mix(vxp, v[key]) + lane_roll(above, -key)
        down[n] = mix(vxm, v[key]) + lane_roll(below, -key)
    cross = mix(vxm, vxp)
    far[0] = row_roll(cross, -1)
    far[1] = row_roll(cross, 1)
    gradient = row_roll(mix(vxp, res), 1) + row_roll(mix(vxm, res), -1)
    for key in OFFSETS:
        gradient = gradient + lane_roll(mix(v[key], res), key)
    grad[...] = gradient

    sub = iota((8, 128), 0)
    lane8 = iota((8, 128), 1)

    def spread(ref, n, x):
        return jnp.broadcast_to(ref[n, pl.ds(x, 1), :], (8, 128))

    def fill(dst, lines, lead):
        for r in range(TILES):
            apart = sub + 8 * r - lane8
            tile = jnp.zeros((8, 128), F32)
            for key, values in lines:
                if 8 * r + 7 - key >= 0 and 8 * r - key < 128:
                    tile = jnp.where(apart == key, values, tile)
            dst[lead + (slice(8 * r, 8 * r + 8), slice(None))] = tile
        dst[lead + (slice(ROWS, 128), slice(None))] = jnp.zeros((128 - ROWS, 128), F32)

    def dense(x, carry):
        fill(hess, [(key, spread(band, n, x)) for key, n in slots.items()], (x,))
        gs[x] = jnp.broadcast_to(grad[pl.ds(x, 1), :], (8, 128))
        return carry

    lax.fori_loop(0, PC, dense, 0)

    def couple(t, carry):
        right = PC - 1 - t
        fill(bl, [(key, spread(up, n, t)) for n, key in enumerate(OFFSETS)], (t, 0))
        fill(bl, [(key, spread(down, n, t + 1)) for n, key in enumerate(OFFSETS)], (t, 1))

        @pl.when(t < 4)
        def _():
            fill(br, [(key, spread(down, n, right)) for n, key in enumerate(OFFSETS)], (t, 0))
            fill(br, [(key, spread(up, n, right - 1)) for n, key in enumerate(OFFSETS)], (t, 1))

        return carry

    lax.fori_loop(0, 5, couple, 0)
    br[4] = jnp.zeros((2, 128, 128), F32)

    apart = [sub + 8 * r - lane8 for r in range(16)]

    def diagonal(n, x):
        values = spread(far, n, x)
        return jnp.concatenate([jnp.where(a == 0, values, 0.0) for a in apart], axis=0)

    def tiles_of(x):
        return [hess[x, 8 * r : 8 * r + 8, :] for r in range(TILES)]

    def whole(chain):
        return jnp.concatenate(chain + [jnp.zeros((128 - ROWS, 128), F32)], axis=0)

    def eliminate(t, carry):
        right = PC - 1 - t
        left_tiles, right_tiles = invert([tiles_of(t), tiles_of(right)])
        for s, tiles, x, step, ref in ((0, left_tiles, t, 1, bl), (1, right_tiles, right, -1, br)):
            q = whole(tiles)
            two = diagonal(s, x)
            w = jnp.concatenate([ref[t, 0], two], axis=1)
            wt = jnp.concatenate([ref[t, 1], two], axis=0)
            y = dot(q, w)
            yt[s, t] = dot(wt, q)
            schur = dot(wt, y)
            g = gs[x]
            zs[s, t] = dot(g, q)
            gy = dot(g, y)
            one, two_on = x + step, x + 2 * step
            hess[one] = hess[one] - schur[0:128, 0:128]
            hess[two_on] = hess[two_on] - schur[128:256, 128:256]
            ref[t + 1, 0] = ref[t + 1, 0] - schur[0:128, 128:256]
            ref[t + 1, 1] = ref[t + 1, 1] - schur[128:256, 0:128]
            gs[one] = gs[one] - gy[:, 0:128]
            gs[two_on] = gs[two_on] - gy[:, 128:256]
        return carry

    lax.fori_loop(0, 4, eliminate, 0)

    def middle(t, carry):
        x = 4 + t
        (tiles,) = invert([tiles_of(x)])
        q = whole(tiles)
        g = gs[x]
        dl[x] = dot(g, q)

        @pl.when(t == 0)
        def _():
            w = bl[4, 0] + br[4, 1]
            wt = bl[4, 1] + br[4, 0]
            y = dot(q, w)
            yt[0, 4, 0:128] = dot(wt, q)
            hess[5] = hess[5] - dot(wt, y)
            gs[5] = gs[5] - dot(g, y)

        return carry

    lax.fori_loop(0, 2, middle, 0)
    dl[4] = dl[4] - dot(dl[5], yt[0, 4, 0:128])
    for t in (3, 2, 1, 0):
        right = PC - 1 - t
        dl[t] = zs[0, t] - dot(jnp.concatenate([dl[t + 1], dl[t + 2]], axis=1), yt[0, t])
        dl[right] = zs[1, t] - dot(jnp.concatenate([dl[right - 1], dl[right - 2]], axis=1), yt[1, t])
    for x in range(PC):
        out[x : x + 1, :] = -dl[x, 0:1, :]
    spare = iota((16 - PC, 128), 1)
    corner = jnp.zeros((16 - PC, 128), F32)
    for n in range(3):
        corner = jnp.where(spare == n, sc[10 + n].astype(F32), corner)
    out[PC:16, :] = corner


def field_kernel(sizes, sc, u, f, m, x1, x2, strip, strip1, strip2, s1, s2, out, ua, ub, fo, mo, cx, cy, cz, iv):
    nx, ny, nz = sizes
    low_first = sc[0] == 0
    sub = iota((8, 128), 0)
    lane = iota((AX, 128), 1)
    lead = DEEP - FSWEEPS
    spot = jnp.where(low_first, 0, BZ - DEEP)
    strip_lanes = (lane >= spot) & (lane < spot + DEEP)

    def build(dest, values16):
        for q in range(8):
            j = q // 2
            a = s1[dest, 8 * j : 8 * j + 8]
            b = s2[dest, 8 * j : 8 * j + 8]
            low, high = jnp.where(low_first, a, b), jnp.where(low_first, b, a)
            if q % 2 == 0:
                high = row_roll(high, 4)
            else:
                low = row_roll(low, 4)
            t0, t1 = row_roll(values16[q][0:8], 4), row_roll(values16[q][8:16], 4)
            tall = jnp.concatenate(
                [jnp.where(sub < 4, low, t0), jnp.where(sub < 4, t0, t1), jnp.where(sub < 4, t1, high)], axis=0
            )
            if q < 7:
                ref = ua.at[q] if q < 3 else (fo.at[q - 3] if q < 6 else mo)
                ref[dest, :, 0:128] = tall
            else:
                for c in range(7):
                    ref = ua.at[c] if c < 3 else (fo.at[c - 3] if c < 6 else mo)
                    ref[dest, :, 128:256] = jnp.where(strip_lanes, lane_roll(tall, spot - DEEP * c), 0.0)

    def inner_plane(i, carry):
        build(i + FSWEEPS, [u[k, i] for k in range(3)] + [f[k, i] for k in range(3)] + [m[i], strip[i]])
        return carry

    lax.fori_loop(0, BX, inner_plane, 0)

    def outer_plane(i, carry):
        for a, b, sa, sb, start, dest in (
            (x1, x2, strip2, strip1, lead, i), (x2, x1, strip1, strip2, 0, i + FSWEEPS + BX),
        ):
            j = i + start
            force = j - (1 if start else 0)

            def pick(index):
                return jnp.where(low_first, a[index], b[index])

            build(
                dest,
                [pick(k * DEEP + j) for k in range(3)]
                + [pick(3 * DEEP + k * (DEEP - 1) + force) for k in range(3)]
                + [pick(PLANES - DEEP + j), jnp.where(low_first, sa[j], sb[j])],
            )
        return carry

    lax.fori_loop(0, FSWEEPS, outer_plane, 0)

    row = iota((AX, 256), 0)
    wide = iota((AX, 256), 1)
    gy = sc[14] - FSWEEPS + row
    second = (wide >= 128 + spot) & (wide < 128 + spot + DEEP)
    inside = (gy >= 0) & (gy < ny) & ((wide < 128) | second)

    def faces(i, carry):
        here = mo[i]
        cx[i] = 0.5 * (here + mo[jnp.minimum(i + 1, AX - 1)])
        cy[i] = 0.5 * (here + row_roll(here, -1))
        cz[i] = 0.5 * (here + lane_roll(here, -1))
        return carry

    lax.fori_loop(0, AX, faces, 0)

    def scale(i, carry):
        total = MASS_TERM + cx[i] + cx[i - 1] + cy[i] + row_roll(cy[i], 1) + cz[i] + lane_roll(cz[i], 1)
        gx = sc[13] - FSWEEPS + i
        good = inside & (gx >= 0) & (gx < nx)
        iv[i] = jnp.where(good, 1.0 / total, 0.0)
        return carry

    lax.fori_loop(1, AX - 1, scale, 0)
    for sweep in range(FSWEEPS):
        src, dst = (ua, ub) if sweep % 2 == 0 else (ub, ua)

        def relax(i, carry, src=src, dst=dst, last=sweep == FSWEEPS - 1):
            for k in range(3):
                here = src[k, i]
                total = fo[k, i] + cx[i] * src[k, i + 1] + cx[i - 1] * src[k, i - 1]
                total = total + cy[i] * row_roll(here, -1) + row_roll(cy[i] * here, 1)
                total = total + cz[i] * lane_roll(here, -1) + lane_roll(cz[i] * here, 1)
                total = total * iv[i]
                if last:
                    out[k, i - FSWEEPS] = row_roll(total[:, 0:128], -FSWEEPS)[0:BY]
                else:
                    dst[k, i] = total
            return carry

        lax.fori_loop(sweep + 1, AX - 1 - sweep, relax, 0)


def taper(offset):
    folded = jnp.minimum(offset, SPAN - 1 - offset)
    total = jnp.zeros(offset.shape, F32)
    for n in range(PC):
        total = jnp.where(folded == float(n), math.sin(math.pi * (n + 0.5) / SPAN), total)
    return total


def final_kernel(sc, m, parts, out, acc):
    number = parts.shape[0]
    row16 = iota((16, 128), 0).astype(F32)
    lane16i = iota((16, 128), 1)
    lane16 = lane16i.astype(F32)
    lane_y = div10(lane16i).astype(F32)
    rows128 = iota((128, 128), 0)
    rows_y = div10(rows128)
    rows_z = (rows128 - PC * rows_y).astype(F32)
    lanes128 = iota((128, 128), 1).astype(F32)
    acc[...] = jnp.zeros(acc.shape, F32)

    def add(n, carry):
        delta = parts[n]

        def place(axis, low):
            return delta[PC : PC + 1, axis : axis + 1] - low.astype(F32)

        cx, cy, cz = place(0, sc[13]), place(1, sc[14]), place(2, sc[15])
        off_x = row16 - cx
        apart = off_x - 2.0 * lane16
        choose = jnp.where((apart >= 0.0) & (apart < 2.0) & (lane16i < PC), 1.0, 0.0).astype(BF16)[:, 0:16]
        picked = [
            lax.dot_general(choose, p, (((1,), (0,)), ((), ())), preferred_element_type=F32) for p in three_parts(delta)
        ]
        lines = (picked[0] + picked[1] + picked[2]) * taper(off_x)
        off_y = row16 - cy
        apart = off_y - 2.0 * lane_y
        cover = jnp.where((apart >= 0.0) & (apart < 2.0) & (lane16i < PC * PC), taper(off_y), 0.0)
        off_z = lanes128 - cz
        apart = off_z - 2.0 * rows_z
        expand = jnp.where((apart >= 0.0) & (apart < 2.0) & (rows128 < PC * PC), 1.0, 0.0).astype(BF16)
        tall = jnp.concatenate([jnp.broadcast_to(lines[x : x + 1, :], (BY, 128)) * cover for x in range(BX)], axis=0)
        acc[...] += dot_exact(tall, expand) * taper(off_z[0:1, :])
        return carry

    lax.fori_loop(0, number, add, 0)
    for x in range(BX):
        out[x] = m[x] * (1.0 + acc[16 * x : 16 * x + 16, :])


def call(kernel, shapes, scratch, inputs, flops):
    specs = [pl.BlockSpec(memory_space=pltpu.SMEM)] + [pl.BlockSpec(memory_space=pltpu.VMEM)] * (len(inputs) - 1)
    single = not isinstance(shapes, list)
    outs = [jax.ShapeDtypeStruct(s, F32) for s in ([shapes] if single else shapes)]
    results = pl.pallas_call(
        kernel,
        out_shape=outs,
        in_specs=specs,
        out_specs=[pl.BlockSpec(memory_space=pltpu.VMEM)] * len(outs),
        scratch_shapes=[pltpu.VMEM(s, F32) for s in scratch],
        compiler_params=pltpu.CompilerParams(vmem_limit_bytes=VMEM_LIMIT),
        cost_estimate=pl.CostEstimate(flops=flops, bytes_accessed=1 << 20, transcendentals=0),
    )(*inputs)
    return results[0] if single else results


def body(forcing, start_field, modulus, corners):
    counts = tuple(lax.axis_size(axis) for axis in AXES)
    sizes = (counts[0] * BX, counts[1] * BY, counts[2] * BZ)
    place = tuple(lax.axis_index(axis) for axis in AXES)
    gz = place[2].astype(jnp.int32)
    lower = jnp.stack([place[0] * BX, place[1] * BY, place[2] * BZ]).astype(jnp.int32)

    def send(values, move):
        pairs = []
        for x in range(counts[0]):
            for y in range(counts[1]):
                for z in range(counts[2]):
                    to = move(x, y, z)
                    if all(0 <= t < c for t, c in zip(to, counts)):
                        pairs.append(((x * counts[1] + y) * counts[2] + z, (to[0] * counts[1] + to[1]) * counts[2] + to[2]))
        return lax.ppermute(values, AXES, pairs)

    def turn(z):
        return 1 if z == 0 else -1

    relative = corners[0] - lower
    near = jnp.broadcast_to(relative[None, :], (1, 3))
    want1 = send(near, lambda x, y, z: (x, y - turn(z), z))
    want2 = send(near, lambda x, y, z: (x, y + turn(z), z))
    scalar = jnp.concatenate([gz[None], relative, want1[0], want2[0], corners[0], lower]).astype(jnp.int32)
    first = gz[None]

    msg1, msg2, strip, strip1, strip2 = call(
        edge_kernel,
        [(PLANES, BY, 128), (PLANES, BY, 128), (BX, BY, 128), (DEEP, BY, 128), (DEEP, BY, 128)],
        [],
        [first, start_field, forcing, modulus],
        1 << 20,
    )
    x1 = send(msg1, lambda x, y, z: (x + turn(z), y, z))
    x2 = send(msg2, lambda x, y, z: (x - turn(z), y, z))
    far_strip = send(strip, lambda x, y, z: (x, y, 1 - z))
    far1 = send(strip1, lambda x, y, z: (x + turn(z), y, 1 - z))
    far2 = send(strip2, lambda x, y, z: (x - turn(z), y, 1 - z))
    own_u, own_f, y1, y2, a1, a2 = call(
        pack_kernel,
        [(WIN, BY, 128)] * 2 + [(WIN // 2, 40, 128)] * 2 + [(AX, 32, 128)] * 2,
        [(3, 36, BY, 128), (3, 36, BY, 128), (36, BY, 128), (36, BY, 128)],
        [scalar, start_field, forcing, modulus, x1, x2, far_strip, far1, far2],
        1 << 22,
    )
    r1 = send(y1, lambda x, y, z: (x, y + turn(z), z))
    r2 = send(y2, lambda x, y, z: (x, y - turn(z), z))
    b1 = send(a1, lambda x, y, z: (x, y + turn(z), z))
    b2 = send(a2, lambda x, y, z: (x, y - turn(z), z))
    window = (WIN, WY, 128)
    delta = call(
        functools.partial(zone_kernel, sizes),
        (16, 128),
        [window] * 8
        + [
            (8, 3, 16, 128), (13, 16, 128), (5, 16, 128), (5, 16, 128), (2, 16, 128), (16, 128),
            (PC, 128, 128), (5, 2, 128, 128), (5, 2, 128, 128), (2, 5, 256, 128), (2, 5, 8, 128), (PC, 8, 128), (PC, 8, 128),
        ],
        [scalar, own_u, own_f, r1, r2],
        1 << 33,
    )
    beside = [delta]
    beside.append(send(delta, lambda x, y, z: (x, y, 1 - z)))
    for step in (1, -1):
        beside.append(send(delta, lambda x, y, z, step=step: (x, y + step * turn(z), z)))
        beside.append(send(delta, lambda x, y, z, step=step: (x, y + step * turn(z), 1 - z)))
    plane = jnp.stack(beside)
    after = send(plane, lambda x, y, z: (x + turn(z), y, z))
    before = send(plane, lambda x, y, z: (x - turn(z), y, z))
    wide = (AX, AX, 256)
    displacement = call(
        functools.partial(field_kernel, sizes),
        (3, BX, BY, BZ),
        [(3,) + wide] * 3 + [wide] * 5,
        [scalar, start_field, forcing, modulus, x1, x2, far_strip, far1, far2, b1, b2],
        1 << 30,
    )
    new_modulus = call(
        final_kernel,
        (BX, BY, BZ),
        [(BX * BY, 128)],
        [scalar, modulus, jnp.concatenate([plane, after, before])],
        1 << 24,
    )
    return displacement, new_modulus


def solution(mesh):
    placed = (
        P(None, "gx", "gy", "gz"),
        P(None, "gx", "gy", "gz"),
        P("gx", "gy", "gz"),
        P(("gx", "gy", "gz"), None),
    )
    return jax.shard_map(
        body,
        mesh=mesh,
        in_specs=placed,
        out_specs=(P(None, "gx", "gy", "gz"), P("gx", "gy", "gz")),
        check_vma=False,
    )
```

```python
import functools
import math

import jax
import jax.numpy as jnp
from jax import lax
from jax.experimental import pallas as pl
from jax.experimental.pallas import tpu as pltpu
from jax.sharding import PartitionSpec as P

PC = 10
SPAN = 2 * PC
FSWEEPS = 4
MASS_TERM = 0.5
DAMPING = 0.1
EPSILON = 1e-06
BX, BY, BZ = 16, 16, 128
DEEP = 10
WIN = 30
WY = 32
AX = 24
ROWS = 104
TILES = ROWS // 8
PLANES = 3 * DEEP + 3 * (DEEP - 1) + DEEP
AXES = ("gx", "gy", "gz")
F32 = jnp.float32
BF16 = jnp.bfloat16
HIGH = lax.Precision.HIGHEST
VMEM_LIMIT = 48 * 1024 * 1024


def iota(shape, dim):
    return lax.broadcasted_iota(jnp.int32, shape, dim)


def lane_roll(values, shift):
    if isinstance(shift, int):
        shift = shift % values.shape[-1]
        return values if shift == 0 else pltpu.roll(values, shift, values.ndim - 1)
    size = values.shape[-1]
    return pltpu.roll(values, lax.rem(shift + 8 * size, size), values.ndim - 1)


def row_roll(values, shift):
    if isinstance(shift, int):
        shift = shift % values.shape[-2]
        return values if shift == 0 else pltpu.roll(values, shift, values.ndim - 2)
    size = values.shape[-2]
    return pltpu.roll(values, lax.rem(shift + 8 * size, size), values.ndim - 2)


def loop(low, high, step, unroll):
    whole = (high - low) // unroll
    if whole == 1:
        for i in range(low, low + unroll):
            step(i)
    elif whole > 1:

        def chunk(t, carry):
            for n in range(unroll):
                step(low + t * unroll + n)
            return carry

        lax.fori_loop(0, whole, chunk, 0)
    for i in range(low + whole * unroll, high):
        step(i)


def three_parts(values):
    first = values.astype(BF16)
    rest = values - first.astype(F32)
    second = rest.astype(BF16)
    third = (rest - second.astype(F32)).astype(BF16)
    return first, second, third


def dot(a, b):
    return lax.dot_general(a, b, (((1,), (0,)), ((), ())), precision=HIGH, preferred_element_type=F32)


def dot_exact(values, selector):
    parts = [
        lax.dot_general(part, selector, (((1,), (0,)), ((), ())), preferred_element_type=F32)
        for part in three_parts(values)
    ]
    return parts[0] + parts[1] + parts[2]


def div10(value):
    return lax.shift_right_arithmetic(value * 205, 11)


def edge_kernel(sc, u, f, m, msg1, msg2, strip, strip1, strip2, vu, vf, vm, sems):
    gz = sc[0]
    low_first = gz == 0
    s1 = jnp.where(low_first, BX - DEEP, 0)
    s2 = BX - DEEP - s1
    f1 = jnp.where(low_first, BX - DEEP + 1, 0)
    f2 = BX - DEEP + 1 - f1
    loads = [pltpu.make_async_copy(u, vu, sems.at[0]), pltpu.make_async_copy(f, vf, sems.at[1])]
    loads.append(pltpu.make_async_copy(m, vm, sems.at[2]))
    for load in loads:
        load.start()
    for load in loads:
        load.wait()
    lane = iota((BY, 128), 1)
    extra = jnp.where(low_first, DEEP, 0)

    def one(x):
        total = jnp.zeros((BY, 128), F32)
        for c in range(7):
            source = vu[c, x] if c < 3 else (vf[c - 3, x] if c < 6 else vm[x])
            moved = lane_roll(source, extra + DEEP * c)
            total = jnp.where((lane >= DEEP * c) & (lane < DEEP * (c + 1)), moved, total)
        strip[x] = total

    loop(0, BX, one, 8)
    for out, s, fs in ((msg1, s1, f1), (msg2, s2, f2)):
        for k in range(3):
            out[k * DEEP : (k + 1) * DEEP] = vu[k, pl.ds(s, DEEP)]
            base = 3 * DEEP + k * (DEEP - 1)
            out[base : base + DEEP - 1] = vf[k, pl.ds(fs, DEEP - 1)]
        out[PLANES - DEEP : PLANES] = vm[pl.ds(s, DEEP)]
    strip1[...] = strip[pl.ds(s1, DEEP)]
    strip2[...] = strip[pl.ds(s2, DEEP)]


def pack_kernel(sc, u, f, m, x1, x2, strip, strip1, strip2, own_u, own_f, msg1, msg2, side1, side2, eu, ef, em, es):
    gz = sc[0]
    low_first = gz == 0
    p1 = jnp.where(low_first, 0, BX + DEEP)
    p2 = BX + DEEP - p1
    q1 = jnp.where(low_first, 1, BX + DEEP)
    q2 = BX + DEEP + 1 - q1
    for k in range(3):
        eu[k, DEEP : DEEP + BX] = u[k]
        ef[k, DEEP : DEEP + BX] = f[k]
        ef[k, 0] = jnp.zeros((BY, 128), F32)
        ef[k, 2 * DEEP + BX - 1] = jnp.zeros((BY, 128), F32)
        for msg, p, q in ((x1, p1, q1), (x2, p2, q2)):
            eu[k, pl.ds(p, DEEP)] = msg[k * DEEP : (k + 1) * DEEP]
            base = 3 * DEEP + k * (DEEP - 1)
            ef[k, pl.ds(q, DEEP - 1)] = msg[base : base + DEEP - 1]
    em[DEEP : DEEP + BX] = m[...]
    es[DEEP : DEEP + BX] = strip[...]
    em[pl.ds(p1, DEEP)] = x1[PLANES - DEEP : PLANES]
    em[pl.ds(p2, DEEP)] = x2[PLANES - DEEP : PLANES]
    es[pl.ds(p2, DEEP)] = strip1[...]
    es[pl.ds(p1, DEEP)] = strip2[...]

    lane = iota((BY, 128), 1)
    group = lax.shift_right_arithmetic(lane, 5)
    inner = lane & 31
    zoff = jnp.where(low_first, BZ, -DEEP)

    def window(relz):
        w0 = relz - (DEEP - 5)
        z = inner + w0
        main_ok = (z >= 0) & (z < BZ)
        strip_ok = (z >= zoff) & (z < zoff + DEEP)

        def take(x):
            side = es[x]
            values = []
            for sources in ((eu, 0), (ef, 3)):
                ref, first = sources
                main = jnp.zeros((BY, 128), F32)
                far = jnp.zeros((BY, 128), F32)
                for k in range(4 if first == 0 else 3):
                    source, c = (ref[k, x], first + k) if k < 3 else (em[x], 6)
                    main = jnp.where(group == k, lane_roll(source, 32 * k - w0), main)
                    far = jnp.where(group == k, lane_roll(side, 32 * k + zoff - w0 - DEEP * c), far)
                values.append(jnp.where(main_ok, main, jnp.where(strip_ok, far, 0.0)))
            return values

        return take

    take_own = window(sc[3])
    x0 = sc[1] + 5

    def own(i):
        field, force = take_own(x0 + i)
        own_u[i] = field
        own_f[i] = force

    loop(0, WIN, own, 6)

    sub = iota((8, 128), 0)
    for msg, side, base, upward in ((msg1, side1, 4, low_first), (msg2, side2, 7, gz != 0)):
        take = window(sc[base + 2])
        start = sc[base] + 5

        def pair(i, msg=msg, take=take, start=start, upward=upward):
            mixed = jnp.zeros((8, 128), F32)
            number = 0
            for step in range(2):
                for values in take(start + 2 * i + step):
                    top, bottom = values[0:8], values[8:16]
                    msg[i, 8 * number : 8 * number + 8] = jnp.where(upward, bottom, top)
                    edge = jnp.where(upward, row_roll(top, 2), bottom)
                    mixed = jnp.where((sub >= 2 * number) & (sub < 2 * number + 2), row_roll(edge, 2 * number), mixed)
                    number += 1
            msg[i, 32:40] = mixed

        loop(0, WIN // 2, pair, 3)

        def plane(i, side=side, upward=upward):
            x = i + DEEP - FSWEEPS

            def edge(values):
                return jnp.where(upward, row_roll(values[8:16], 4), values[0:8])

            every = [edge(eu[k, x]) for k in range(3)] + [edge(ef[k, x]) for k in range(3)] + [edge(em[x]), edge(es[x])]
            for j in range(4):
                side[i, 8 * j : 8 * j + 8] = jnp.where(sub < 4, every[2 * j], row_roll(every[2 * j + 1], 4))

        loop(0, AX, plane, 6)


def invert(chains):
    sub = iota((8, 128), 0)
    lane = iota((8, 128), 1)

    def row_of(values, j):
        return jnp.broadcast_to(values[j : j + 1, :], (8, 128))

    def column_of(values, j):
        return jnp.broadcast_to(values[:, j : j + 1], (8, 128))

    empty = jnp.zeros((8, 128), F32)
    for b in range(TILES):
        in_block = (lane >= 8 * b) & (lane < 8 * b + 8)
        for chain in chains:
            pivot = chain[b]
            own = [column_of(pivot, 8 * b + j) for j in range(8)]
            for j in range(0, 8, 2):
                here0, here1 = sub == j, sub == j + 1
                at0, at1 = lane == 8 * b + j, lane == 8 * b + j + 1
                p00, p01 = row_of(own[j], j), row_of(own[j + 1], j)
                p10, p11 = row_of(own[j], j + 1), row_of(own[j + 1], j + 1)
                scale = pl.reciprocal(p00 * p11 - p01 * p10, approx=True)
                side0 = jnp.where(here0, -1.0, jnp.where(here1, 0.0, own[j]))
                side1 = jnp.where(here0, 0.0, jnp.where(here1, -1.0, own[j + 1]))
                both = here0 | here1

                def step(values, line0, line1):
                    first = p11 * line0 - p01 * line1
                    second = p00 * line1 - p10 * line0
                    return jnp.where(both, 0.0, values) - (side0 * first + side1 * second) * scale

                for n in range(j + 2, 8):
                    own[n] = step(own[n], row_of(own[n], j), row_of(own[n], j + 1))
                line0 = jnp.where(at0, 1.0, jnp.where(at1, 0.0, row_of(pivot, j)))
                line1 = jnp.where(at0, 0.0, jnp.where(at1, 1.0, row_of(pivot, j + 1)))
                pivot = step(jnp.where(at0 | at1, 0.0, pivot), line0, line1)
            if b + 1 < TILES:
                after = jnp.where(in_block, 0.0, chain[b + 1])
                terms = [column_of(chain[b + 1], 8 * b + j) * row_of(pivot, j) for j in range(8)]
                while len(terms) > 1:
                    terms = [p + q for p, q in zip(terms[0::2], terms[1::2])]
                after = after - terms[0]
            spread = jnp.concatenate([pivot if r == b else empty for r in range(16)], axis=0)
            change = dot(jnp.concatenate(chain, axis=0), spread)
            for i in range(TILES):
                if i == b:
                    chain[i] = pivot
                elif i == b + 1:
                    chain[i] = after
                else:
                    chain[i] = jnp.where(in_block, 0.0, chain[i]) - change[8 * i : 8 * i + 8]
    return chains


OFFSETS = (0, PC, -PC, 1, -1)
BANDS = (0, 1, 2, 9, 10, 11, 20)


def zone_kernel(
    sizes, sc, own_u, own_f, r1, r2, out,
    ua, ub, fo, m3, cx, cy, cz, iv, rows, band, up, down, far, grad, hess, bl, br, yt, zs, dl, gs,
):
    nx, ny, nz = sizes
    low_first = sc[0] == 0
    rely = sc[2]
    lane32 = iota((WY, 128), 1)
    group = lax.shift_right_arithmetic(lane32, 5)
    inner = lane32 & 31
    row32 = iota((WY, 128), 0)
    shift = -(rely + 11)

    inside_y = sc[11] - 5 + row32
    inside_z = sc[12] - 5 + inner
    inside = (inside_y >= 0) & (inside_y < ny) & (inside_z >= 0) & (inside_z < nz)

    def unpack(i):
        for step in range(2):
            gx = sc[10] - 5 + 2 * i + step
            good = inside & (gx >= 0) & (gx < nx)
            for which in range(2):
                number = 2 * step + which
                first = r1[i, 8 * number : 8 * number + 8]
                second = r2[i, 8 * number : 8 * number + 8]
                mix1 = r1[i, 32:40]
                mix2 = r2[i, 32:40]
                low, high = jnp.where(low_first, first, second), jnp.where(low_first, second, first)
                low_mix, high_mix = jnp.where(low_first, mix1, mix2), jnp.where(low_first, mix2, mix1)
                middle = own_u[2 * i + step] if which == 0 else own_f[2 * i + step]
                tall = jnp.concatenate(
                    [row_roll(low_mix, 6 - 2 * number), low, middle, high, row_roll(high_mix, -2 * number)], axis=0
                )
                tall = row_roll(tall, shift)[0:WY]
                if which == 0:
                    tall = jnp.where(good, tall, 0.0)
                    ua[2 * i + step] = tall
                    moved = jnp.where(group == 0, lane_roll(tall, 32), 0.0)
                    moved = jnp.where(group == 1, lane_roll(tall, 64), moved)
                    m3[2 * i + step] = jnp.where(group == 2, lane_roll(tall, 96), moved)
                else:
                    fo[2 * i + step] = tall

    loop(0, WIN // 2, unpack, 3)

    def faces(i):
        here = m3[i]
        cx[i] = 0.5 * (here + m3[jnp.minimum(i + 1, WIN - 1)])
        cy[i] = 0.5 * (here + row_roll(here, -1))
        cz[i] = 0.5 * (here + lane_roll(here, -1))

    loop(0, WIN, faces, 10)

    def scale(i):
        total = MASS_TERM + cx[i] + cx[i - 1] + cy[i] + row_roll(cy[i], 1) + cz[i] + lane_roll(cz[i], 1)
        gx = sc[10] - 5 + i
        good = inside & (gx >= 0) & (gx < nx)
        iv[i] = jnp.where(good, 1.0 / total, 0.0)

    loop(1, WIN - 1, scale, 7)

    for sweep in range(FSWEEPS):
        src, dst = (ua, ub) if sweep % 2 == 0 else (ub, ua)

        def relax(i, src=src, dst=dst):
            here = src[i]
            total = fo[i] + cx[i] * src[i + 1] + cx[i - 1] * src[i - 1]
            total = total + cy[i] * row_roll(here, -1) + row_roll(cy[i] * here, 1)
            total = total + cz[i] * lane_roll(here, -1) + lane_roll(cz[i] * here, 1)
            dst[i] = total * iv[i]

        loop(sweep + 1, WIN - 1 - sweep, relax, WIN)

    line = iota((128, 384), 0)
    column = iota((128, 384), 1)
    part = lax.shift_right_arithmetic(column, 7)
    spot = column & 127
    spot_y = div10(spot)
    spot_z = spot - PC * spot_y
    inner_z = (line & 31) - 5
    hit = (lax.shift_right_arithmetic(line, 5) == part) & (inner_z >= 0) & (inner_z < SPAN) & (spot < PC * PC)
    hit = hit & (lax.shift_right_arithmetic(inner_z, 1) == spot_z)
    selector = jnp.where(hit, 1.0, 0.0).astype(BF16)
    zone_y = row32 - 5
    lane_y = div10(lane32)
    pick_y = (zone_y >= 0) & (zone_y < SPAN) & (lax.shift_right_arithmetic(zone_y, 1) == lane_y) & (lane32 < PC * PC)
    pick_y = jnp.where(pick_y, 1.0, 0.0)
    even_y = (zone_y & 1) == 0
    even_z = ((inner - 5) & 1) == 0
    rows[...] = jnp.zeros(rows.shape, F32)

    def layer(a):
        sums = None
        for odd in range(2):
            i = 5 + 2 * a + odd
            here, m_here = ua[i], m3[i]
            ch_x, ch_b = here - ua[i + 1], ua[i - 1] - here
            ch_y = here - row_roll(here, -1)
            ch_z = here - lane_roll(here, -1)
            flow_y, flow_z = cy[i] * ch_y, cz[i] * ch_z
            applied = MASS_TERM * here + cx[i] * ch_x - cx[i - 1] * ch_b
            applied = applied + flow_y - row_roll(flow_y, 1) + flow_z - lane_roll(flow_z, 1)
            resid = fo[i] - applied
            back_y, back_z = row_roll(ch_y, 1), lane_roll(ch_z, 1)
            laplace = ch_x - ch_b + ch_y - back_y + ch_z - back_z
            xp = -0.5 * m3[i + 1] * ch_x
            xm = 0.5 * m3[i - 1] * ch_b
            yp = -0.5 * row_roll(m_here, -1) * ch_y
            ym = 0.5 * row_roll(m_here, 1) * back_y
            zp = -0.5 * lane_roll(m_here, -1) * ch_z
            zm = 0.5 * lane_roll(m_here, 1) * back_z
            diag = -0.5 * m_here * laplace + jnp.where(even_y, yp, ym) + jnp.where(even_z, zp, zm)
            diag = diag + (xm if odd else xp)
            now = [
                diag, xp if odd else None, None if odd else xm,
                jnp.where(even_y, 0.0, yp), jnp.where(even_y, ym, 0.0),
                jnp.where(even_z, 0.0, zp), jnp.where(even_z, zm, 0.0), resid,
            ]
            if sums is None:
                sums = now
            else:
                sums = [p if q is None else (q if p is None else p + q) for p, q in zip(sums, now)]
        tall = dot_exact(jnp.concatenate(sums, axis=0), selector)
        for n in range(8):
            for k in range(3):
                piece = tall[n * WY : (n + 1) * WY, 128 * k : 128 * k + 128] * pick_y
                rows[n, k, pl.ds(a, 1), :] = jnp.sum(piece, axis=0, keepdims=True)

    loop(0, PC, layer, 2)

    lane16 = iota((16, 128), 1)
    row16 = iota((16, 128), 0)
    at_y = div10(lane16)
    at_z = lane16 - PC * at_y

    def masked(n, keep):
        return [jnp.where(keep, rows[n, k], 0.0) for k in range(3)]

    full = row16 < PC
    v = {
        0: masked(0, full),
        PC: masked(3, full & (at_y < PC - 1)),
        -PC: masked(4, full & (at_y > 0)),
        1: masked(5, full & (at_z < PC - 1)),
        -1: masked(6, full & (at_z > 0)),
    }
    vxp = masked(1, row16 < PC - 1)
    vxm = masked(2, full & (row16 > 0))
    res = masked(7, full)

    def mix(p, q):
        return p[0] * q[0] + p[1] * q[1] + p[2] * q[2]

    bands = {}
    for o1 in OFFSETS:
        for o2 in OFFSETS:
            key = o1 - o2
            if key >= 0:
                term = lane_roll(mix(v[o1], v[o2]), o2)
                bands[key] = bands[key] + term if key in bands else term
    bands[0] = bands[0] + row_roll(mix(vxp, vxp), 1) + row_roll(mix(vxm, vxm), -1)
    trace = jnp.sum(jnp.sum(bands[0], axis=1, keepdims=True), axis=0, keepdims=True)
    ridge = DAMPING * trace / PC**3 + EPSILON
    bands[0] = jnp.where(lane16 < PC * PC, bands[0] + ridge, jnp.where(lane16 < ROWS, 1.0, 0.0))
    slots = {}
    for n, key in enumerate(BANDS):
        band[n] = bands[key]
        slots[key] = n
    for n, key in enumerate(BANDS[1:]):
        band[len(BANDS) + n] = lane_roll(bands[key], key)
        slots[-key] = len(BANDS) + n
    for n, key in enumerate(OFFSETS):
        above = row_roll(mix(vxm, v[-key]), -1)
        below = row_roll(mix(vxp, v[-key]), 1)
        up[n] = mix(vxp, v[key]) + lane_roll(above, -key)
        down[n] = mix(vxm, v[key]) + lane_roll(below, -key)
    cross = mix(vxm, vxp)
    far[0] = row_roll(cross, -1)
    far[1] = row_roll(cross, 1)
    gradient = row_roll(mix(vxp, res), 1) + row_roll(mix(vxm, res), -1)
    for key in OFFSETS:
        gradient = gradient + lane_roll(mix(v[key], res), key)
    grad[...] = gradient

    sub = iota((8, 128), 0)
    lane8 = iota((8, 128), 1)

    def spread(ref, n, x):
        return jnp.broadcast_to(ref[n, pl.ds(x, 1), :], (8, 128))

    def fill(dst, lines, lead):
        for r in range(TILES):
            apart = sub + 8 * r - lane8
            tile = jnp.zeros((8, 128), F32)
            for key, values in lines:
                if 8 * r + 7 - key >= 0 and 8 * r - key < 128:
                    tile = jnp.where(apart == key, values, tile)
            dst[lead + (slice(8 * r, 8 * r + 8), slice(None))] = tile
        dst[lead + (slice(ROWS, 128), slice(None))] = jnp.zeros((128 - ROWS, 128), F32)

    def dense(x, carry):
        fill(hess, [(key, spread(band, n, x)) for key, n in slots.items()], (x,))
        gs[x] = jnp.broadcast_to(grad[pl.ds(x, 1), :], (8, 128))
        return carry

    lax.fori_loop(0, PC, dense, 0)

    def couple(t, carry):
        right = PC - 1 - t
        fill(bl, [(key, spread(up, n, t)) for n, key in enumerate(OFFSETS)], (t, 0))
        fill(bl, [(key, spread(down, n, t + 1)) for n, key in enumerate(OFFSETS)], (t, 1))

        @pl.when(t < 4)
        def _():
            fill(br, [(key, spread(down, n, right)) for n, key in enumerate(OFFSETS)], (t, 0))
            fill(br, [(key, spread(up, n, right - 1)) for n, key in enumerate(OFFSETS)], (t, 1))

        return carry

    lax.fori_loop(0, 5, couple, 0)
    br[4] = jnp.zeros((2, 128, 128), F32)

    on_diagonal = iota((128, 128), 0) == iota((128, 128), 1)
    ones = jnp.ones((128, 128), BF16)

    def tiles_of(x):
        return [hess[x, 8 * r : 8 * r + 8, :] for r in range(TILES)]

    def whole(chain):
        return jnp.concatenate(chain + [jnp.zeros((128 - ROWS, 128), F32)], axis=0)

    def eliminate(t, carry):
        right = PC - 1 - t
        left_tiles, right_tiles = invert([tiles_of(t), tiles_of(right)])
        for s, tiles, x, step, ref in ((0, left_tiles, t, 1, bl), (1, right_tiles, right, -1, br)):
            q = whole(tiles)
            row = jnp.broadcast_to(far[s, pl.ds(x, 1), :], (128, 128))
            column = dot_exact(jnp.where(on_diagonal, row, 0.0), ones)
            w, wt = ref[t, 0], ref[t, 1]
            y1, y2 = dot(q, w), q * row
            yt[s, t, 0:128] = dot(wt, q)
            yt[s, t, 128:256] = column * q
            s1 = dot(wt, jnp.concatenate([y1, y2], axis=1))
            g = gs[x]
            z = dot(g, q)
            zs[s, t] = z
            one, two_on = x + step, x + 2 * step
            hess[one] = hess[one] - s1[:, 0:128]
            hess[two_on] = hess[two_on] - column * y2
            ref[t + 1, 0] = ref[t + 1, 0] - s1[:, 128:256]
            ref[t + 1, 1] = ref[t + 1, 1] - column * y1
            gs[one] = gs[one] - dot(z, w)
            gs[two_on] = gs[two_on] - z * row[0:8]
        return carry

    lax.fori_loop(0, 4, eliminate, 0)

    def middle(t, carry):
        x = 4 + t
        (tiles,) = invert([tiles_of(x)])
        q = whole(tiles)
        g = gs[x]
        dl[x] = dot(g, q)

        @pl.when(t == 0)
        def _():
            w = bl[4, 0] + br[4, 1]
            wt = bl[4, 1] + br[4, 0]
            y = dot(q, w)
            yt[0, 4, 0:128] = dot(wt, q)
            hess[5] = hess[5] - dot(wt, y)
            gs[5] = gs[5] - dot(g, y)

        return carry

    lax.fori_loop(0, 2, middle, 0)
    dl[4] = dl[4] - dot(dl[5], yt[0, 4, 0:128])
    for t in (3, 2, 1, 0):
        right = PC - 1 - t
        dl[t] = zs[0, t] - dot(jnp.concatenate([dl[t + 1], dl[t + 2]], axis=1), yt[0, t])
        dl[right] = zs[1, t] - dot(jnp.concatenate([dl[right - 1], dl[right - 2]], axis=1), yt[1, t])
    for x in range(PC):
        out[x : x + 1, :] = -dl[x, 0:1, :]
    spare = iota((16 - PC, 128), 1)
    corner = jnp.zeros((16 - PC, 128), F32)
    for n in range(3):
        corner = jnp.where(spare == n, sc[10 + n].astype(F32), corner)
    out[PC:16, :] = corner


def field_kernel(sizes, sc, u, f, m, x1, x2, strip, strip1, strip2, s1, s2, out, ua, ub, fo, mo, cx, cy, cz, iv):
    nx, ny, nz = sizes
    low_first = sc[0] == 0
    sub = iota((8, 128), 0)
    lane = iota((AX, 128), 1)
    lead = DEEP - FSWEEPS
    spot = jnp.where(low_first, 0, BZ - DEEP)
    strip_lanes = (lane >= spot) & (lane < spot + DEEP)

    row24 = iota((AX, 128), 0)
    inside24 = (sc[14] - FSWEEPS + row24 >= 0) & (sc[14] - FSWEEPS + row24 < ny)

    def build(dest, values16):
        gx = sc[13] - FSWEEPS + dest
        good = inside24 & (gx >= 0) & (gx < nx)
        for q in range(8):
            j = q // 2
            a = s1[dest, 8 * j : 8 * j + 8]
            b = s2[dest, 8 * j : 8 * j + 8]
            low, high = jnp.where(low_first, a, b), jnp.where(low_first, b, a)
            if q % 2 == 0:
                high = row_roll(high, 4)
            else:
                low = row_roll(low, 4)
            t0, t1 = row_roll(values16[q][0:8], 4), row_roll(values16[q][8:16], 4)
            tall = jnp.concatenate(
                [jnp.where(sub < 4, low, t0), jnp.where(sub < 4, t0, t1), jnp.where(sub < 4, t1, high)], axis=0
            )
            tall = jnp.where(good, tall, 0.0)
            if q < 7:
                ref = ua.at[q] if q < 3 else (fo.at[q - 3] if q < 6 else mo)
                ref[dest, :, 0:128] = tall
            else:
                for c in range(7):
                    ref = ua.at[c] if c < 3 else (fo.at[c - 3] if c < 6 else mo)
                    ref[dest, :, 128:256] = jnp.where(strip_lanes, lane_roll(tall, spot - DEEP * c), 0.0)

    def inner_plane(i):
        build(i + FSWEEPS, [u[k, i] for k in range(3)] + [f[k, i] for k in range(3)] + [m[i], strip[i]])

    loop(0, BX, inner_plane, 2)

    def outer_plane(i):
        for a, b, sa, sb, start, dest in (
            (x1, x2, strip2, strip1, lead, i), (x2, x1, strip1, strip2, 0, i + FSWEEPS + BX),
        ):
            j = i + start
            force = j - (1 if start else 0)

            def pick(index):
                return jnp.where(low_first, a[index], b[index])

            build(
                dest,
                [pick(k * DEEP + j) for k in range(3)]
                + [pick(3 * DEEP + k * (DEEP - 1) + force) for k in range(3)]
                + [pick(PLANES - DEEP + j), jnp.where(low_first, sa[j], sb[j])],
            )

    loop(0, FSWEEPS, outer_plane, 1)

    row = iota((AX, 256), 0)
    wide = iota((AX, 256), 1)
    gy = sc[14] - FSWEEPS + row
    second = (wide >= 128 + spot) & (wide < 128 + spot + DEEP)
    inside = (gy >= 0) & (gy < ny) & ((wide < 128) | second)

    def faces(i):
        here = mo[i]
        cx[i] = 0.5 * (here + mo[jnp.minimum(i + 1, AX - 1)])
        cy[i] = 0.5 * (here + row_roll(here, -1))
        cz[i] = 0.5 * (here + lane_roll(here, -1))

    loop(0, AX, faces, 4)

    def scale(i):
        total = MASS_TERM + cx[i] + cx[i - 1] + cy[i] + row_roll(cy[i], 1) + cz[i] + lane_roll(cz[i], 1)
        gx = sc[13] - FSWEEPS + i
        good = inside & (gx >= 0) & (gx < nx)
        iv[i] = jnp.where(good, 1.0 / total, 0.0)

    loop(1, AX - 1, scale, 2)
    for sweep in range(FSWEEPS):
        src, dst = (ua, ub) if sweep % 2 == 0 else (ub, ua)

        def relax(i, src=src, dst=dst, last=sweep == FSWEEPS - 1):
            for k in range(3):
                here = src[k, i]
                total = fo[k, i] + cx[i] * src[k, i + 1] + cx[i - 1] * src[k, i - 1]
                total = total + cy[i] * row_roll(here, -1) + row_roll(cy[i] * here, 1)
                total = total + cz[i] * lane_roll(here, -1) + lane_roll(cz[i] * here, 1)
                total = total * iv[i]
                if last:
                    out[k, i - FSWEEPS] = row_roll(total[:, 0:128], -FSWEEPS)[0:BY]
                else:
                    dst[k, i] = total

        loop(sweep + 1, AX - 1 - sweep, relax, 2)


def taper(offset):
    folded = jnp.minimum(offset, SPAN - 1 - offset)
    total = jnp.zeros(offset.shape, F32)
    for n in range(PC):
        total = jnp.where(folded == float(n), math.sin(math.pi * (n + 0.5) / SPAN), total)
    return total


def final_kernel(sc, m, parts, out, acc):
    number = parts.shape[0]
    row16 = iota((16, 128), 0).astype(F32)
    lane16i = iota((16, 128), 1)
    lane16 = lane16i.astype(F32)
    lane_y = div10(lane16i).astype(F32)
    rows128 = iota((128, 128), 0)
    rows_y = div10(rows128)
    rows_z = (rows128 - PC * rows_y).astype(F32)
    lanes128 = iota((128, 128), 1).astype(F32)
    acc[...] = jnp.zeros(acc.shape, F32)

    def add(n):
        delta = parts[n]

        def place(axis, low):
            return delta[PC : PC + 1, axis : axis + 1] - low.astype(F32)

        cx, cy, cz = place(0, sc[13]), place(1, sc[14]), place(2, sc[15])
        off_x = row16 - cx
        apart = off_x - 2.0 * lane16
        choose = jnp.where((apart >= 0.0) & (apart < 2.0) & (lane16i < PC), 1.0, 0.0).astype(BF16)[:, 0:16]
        picked = [
            lax.dot_general(choose, p, (((1,), (0,)), ((), ())), preferred_element_type=F32) for p in three_parts(delta)
        ]
        lines = (picked[0] + picked[1] + picked[2]) * taper(off_x)
        off_y = row16 - cy
        apart = off_y - 2.0 * lane_y
        cover = jnp.where((apart >= 0.0) & (apart < 2.0) & (lane16i < PC * PC), taper(off_y), 0.0)
        off_z = lanes128 - cz
        apart = off_z - 2.0 * rows_z
        expand = jnp.where((apart >= 0.0) & (apart < 2.0) & (rows128 < PC * PC), 1.0, 0.0).astype(BF16)
        tall = jnp.concatenate([jnp.broadcast_to(lines[x : x + 1, :], (BY, 128)) * cover for x in range(BX)], axis=0)
        acc[...] += dot_exact(tall, expand) * taper(off_z[0:1, :])

    loop(0, number, add, 3)
    for x in range(BX):
        out[x] = m[x] * (1.0 + acc[16 * x : 16 * x + 16, :])


def call(kernel, shapes, scratch, inputs, flops, space=pltpu.VMEM):
    specs = [pl.BlockSpec(memory_space=pltpu.SMEM)] + [pl.BlockSpec(memory_space=space)] * (len(inputs) - 1)
    single = not isinstance(shapes, list)
    outs = [jax.ShapeDtypeStruct(s, F32) for s in ([shapes] if single else shapes)]
    results = pl.pallas_call(
        kernel,
        out_shape=outs,
        in_specs=specs,
        out_specs=[pl.BlockSpec(memory_space=pltpu.VMEM)] * len(outs),
        scratch_shapes=[pltpu.VMEM(s, F32) if isinstance(s, tuple) else s for s in scratch],
        compiler_params=pltpu.CompilerParams(vmem_limit_bytes=VMEM_LIMIT),
        cost_estimate=pl.CostEstimate(flops=flops, bytes_accessed=1 << 20, transcendentals=0),
    )(*inputs)
    return results[0] if single else results


def body(forcing, start_field, modulus, corners):
    counts = tuple(lax.axis_size(axis) for axis in AXES)
    sizes = (counts[0] * BX, counts[1] * BY, counts[2] * BZ)
    place = tuple(lax.axis_index(axis) for axis in AXES)
    gz = place[2].astype(jnp.int32)
    lower = jnp.stack([place[0] * BX, place[1] * BY, place[2] * BZ]).astype(jnp.int32)

    def send(values, move):
        pairs = []
        for x in range(counts[0]):
            for y in range(counts[1]):
                for z in range(counts[2]):
                    to = [t % c for t, c in zip(move(x, y, z), counts)]
                    pairs.append(((x * counts[1] + y) * counts[2] + z, (to[0] * counts[1] + to[1]) * counts[2] + to[2]))
        return lax.ppermute(values, AXES, pairs)

    def turn(z):
        return 1 if z == 0 else -1

    relative = corners[0] - lower
    near = jnp.broadcast_to(relative[None, :], (1, 3))
    want1 = send(near, lambda x, y, z: (x, y - turn(z), z))
    want2 = send(near, lambda x, y, z: (x, y + turn(z), z))
    scalar = jnp.concatenate([gz[None], relative, want1[0], want2[0], corners[0], lower]).astype(jnp.int32)
    first = gz[None]

    msg1, msg2, strip, strip1, strip2 = call(
        edge_kernel,
        [(PLANES, BY, 128), (PLANES, BY, 128), (BX, BY, 128), (DEEP, BY, 128), (DEEP, BY, 128)],
        [(3, BX, BY, BZ), (3, BX, BY, BZ), (BX, BY, BZ), pltpu.SemaphoreType.DMA((3,))],
        [first, start_field, forcing, modulus],
        1 << 20,
        pl.ANY,
    )
    x1 = send(msg1, lambda x, y, z: (x + turn(z), y, z))
    x2 = send(msg2, lambda x, y, z: (x - turn(z), y, z))
    far_strip = send(strip, lambda x, y, z: (x, y, 1 - z))
    far1 = send(strip1, lambda x, y, z: (x + turn(z), y, 1 - z))
    far2 = send(strip2, lambda x, y, z: (x - turn(z), y, 1 - z))
    own_u, own_f, y1, y2, a1, a2 = call(
        pack_kernel,
        [(WIN, BY, 128)] * 2 + [(WIN // 2, 40, 128)] * 2 + [(AX, 32, 128)] * 2,
        [(3, 36, BY, 128), (3, 36, BY, 128), (36, BY, 128), (36, BY, 128)],
        [scalar, start_field, forcing, modulus, x1, x2, far_strip, far1, far2],
        1 << 22,
    )
    r1 = send(y1, lambda x, y, z: (x, y + turn(z), z))
    r2 = send(y2, lambda x, y, z: (x, y - turn(z), z))
    b1 = send(a1, lambda x, y, z: (x, y + turn(z), z))
    b2 = send(a2, lambda x, y, z: (x, y - turn(z), z))
    window = (WIN, WY, 128)
    delta = call(
        functools.partial(zone_kernel, sizes),
        (16, 128),
        [window] * 8
        + [
            (8, 3, 16, 128), (13, 16, 128), (5, 16, 128), (5, 16, 128), (2, 16, 128), (16, 128),
            (PC, 128, 128), (5, 2, 128, 128), (5, 2, 128, 128), (2, 5, 256, 128), (2, 5, 8, 128), (PC, 8, 128), (PC, 8, 128),
        ],
        [scalar, own_u, own_f, r1, r2],
        1 << 33,
    )
    plane = jnp.stack([delta, send(delta, lambda x, y, z: (x, y, 1 - z))])
    right = send(plane, lambda x, y, z: (x, y + turn(z), z))
    left = send(plane, lambda x, y, z: (x, y - turn(z), z))
    wide = (AX, AX, 256)
    displacement = call(
        functools.partial(field_kernel, sizes),
        (3, BX, BY, BZ),
        [(3,) + wide] * 3 + [wide] * 5,
        [scalar, start_field, forcing, modulus, x1, x2, far_strip, far1, far2, b1, b2],
        1 << 30,
    )
    right, left, displacement = lax.optimization_barrier((right, left, displacement))
    plane = jnp.concatenate([plane, right, left])
    after = send(plane, lambda x, y, z: (x + turn(z), y, z))
    before = send(plane, lambda x, y, z: (x - turn(z), y, z))
    new_modulus = call(
        final_kernel,
        (BX, BY, BZ),
        [(BX * BY, 128)],
        [scalar, modulus, jnp.concatenate([plane, after, before])],
        1 << 24,
    )
    return displacement, new_modulus


def solution(mesh):
    placed = (
        P(None, "gx", "gy", "gz"),
        P(None, "gx", "gy", "gz"),
        P("gx", "gy", "gz"),
        P(("gx", "gy", "gz"), None),
    )
    return jax.shard_map(
        body,
        mesh=mesh,
        in_specs=placed,
        out_specs=(P(None, "gx", "gy", "gz"), P("gx", "gy", "gz")),
        check_vma=False,
    )
```

```python
import functools
import math

import jax
import jax.numpy as jnp
from jax import lax
from jax.experimental import pallas as pl
from jax.experimental.pallas import tpu as pltpu
from jax.sharding import PartitionSpec as P

PC = 10
SPAN = 2 * PC
FSWEEPS = 4
MASS_TERM = 0.5
DAMPING = 0.1
EPSILON = 1e-06
BX, BY, BZ = 16, 16, 128
HALO = 6
DEEP = 10
WIN = 30
WY = 32
AX = 24
ROWS = 104
TILES = ROWS // 8
PLANES = 3 * DEEP + 3 * (DEEP - 1) + DEEP
AXES = ("gx", "gy", "gz")
F32 = jnp.float32
BF16 = jnp.bfloat16
HIGH = lax.Precision.HIGHEST
VMEM_LIMIT = 48 * 1024 * 1024


def iota(shape, dim):
    return lax.broadcasted_iota(jnp.int32, shape, dim)


def lane_roll(values, shift):
    if isinstance(shift, int):
        shift = shift % values.shape[-1]
        return values if shift == 0 else pltpu.roll(values, shift, values.ndim - 1)
    size = values.shape[-1]
    return pltpu.roll(values, lax.rem(shift + 8 * size, size), values.ndim - 1)


def row_roll(values, shift):
    if isinstance(shift, int):
        shift = shift % values.shape[-2]
        return values if shift == 0 else pltpu.roll(values, shift, values.ndim - 2)
    size = values.shape[-2]
    return pltpu.roll(values, lax.rem(shift + 8 * size, size), values.ndim - 2)


def loop(low, high, step, unroll):
    whole = (high - low) // unroll
    if whole == 1:
        for i in range(low, low + unroll):
            step(i)
    elif whole > 1:

        def chunk(t, carry):
            for n in range(unroll):
                step(low + t * unroll + n)
            return carry

        lax.fori_loop(0, whole, chunk, 0)
    for i in range(low + whole * unroll, high):
        step(i)


def three_parts(values):
    first = values.astype(BF16)
    rest = values - first.astype(F32)
    second = rest.astype(BF16)
    third = (rest - second.astype(F32)).astype(BF16)
    return first, second, third


def dot(a, b):
    return lax.dot_general(a, b, (((1,), (0,)), ((), ())), precision=HIGH, preferred_element_type=F32)


def dot_exact(values, selector):
    parts = [
        lax.dot_general(part, selector, (((1,), (0,)), ((), ())), preferred_element_type=F32)
        for part in three_parts(values)
    ]
    return parts[0] + parts[1] + parts[2]


def div10(value):
    return lax.shift_right_arithmetic(value * 205, 11)


def edge_kernel(sc, u, f, m, msg1, msg2, strip, strip1, strip2, vu, vf, vm, sems):
    gz = sc[0]
    low_first = gz == 0
    s1 = jnp.where(low_first, BX - DEEP, 0)
    s2 = BX - DEEP - s1
    f1 = jnp.where(low_first, BX - DEEP + 1, 0)
    f2 = BX - DEEP + 1 - f1
    loads = [pltpu.make_async_copy(u, vu, sems.at[0]), pltpu.make_async_copy(f, vf, sems.at[1])]
    loads.append(pltpu.make_async_copy(m, vm, sems.at[2]))
    for load in loads:
        load.start()
    for load in loads:
        load.wait()
    lane = iota((BY, 128), 1)
    extra = jnp.where(low_first, DEEP, 0)

    def one(x):
        total = jnp.zeros((BY, 128), F32)
        for c in range(7):
            source = vu[c, x] if c < 3 else (vf[c - 3, x] if c < 6 else vm[x])
            moved = lane_roll(source, extra + DEEP * c)
            total = jnp.where((lane >= DEEP * c) & (lane < DEEP * (c + 1)), moved, total)
        strip[x] = total

    loop(0, BX, one, 8)
    for out, s, fs in ((msg1, s1, f1), (msg2, s2, f2)):
        for k in range(3):
            out[k * DEEP : (k + 1) * DEEP] = vu[k, pl.ds(s, DEEP)]
            base = 3 * DEEP + k * (DEEP - 1)
            out[base : base + DEEP - 1] = vf[k, pl.ds(fs, DEEP - 1)]
        out[PLANES - DEEP : PLANES] = vm[pl.ds(s, DEEP)]
    strip1[...] = strip[pl.ds(s1, DEEP)]
    strip2[...] = strip[pl.ds(s2, DEEP)]


def pack_kernel(sc, u, f, m, x1, x2, strip, strip1, strip2, own_u, own_f, msg1, msg2, side1, side2, eu, ef, em, es):
    gz = sc[0]
    low_first = gz == 0
    p1 = jnp.where(low_first, 0, BX + DEEP)
    p2 = BX + DEEP - p1
    q1 = jnp.where(low_first, 1, BX + DEEP)
    q2 = BX + DEEP + 1 - q1
    for k in range(3):
        eu[k, DEEP : DEEP + BX] = u[k]
        ef[k, DEEP : DEEP + BX] = f[k]
        ef[k, 0] = jnp.zeros((BY, 128), F32)
        ef[k, 2 * DEEP + BX - 1] = jnp.zeros((BY, 128), F32)
        for msg, p, q in ((x1, p1, q1), (x2, p2, q2)):
            eu[k, pl.ds(p, DEEP)] = msg[k * DEEP : (k + 1) * DEEP]
            base = 3 * DEEP + k * (DEEP - 1)
            ef[k, pl.ds(q, DEEP - 1)] = msg[base : base + DEEP - 1]
    em[DEEP : DEEP + BX] = m[...]
    es[DEEP : DEEP + BX] = strip[...]
    em[pl.ds(p1, DEEP)] = x1[PLANES - DEEP : PLANES]
    em[pl.ds(p2, DEEP)] = x2[PLANES - DEEP : PLANES]
    es[pl.ds(p2, DEEP)] = strip1[...]
    es[pl.ds(p1, DEEP)] = strip2[...]

    lane = iota((BY, 128), 1)
    group = lax.shift_right_arithmetic(lane, 5)
    inner = lane & 31
    zoff = jnp.where(low_first, BZ, -DEEP)

    def window(relz):
        w0 = relz - (DEEP - 5)
        z = inner + w0
        main_ok = (z >= 0) & (z < BZ)
        strip_ok = (z >= zoff) & (z < zoff + DEEP)

        def take(x):
            side = es[x]
            values = []
            for sources in ((eu, 0), (ef, 3)):
                ref, first = sources
                main = jnp.zeros((BY, 128), F32)
                far = jnp.zeros((BY, 128), F32)
                for k in range(4 if first == 0 else 3):
                    source, c = (ref[k, x], first + k) if k < 3 else (em[x], 6)
                    main = jnp.where(group == k, lane_roll(source, 32 * k - w0), main)
                    far = jnp.where(group == k, lane_roll(side, 32 * k + zoff - w0 - DEEP * c), far)
                values.append(jnp.where(main_ok, main, jnp.where(strip_ok, far, 0.0)))
            return values

        return take

    take_own = window(sc[3])
    x0 = sc[1] + 5

    def own(i):
        field, force = take_own(x0 + i)
        own_u[i] = field
        own_f[i] = force

    loop(0, WIN, own, 6)

    sub = iota((8, 128), 0)
    for msg, side, base, upward in ((msg1, side1, 4, low_first), (msg2, side2, 7, gz != 0)):
        take = window(sc[base + 2])
        start = sc[base] + 5

        def pair(i, msg=msg, take=take, start=start, upward=upward):
            mixed = jnp.zeros((8, 128), F32)
            number = 0
            for step in range(2):
                for values in take(start + 2 * i + step):
                    top, bottom = values[0:8], values[8:16]
                    msg[i, 8 * number : 8 * number + 8] = jnp.where(upward, bottom, top)
                    edge = jnp.where(upward, row_roll(top, 2), bottom)
                    mixed = jnp.where((sub >= 2 * number) & (sub < 2 * number + 2), row_roll(edge, 2 * number), mixed)
                    number += 1
            msg[i, 32:40] = mixed

        loop(0, WIN // 2, pair, 3)

        def plane(i, side=side, upward=upward):
            x = i + DEEP - FSWEEPS

            def edge(values):
                return jnp.where(upward, row_roll(values[8:16], 4), values[0:8])

            every = [edge(eu[k, x]) for k in range(3)] + [edge(ef[k, x]) for k in range(3)] + [edge(em[x]), edge(es[x])]
            for j in range(4):
                side[i, 8 * j : 8 * j + 8] = jnp.where(sub < 4, every[2 * j], row_roll(every[2 * j + 1], 4))

        loop(0, AX, plane, 6)


def invert(chains):
    sub = iota((8, 128), 0)
    lane = iota((8, 128), 1)

    def row_of(values, j):
        return jnp.broadcast_to(values[j : j + 1, :], (8, 128))

    def column_of(values, j):
        return jnp.broadcast_to(values[:, j : j + 1], (8, 128))

    empty = jnp.zeros((8, 128), F32)

    def eliminate(b, tile):
        own = [column_of(tile, 8 * b + j) for j in range(8)]
        for j in range(0, 8, 2):
            here0, here1 = sub == j, sub == j + 1
            at0, at1 = lane == 8 * b + j, lane == 8 * b + j + 1
            p00, p01 = row_of(own[j], j), row_of(own[j + 1], j)
            p10, p11 = row_of(own[j], j + 1), row_of(own[j + 1], j + 1)
            scale = pl.reciprocal(p00 * p11 - p01 * p10, approx=True)
            side0 = jnp.where(here0, -1.0, jnp.where(here1, 0.0, own[j]))
            side1 = jnp.where(here0, 0.0, jnp.where(here1, -1.0, own[j + 1]))
            both = here0 | here1

            def step(values, line0, line1):
                first = p11 * line0 - p01 * line1
                second = p00 * line1 - p10 * line0
                return jnp.where(both, 0.0, values) - (side0 * first + side1 * second) * scale

            for n in range(j + 2, 8):
                own[n] = step(own[n], row_of(own[n], j), row_of(own[n], j + 1))
            line0 = jnp.where(at0, 1.0, jnp.where(at1, 0.0, row_of(tile, j)))
            line1 = jnp.where(at0, 0.0, jnp.where(at1, 1.0, row_of(tile, j + 1)))
            tile = step(jnp.where(at0 | at1, 0.0, tile), line0, line1)
        return tile

    def reduced(b, tile, pivot):
        terms = [column_of(tile, 8 * b + j) * row_of(pivot, j) for j in range(8)]
        while len(terms) > 1:
            terms = [p + q for p, q in zip(terms[0::2], terms[1::2])]
        return jnp.where((lane >= 8 * b) & (lane < 8 * b + 8), 0.0, tile) - terms[0]

    for first in range(0, TILES, 2):
        blocks = [b for b in (first, first + 1) if b < TILES]
        in_blocks = (lane >= 8 * first) & (lane < 8 * first + 8 * len(blocks))
        before = [list(chain) for chain in chains]
        for b in blocks:
            for chain in chains:
                chain[b] = eliminate(b, chain[b])
                for i in range(first, min(first + 4, TILES)):
                    if i != b:
                        chain[i] = reduced(b, chain[i], chain[b])
        for chain, old in zip(chains, before):
            spread = jnp.concatenate([chain[r] if r in blocks else empty for r in range(16)], axis=0)
            change = dot(jnp.concatenate(old, axis=0), spread)
            for i in range(TILES):
                if not first <= i < first + 4:
                    chain[i] = jnp.where(in_blocks, 0.0, old[i]) - change[8 * i : 8 * i + 8]
    return chains


OFFSETS = (0, PC, -PC, 1, -1)
BANDS = (0, 1, 2, 9, 10, 11, 20)


def zone_kernel(
    sizes, sc, own_u, own_f, r1, r2, out,
    ua, ub, fo, m3, cx, cy, cz, iv, rows, band, up, down, far, grad, hess, bl, br, yt, zs, dl, gs,
):
    nx, ny, nz = sizes
    low_first = sc[0] == 0
    rely = sc[2]
    lane32 = iota((WY, 128), 1)
    group = lax.shift_right_arithmetic(lane32, 5)
    inner = lane32 & 31
    row32 = iota((WY, 128), 0)
    shift = -(rely + 11)

    inside_y = sc[11] - 5 + row32
    inside_z = sc[12] - 5 + inner
    inside = (inside_y >= 0) & (inside_y < ny) & (inside_z >= 0) & (inside_z < nz)

    def unpack(i):
        for step in range(2):
            gx = sc[10] - 5 + 2 * i + step
            good = inside & (gx >= 0) & (gx < nx)
            for which in range(2):
                number = 2 * step + which
                first = r1[i, 8 * number : 8 * number + 8]
                second = r2[i, 8 * number : 8 * number + 8]
                mix1 = r1[i, 32:40]
                mix2 = r2[i, 32:40]
                low, high = jnp.where(low_first, first, second), jnp.where(low_first, second, first)
                low_mix, high_mix = jnp.where(low_first, mix1, mix2), jnp.where(low_first, mix2, mix1)
                middle = own_u[2 * i + step] if which == 0 else own_f[2 * i + step]
                tall = jnp.concatenate(
                    [row_roll(low_mix, 6 - 2 * number), low, middle, high, row_roll(high_mix, -2 * number)], axis=0
                )
                tall = row_roll(tall, shift)[0:WY]
                if which == 0:
                    tall = jnp.where(good, tall, 0.0)
                    ua[2 * i + step] = tall
                    moved = jnp.where(group == 0, lane_roll(tall, 32), 0.0)
                    moved = jnp.where(group == 1, lane_roll(tall, 64), moved)
                    m3[2 * i + step] = jnp.where(group == 2, lane_roll(tall, 96), moved)
                else:
                    fo[2 * i + step] = tall

    loop(0, WIN // 2, unpack, 3)

    def faces(i):
        here = m3[i]
        cx[i] = 0.5 * (here + m3[jnp.minimum(i + 1, WIN - 1)])
        cy[i] = 0.5 * (here + row_roll(here, -1))
        cz[i] = 0.5 * (here + lane_roll(here, -1))

    loop(0, WIN, faces, 15)

    def scale(i):
        total = MASS_TERM + cx[i] + cx[i - 1] + cy[i] + row_roll(cy[i], 1) + cz[i] + lane_roll(cz[i], 1)
        gx = sc[10] - 5 + i
        good = inside & (gx >= 0) & (gx < nx)
        iv[i] = jnp.where(good, 1.0 / total, 0.0)

    loop(1, WIN - 1, scale, 14)

    for sweep in range(FSWEEPS):
        src, dst = (ua, ub) if sweep % 2 == 0 else (ub, ua)

        def relax(i, src=src, dst=dst):
            here = src[i]
            total = fo[i] + cx[i] * src[i + 1] + cx[i - 1] * src[i - 1]
            total = total + cy[i] * row_roll(here, -1) + row_roll(cy[i] * here, 1)
            total = total + cz[i] * lane_roll(here, -1) + lane_roll(cz[i] * here, 1)
            dst[i] = total * iv[i]

        loop(sweep + 1, WIN - 1 - sweep, relax, WIN - 2 - 2 * sweep)

    line = iota((128, 384), 0)
    column = iota((128, 384), 1)
    part = lax.shift_right_arithmetic(column, 7)
    spot = column & 127
    spot_y = div10(spot)
    spot_z = spot - PC * spot_y
    inner_z = (line & 31) - 5
    hit = (lax.shift_right_arithmetic(line, 5) == part) & (inner_z >= 0) & (inner_z < SPAN) & (spot < PC * PC)
    hit = hit & (lax.shift_right_arithmetic(inner_z, 1) == spot_z)
    selector = jnp.where(hit, 1.0, 0.0).astype(BF16)
    zone_y = row32 - 5
    lane_y = div10(lane32)
    pick_y = (zone_y >= 0) & (zone_y < SPAN) & (lax.shift_right_arithmetic(zone_y, 1) == lane_y) & (lane32 < PC * PC)
    pick_y = jnp.where(pick_y, 1.0, 0.0)
    even_y = (zone_y & 1) == 0
    even_z = ((inner - 5) & 1) == 0
    rows[...] = jnp.zeros(rows.shape, F32)

    def layer(a):
        sums = None
        for odd in range(2):
            i = 5 + 2 * a + odd
            here, m_here = ua[i], m3[i]
            ch_x, ch_b = here - ua[i + 1], ua[i - 1] - here
            ch_y = here - row_roll(here, -1)
            ch_z = here - lane_roll(here, -1)
            flow_y, flow_z = cy[i] * ch_y, cz[i] * ch_z
            applied = MASS_TERM * here + cx[i] * ch_x - cx[i - 1] * ch_b
            applied = applied + flow_y - row_roll(flow_y, 1) + flow_z - lane_roll(flow_z, 1)
            resid = fo[i] - applied
            back_y, back_z = row_roll(ch_y, 1), lane_roll(ch_z, 1)
            laplace = ch_x - ch_b + ch_y - back_y + ch_z - back_z
            xp = -0.5 * m3[i + 1] * ch_x
            xm = 0.5 * m3[i - 1] * ch_b
            yp = -0.5 * row_roll(m_here, -1) * ch_y
            ym = 0.5 * row_roll(m_here, 1) * back_y
            zp = -0.5 * lane_roll(m_here, -1) * ch_z
            zm = 0.5 * lane_roll(m_here, 1) * back_z
            diag = -0.5 * m_here * laplace + jnp.where(even_y, yp, ym) + jnp.where(even_z, zp, zm)
            diag = diag + (xm if odd else xp)
            now = [
                diag, xp if odd else None, None if odd else xm,
                jnp.where(even_y, 0.0, yp), jnp.where(even_y, ym, 0.0),
                jnp.where(even_z, 0.0, zp), jnp.where(even_z, zm, 0.0), resid,
            ]
            if sums is None:
                sums = now
            else:
                sums = [p if q is None else (q if p is None else p + q) for p, q in zip(sums, now)]
        tall = dot_exact(jnp.concatenate(sums, axis=0), selector)
        for n in range(8):
            for k in range(3):
                piece = tall[n * WY : (n + 1) * WY, 128 * k : 128 * k + 128] * pick_y
                rows[n, k, pl.ds(a, 1), :] = jnp.sum(piece, axis=0, keepdims=True)

    loop(0, PC, layer, 5)

    lane16 = iota((16, 128), 1)
    row16 = iota((16, 128), 0)
    at_y = div10(lane16)
    at_z = lane16 - PC * at_y

    def masked(n, keep):
        return [jnp.where(keep, rows[n, k], 0.0) for k in range(3)]

    full = row16 < PC
    v = {
        0: masked(0, full),
        PC: masked(3, full & (at_y < PC - 1)),
        -PC: masked(4, full & (at_y > 0)),
        1: masked(5, full & (at_z < PC - 1)),
        -1: masked(6, full & (at_z > 0)),
    }
    vxp = masked(1, row16 < PC - 1)
    vxm = masked(2, full & (row16 > 0))
    res = masked(7, full)

    def mix(p, q):
        return p[0] * q[0] + p[1] * q[1] + p[2] * q[2]

    bands = {}
    for o1 in OFFSETS:
        for o2 in OFFSETS:
            key = o1 - o2
            if key >= 0:
                term = lane_roll(mix(v[o1], v[o2]), o2)
                bands[key] = bands[key] + term if key in bands else term
    bands[0] = bands[0] + row_roll(mix(vxp, vxp), 1) + row_roll(mix(vxm, vxm), -1)
    trace = jnp.sum(jnp.sum(bands[0], axis=1, keepdims=True), axis=0, keepdims=True)
    ridge = DAMPING * trace / PC**3 + EPSILON
    bands[0] = jnp.where(lane16 < PC * PC, bands[0] + ridge, jnp.where(lane16 < ROWS, 1.0, 0.0))
    slots = {}
    for n, key in enumerate(BANDS):
        band[n] = bands[key]
        slots[key] = n
    for n, key in enumerate(BANDS[1:]):
        band[len(BANDS) + n] = lane_roll(bands[key], key)
        slots[-key] = len(BANDS) + n
    for n, key in enumerate(OFFSETS):
        above = row_roll(mix(vxm, v[-key]), -1)
        below = row_roll(mix(vxp, v[-key]), 1)
        up[n] = mix(vxp, v[key]) + lane_roll(above, -key)
        down[n] = mix(vxm, v[key]) + lane_roll(below, -key)
    cross = mix(vxm, vxp)
    far[0] = row_roll(cross, -1)
    far[1] = row_roll(cross, 1)
    gradient = row_roll(mix(vxp, res), 1) + row_roll(mix(vxm, res), -1)
    for key in OFFSETS:
        gradient = gradient + lane_roll(mix(v[key], res), key)
    grad[...] = gradient

    sub = iota((8, 128), 0)
    lane8 = iota((8, 128), 1)

    def spread(ref, n, x):
        return jnp.broadcast_to(ref[n, pl.ds(x, 1), :], (8, 128))

    def fill(dst, lines, lead):
        for r in range(TILES):
            apart = sub + 8 * r - lane8
            tile = jnp.zeros((8, 128), F32)
            for key, values in lines:
                if 8 * r + 7 - key >= 0 and 8 * r - key < 128:
                    tile = jnp.where(apart == key, values, tile)
            dst[lead + (slice(8 * r, 8 * r + 8), slice(None))] = tile
        dst[lead + (slice(ROWS, 128), slice(None))] = jnp.zeros((128 - ROWS, 128), F32)

    def dense(x, carry):
        fill(hess, [(key, spread(band, n, x)) for key, n in slots.items()], (x,))
        gs[x] = jnp.broadcast_to(grad[pl.ds(x, 1), :], (8, 128))
        return carry

    lax.fori_loop(0, PC, dense, 0)

    def couple(t, carry):
        right = PC - 1 - t
        fill(bl, [(key, spread(up, n, t)) for n, key in enumerate(OFFSETS)], (t, 0))
        fill(bl, [(key, spread(down, n, t + 1)) for n, key in enumerate(OFFSETS)], (t, 1))

        @pl.when(t < 4)
        def _():
            fill(br, [(key, spread(down, n, right)) for n, key in enumerate(OFFSETS)], (t, 0))
            fill(br, [(key, spread(up, n, right - 1)) for n, key in enumerate(OFFSETS)], (t, 1))

        return carry

    lax.fori_loop(0, 5, couple, 0)
    br[4] = jnp.zeros((2, 128, 128), F32)

    on_diagonal = iota((128, 128), 0) == iota((128, 128), 1)
    ones = jnp.ones((128, 128), BF16)

    def tiles_of(x):
        return [hess[x, 8 * r : 8 * r + 8, :] for r in range(TILES)]

    def whole(chain):
        return jnp.concatenate(chain + [jnp.zeros((128 - ROWS, 128), F32)], axis=0)

    def eliminate(t, carry):
        right = PC - 1 - t
        left_tiles, right_tiles = invert([tiles_of(t), tiles_of(right)])
        for s, tiles, x, step, ref in ((0, left_tiles, t, 1, bl), (1, right_tiles, right, -1, br)):
            q = whole(tiles)
            row = jnp.broadcast_to(far[s, pl.ds(x, 1), :], (128, 128))
            column = dot_exact(jnp.where(on_diagonal, row, 0.0), ones)
            w, wt = ref[t, 0], ref[t, 1]
            y1, y2 = dot(q, w), q * row
            yt[s, t, 0:128] = dot(wt, q)
            yt[s, t, 128:256] = column * q
            s1 = dot(wt, jnp.concatenate([y1, y2], axis=1))
            g = gs[x]
            z = dot(g, q)
            zs[s, t] = z
            one, two_on = x + step, x + 2 * step
            hess[one] = hess[one] - s1[:, 0:128]
            hess[two_on] = hess[two_on] - column * y2
            ref[t + 1, 0] = ref[t + 1, 0] - s1[:, 128:256]
            ref[t + 1, 1] = ref[t + 1, 1] - column * y1
            gs[one] = gs[one] - dot(z, w)
            gs[two_on] = gs[two_on] - z * row[0:8]
        return carry

    lax.fori_loop(0, 4, eliminate, 0)

    def middle(t, carry):
        x = 4 + t
        (tiles,) = invert([tiles_of(x)])
        q = whole(tiles)
        g = gs[x]
        dl[x] = dot(g, q)

        @pl.when(t == 0)
        def _():
            w = bl[4, 0] + br[4, 1]
            wt = bl[4, 1] + br[4, 0]
            y = dot(q, w)
            yt[0, 4, 0:128] = dot(wt, q)
            hess[5] = hess[5] - dot(wt, y)
            gs[5] = gs[5] - dot(g, y)

        return carry

    lax.fori_loop(0, 2, middle, 0)
    dl[4] = dl[4] - dot(dl[5], yt[0, 4, 0:128])
    for t in (3, 2, 1, 0):
        right = PC - 1 - t
        dl[t] = zs[0, t] - dot(jnp.concatenate([dl[t + 1], dl[t + 2]], axis=1), yt[0, t])
        dl[right] = zs[1, t] - dot(jnp.concatenate([dl[right - 1], dl[right - 2]], axis=1), yt[1, t])
    for x in range(PC):
        out[x : x + 1, :] = -dl[x, 0:1, :]
    spare = iota((16 - PC, 128), 1)
    corner = jnp.zeros((16 - PC, 128), F32)
    for n in range(3):
        corner = jnp.where(spare == n, sc[10 + n].astype(F32), corner)
    out[PC:16, :] = corner


def field_kernel(
    sizes, sc, u, f, m, x1, x2, strip, strip1, strip2, s1, s2, out,
    ua, ub, fo, mo, cx, cy, zu, zd, ze, iv, ba, bb, bf, bm, bx, by, bz, bi,
):
    nx, ny, nz = sizes
    low_first = sc[0] == 0
    sub = iota((8, 128), 0)
    lane = iota((AX, 128), 1)
    group = lax.shift_right_arithmetic(lane, 5)
    inner = lane & 31
    lead = DEEP - FSWEEPS
    w0 = jnp.where(low_first, BZ - 8, -8)
    zoff = jnp.where(low_first, BZ, -DEEP)
    z = inner + w0
    main_ok = (z >= 0) & (z < BZ)
    far_ok = (z >= zoff) & (z < zoff + DEEP)
    edge_lane = jnp.where(low_first, BZ - 1, 0)
    edge_from = jnp.where(low_first, 8, 7)
    at_edge = lane == edge_lane
    row24 = iota((AX, 128), 0)
    gy = sc[14] - FSWEEPS + row24
    inside = (gy >= 0) & (gy < ny)

    def build(dest, values16):
        gx = sc[13] - FSWEEPS + dest
        good = inside & (gx >= 0) & (gx < nx)
        every = []
        for q in range(8):
            j = q // 2
            a = s1[dest, 8 * j : 8 * j + 8]
            b = s2[dest, 8 * j : 8 * j + 8]
            low, high = jnp.where(low_first, a, b), jnp.where(low_first, b, a)
            if q % 2 == 0:
                high = row_roll(high, 4)
            else:
                low = row_roll(low, 4)
            t0, t1 = row_roll(values16[q][0:8], 4), row_roll(values16[q][8:16], 4)
            tall = jnp.concatenate(
                [jnp.where(sub < 4, low, t0), jnp.where(sub < 4, t0, t1), jnp.where(sub < 4, t1, high)], axis=0
            )
            every.append(jnp.where(good, tall, 0.0))
        for k in range(3):
            ua[k, dest] = every[k]
            fo[k, dest] = every[3 + k]
        mo[dest] = every[6]
        side = []
        for channels in ((0, 1, 2), (3, 4, 5)):
            main, far = jnp.zeros((AX, 128), F32), jnp.zeros((AX, 128), F32)
            for k, c in enumerate(channels):
                main = jnp.where(group == k, lane_roll(every[c], 32 * k - w0), main)
                far = jnp.where(group == k, lane_roll(every[7], 32 * k + zoff - w0 - DEEP * c), far)
            side.append(jnp.where(main_ok, main, jnp.where(far_ok, far, 0.0)))
        ba[dest], bf[dest] = side
        main = jnp.where(main_ok, lane_roll(every[6], -w0), jnp.where(far_ok, lane_roll(every[7], zoff - w0 - DEEP * 6), 0.0))
        first = jnp.where(group == 0, main, 0.0)
        first = jnp.where(group == 1, lane_roll(main, 32), first)
        bm[dest] = jnp.where(group == 2, lane_roll(main, 64), first)

    def inner_plane(i):
        build(i + FSWEEPS, [u[k, i] for k in range(3)] + [f[k, i] for k in range(3)] + [m[i], strip[i]])

    loop(0, BX, inner_plane, 4)

    def outer_plane(i):
        for a, b, sa, sb, start, dest in (
            (x1, x2, strip2, strip1, lead, i), (x2, x1, strip1, strip2, 0, i + FSWEEPS + BX),
        ):
            j = i + start
            force = j - (1 if start else 0)

            def pick(index):
                return jnp.where(low_first, a[index], b[index])

            build(
                dest,
                [pick(k * DEEP + j) for k in range(3)]
                + [pick(3 * DEEP + k * (DEEP - 1) + force) for k in range(3)]
                + [pick(PLANES - DEEP + j), jnp.where(low_first, sa[j], sb[j])],
            )

    loop(0, FSWEEPS, outer_plane, 2)

    def edge(values, k):
        return jnp.where(at_edge, lane_roll(values, edge_lane - edge_from - 32 * k), 0.0)

    def faces(i):
        here, there = mo[i], bm[i]
        cx[i] = 0.5 * (here + mo[jnp.minimum(i + 1, AX - 1)])
        bx[i] = 0.5 * (there + bm[jnp.minimum(i + 1, AX - 1)])
        cy[i] = 0.5 * (here + row_roll(here, -1))
        by[i] = 0.5 * (there + row_roll(there, -1))
        bz[i] = 0.5 * (there + lane_roll(there, -1))
        zu[i] = jnp.where(lane == BZ - 1, 0.0, 0.5 * (here + lane_roll(here, -1)))
        zd[i] = jnp.where(lane == 0, 0.0, 0.5 * (here + lane_roll(here, 1)))
        ze[i] = jnp.where(at_edge, 0.5 * (here + edge(there, 0)), 0.0)

    loop(0, AX, faces, 12)
    side_inside = (sc[15] + z >= 0) & (sc[15] + z < nz)
    far_edge = BZ - 1 - edge_lane

    def scale(i):
        open_face = jnp.where(lane == far_edge, 0.5 * mo[i], 0.0)
        total = MASS_TERM + cx[i] + cx[i - 1] + cy[i] + row_roll(cy[i], 1) + zu[i] + zd[i] + ze[i] + open_face
        gx = sc[13] - FSWEEPS + i
        good = inside & (gx >= 0) & (gx < nx)
        iv[i] = jnp.where(good, 1.0 / total, 0.0)
        total = MASS_TERM + bx[i] + bx[i - 1] + by[i] + row_roll(by[i], 1) + bz[i] + lane_roll(bz[i], 1)
        bi[i] = jnp.where(good & side_inside, 1.0 / total, 0.0)

    loop(1, AX - 1, scale, 11)
    for sweep in range(FSWEEPS):
        src, dst = (ua, ub) if sweep % 2 == 0 else (ub, ua)
        bsrc, bdst = (ba, bb) if sweep % 2 == 0 else (bb, ba)

        def relax(i, src=src, dst=dst, bsrc=bsrc, bdst=bdst, last=sweep == FSWEEPS - 1):
            there = bsrc[i]
            for k in range(3):
                here = src[k, i]
                total = fo[k, i] + cx[i] * src[k, i + 1] + cx[i - 1] * src[k, i - 1]
                total = total + cy[i] * row_roll(here, -1) + row_roll(cy[i] * here, 1)
                total = total + zu[i] * lane_roll(here, -1) + zd[i] * lane_roll(here, 1) + ze[i] * edge(there, k)
                total = total * iv[i]
                if last:
                    out[k, i - FSWEEPS] = row_roll(total, -FSWEEPS)[0:BY]
                else:
                    dst[k, i] = total
            if not last:
                total = bf[i] + bx[i] * bsrc[i + 1] + bx[i - 1] * bsrc[i - 1]
                total = total + by[i] * row_roll(there, -1) + row_roll(by[i] * there, 1)
                total = total + bz[i] * lane_roll(there, -1) + lane_roll(bz[i] * there, 1)
                bdst[i] = total * bi[i]

        loop(sweep + 1, AX - 1 - sweep, relax, AX - 2 - 2 * sweep)


def taper(offset):
    folded = jnp.minimum(offset, SPAN - 1 - offset)
    total = jnp.zeros(offset.shape, F32)
    for n in range(PC):
        total = jnp.where(folded == float(n), math.sin(math.pi * (n + 0.5) / SPAN), total)
    return total


def contribution(sc, delta, start, planes):
    rows = 16 if planes > 8 else 8
    laneix = iota((rows, 128), 1)
    lane16i = iota((16, 128), 1)
    lane_y = div10(lane16i).astype(F32)
    rows128 = iota((128, 128), 0)
    rows_z = (rows128 - PC * div10(rows128)).astype(F32)

    def place(axis):
        return delta[PC : PC + 1, axis : axis + 1] - sc[13 + axis].astype(F32)

    off_x = (iota((rows, 128), 0) + start).astype(F32) - place(0)
    apart = off_x - 2.0 * laneix.astype(F32)
    choose = jnp.where((apart >= 0.0) & (apart < 2.0) & (laneix < PC), 1.0, 0.0).astype(BF16)[:, 0:16]
    picked = [lax.dot_general(choose, p, (((1,), (0,)), ((), ())), preferred_element_type=F32) for p in three_parts(delta)]
    lines = (picked[0] + picked[1] + picked[2]) * taper(off_x)
    off_y = iota((16, 128), 0).astype(F32) - place(1)
    apart = off_y - 2.0 * lane_y
    cover = jnp.where((apart >= 0.0) & (apart < 2.0) & (lane16i < PC * PC), taper(off_y), 0.0)
    off_z = iota((128, 128), 1).astype(F32) - place(2)
    apart = off_z - 2.0 * rows_z
    expand = jnp.where((apart >= 0.0) & (apart < 2.0) & (rows128 < PC * PC), 1.0, 0.0).astype(BF16)
    tall = jnp.concatenate([jnp.broadcast_to(lines[x : x + 1, :], (BY, 128)) * cover for x in range(planes)], axis=0)
    return dot_exact(tall, expand) * taper(off_z[0:1, :])


def near_kernel(sc, parts, acc):
    acc[...] = jnp.zeros(acc.shape, F32)

    def add(n):
        acc[...] += contribution(sc, parts[n], 0, BX)

    loop(0, parts.shape[0], add, 3)


def final_kernel(sc, m, near, parts1, parts2, out, acc):
    acc[...] = near[...]
    reach = HALO - 1
    start1 = jnp.where(sc[0] == 0, 0, BX - reach)
    start2 = BX - reach - start1

    def add(n):
        for parts, start in ((parts1, start1), (parts2, start2)):
            where = pl.ds(pl.multiple_of(start * BY, BY), reach * BY)
            acc[where, :] += contribution(sc, parts[n], start, reach)

    loop(0, parts1.shape[0], add, 3)
    for x in range(BX):
        out[x] = m[x] * (1.0 + acc[16 * x : 16 * x + 16, :])


def call(kernel, shapes, scratch, inputs, flops, space=pltpu.VMEM):
    specs = [pl.BlockSpec(memory_space=pltpu.SMEM)] + [pl.BlockSpec(memory_space=space)] * (len(inputs) - 1)
    single = not isinstance(shapes, list)
    outs = [jax.ShapeDtypeStruct(s, F32) for s in ([shapes] if single else shapes)]
    results = pl.pallas_call(
        kernel,
        out_shape=outs,
        in_specs=specs,
        out_specs=[pl.BlockSpec(memory_space=pltpu.VMEM)] * len(outs),
        scratch_shapes=[pltpu.VMEM(s, F32) if isinstance(s, tuple) else s for s in scratch],
        compiler_params=pltpu.CompilerParams(vmem_limit_bytes=VMEM_LIMIT),
        cost_estimate=pl.CostEstimate(flops=flops, bytes_accessed=1 << 20, transcendentals=0),
    )(*inputs)
    return results[0] if single else results


def body(forcing, start_field, modulus, corners):
    counts = tuple(lax.axis_size(axis) for axis in AXES)
    sizes = (counts[0] * BX, counts[1] * BY, counts[2] * BZ)
    place = tuple(lax.axis_index(axis) for axis in AXES)
    gz = place[2].astype(jnp.int32)
    lower = jnp.stack([place[0] * BX, place[1] * BY, place[2] * BZ]).astype(jnp.int32)

    def send(values, move):
        pairs = []
        for x in range(counts[0]):
            for y in range(counts[1]):
                for z in range(counts[2]):
                    to = [t % c for t, c in zip(move(x, y, z), counts)]
                    pairs.append(((x * counts[1] + y) * counts[2] + z, (to[0] * counts[1] + to[1]) * counts[2] + to[2]))
        return lax.ppermute(values, AXES, pairs)

    def turn(z):
        return 1 if z == 0 else -1

    relative = corners[0] - lower
    near = jnp.broadcast_to(relative[None, :], (1, 3))
    want1 = send(near, lambda x, y, z: (x, y - turn(z), z))
    want2 = send(near, lambda x, y, z: (x, y + turn(z), z))
    scalar = jnp.concatenate([gz[None], relative, want1[0], want2[0], corners[0], lower]).astype(jnp.int32)
    first = gz[None]

    msg1, msg2, strip, strip1, strip2 = call(
        edge_kernel,
        [(PLANES, BY, 128), (PLANES, BY, 128), (BX, BY, 128), (DEEP, BY, 128), (DEEP, BY, 128)],
        [(3, BX, BY, BZ), (3, BX, BY, BZ), (BX, BY, BZ), pltpu.SemaphoreType.DMA((3,))],
        [first, start_field, forcing, modulus],
        1 << 20,
        pltpu.HBM,
    )
    x1 = send(msg1, lambda x, y, z: (x + turn(z), y, z))
    x2 = send(msg2, lambda x, y, z: (x - turn(z), y, z))
    far_strip = send(strip, lambda x, y, z: (x, y, 1 - z))
    far1 = send(strip1, lambda x, y, z: (x + turn(z), y, 1 - z))
    far2 = send(strip2, lambda x, y, z: (x - turn(z), y, 1 - z))
    own_u, own_f, y1, y2, a1, a2 = call(
        pack_kernel,
        [(WIN, BY, 128)] * 2 + [(WIN // 2, 40, 128)] * 2 + [(AX, 32, 128)] * 2,
        [(3, 36, BY, 128), (3, 36, BY, 128), (36, BY, 128), (36, BY, 128)],
        [scalar, start_field, forcing, modulus, x1, x2, far_strip, far1, far2],
        1 << 22,
    )
    r1 = send(y1, lambda x, y, z: (x, y + turn(z), z))
    r2 = send(y2, lambda x, y, z: (x, y - turn(z), z))
    b1 = send(a1, lambda x, y, z: (x, y + turn(z), z))
    b2 = send(a2, lambda x, y, z: (x, y - turn(z), z))
    window = (WIN, WY, 128)
    delta = call(
        functools.partial(zone_kernel, sizes),
        (16, 128),
        [window] * 8
        + [
            (8, 3, 16, 128), (13, 16, 128), (5, 16, 128), (5, 16, 128), (2, 16, 128), (16, 128),
            (PC, 128, 128), (5, 2, 128, 128), (5, 2, 128, 128), (2, 5, 256, 128), (2, 5, 8, 128), (PC, 8, 128), (PC, 8, 128),
        ],
        [scalar, own_u, own_f, r1, r2],
        1 << 33,
    )
    plane = jnp.stack([delta, send(delta, lambda x, y, z: (x, y, 1 - z))])
    right = send(plane, lambda x, y, z: (x, y + turn(z), z))
    left = send(plane, lambda x, y, z: (x, y - turn(z), z))
    wide = (AX, AX, 128)
    displacement = call(
        functools.partial(field_kernel, sizes),
        (3, BX, BY, BZ),
        [(3,) + wide] * 3 + [wide] * 15,
        [scalar, start_field, forcing, modulus, x1, x2, far_strip, far1, far2, b1, b2],
        1 << 30,
    )
    right, left, displacement = lax.optimization_barrier((right, left, displacement))
    plane = jnp.concatenate([plane, right, left])
    after = send(plane, lambda x, y, z: (x + turn(z), y, z))
    before = send(plane, lambda x, y, z: (x - turn(z), y, z))
    near = call(near_kernel, (BX * BY, 128), [], [scalar, plane], 1 << 29)
    near, after, before = lax.optimization_barrier((near, after, before))
    new_modulus = call(
        final_kernel, (BX, BY, BZ), [(BX * BY, 128)], [scalar, modulus, near, after, before], 1 << 24
    )
    return displacement, new_modulus


def solution(mesh):
    placed = (
        P(None, "gx", "gy", "gz"),
        P(None, "gx", "gy", "gz"),
        P("gx", "gy", "gz"),
        P(("gx", "gy", "gz"), None),
    )
    return jax.shard_map(
        body,
        mesh=mesh,
        in_specs=placed,
        out_specs=(P(None, "gx", "gy", "gz"), P("gx", "gy", "gz")),
        check_vma=False,
    )
```

```python
import functools
import math

import jax
import jax.numpy as jnp
from jax import lax
from jax.experimental import pallas as pl
from jax.experimental.pallas import tpu as pltpu
from jax.sharding import PartitionSpec as P

PC = 10
SPAN = 2 * PC
FSWEEPS = 4
MASS_TERM = 0.5
DAMPING = 0.1
EPSILON = 1e-06
BX, BY, BZ = 16, 16, 128
HALO = 6
DEEP = 10
WIN = 30
WY = 32
AX = 24
ROWS = 104
TILES = ROWS // 8
PLANES = 3 * DEEP + 3 * (DEEP - 1) + DEEP
AXES = ("gx", "gy", "gz")
F32 = jnp.float32
BF16 = jnp.bfloat16
HIGH = lax.Precision.HIGHEST
VMEM_LIMIT = 48 * 1024 * 1024
LARGE_LIMIT = 61 * 1024 * 1024


def iota(shape, dim):
    return lax.broadcasted_iota(jnp.int32, shape, dim)


def lane_roll(values, shift):
    if isinstance(shift, int):
        shift = shift % values.shape[-1]
        return values if shift == 0 else pltpu.roll(values, shift, values.ndim - 1)
    size = values.shape[-1]
    return pltpu.roll(values, lax.rem(shift + 8 * size, size), values.ndim - 1)


def row_roll(values, shift):
    if isinstance(shift, int):
        shift = shift % values.shape[-2]
        return values if shift == 0 else pltpu.roll(values, shift, values.ndim - 2)
    size = values.shape[-2]
    return pltpu.roll(values, lax.rem(shift + 8 * size, size), values.ndim - 2)


def loop(low, high, step, unroll):
    whole = (high - low) // unroll
    if whole == 1:
        for i in range(low, low + unroll):
            step(i)
    elif whole > 1:

        def chunk(t, carry):
            for n in range(unroll):
                step(low + t * unroll + n)
            return carry

        lax.fori_loop(0, whole, chunk, 0)
    for i in range(low + whole * unroll, high):
        step(i)


def three_parts(values):
    first = values.astype(BF16)
    rest = values - first.astype(F32)
    second = rest.astype(BF16)
    third = (rest - second.astype(F32)).astype(BF16)
    return first, second, third


def dot(a, b):
    return lax.dot_general(a, b, (((1,), (0,)), ((), ())), precision=HIGH, preferred_element_type=F32)


def dot_exact(values, selector):
    parts = [
        lax.dot_general(part, selector, (((1,), (0,)), ((), ())), preferred_element_type=F32)
        for part in three_parts(values)
    ]
    return parts[0] + parts[1] + parts[2]


def div10(value):
    return lax.shift_right_arithmetic(value * 205, 11)


def edge_kernel(sc, u, f, m, msg1, msg2, strip, strip1, strip2, vu, vf, vm, sems):
    gz = sc[0]
    low_first = gz == 0
    s1 = jnp.where(low_first, BX - DEEP, 0)
    s2 = BX - DEEP - s1
    f1 = jnp.where(low_first, BX - DEEP + 1, 0)
    f2 = BX - DEEP + 1 - f1
    loads = [pltpu.make_async_copy(u, vu, sems.at[0]), pltpu.make_async_copy(f, vf, sems.at[1])]
    loads.append(pltpu.make_async_copy(m, vm, sems.at[2]))
    for load in loads:
        load.start()
    for load in loads:
        load.wait()
    lane = iota((BY, 128), 1)
    extra = jnp.where(low_first, DEEP, 0)

    def one(x):
        total = jnp.zeros((BY, 128), F32)
        for c in range(7):
            source = vu[c, x] if c < 3 else (vf[c - 3, x] if c < 6 else vm[x])
            moved = lane_roll(source, extra + DEEP * c)
            total = jnp.where((lane >= DEEP * c) & (lane < DEEP * (c + 1)), moved, total)
        strip[x] = total

    loop(0, BX, one, 8)
    for out, s, fs in ((msg1, s1, f1), (msg2, s2, f2)):
        for k in range(3):
            out[k * DEEP : (k + 1) * DEEP] = vu[k, pl.ds(s, DEEP)]
            base = 3 * DEEP + k * (DEEP - 1)
            out[base : base + DEEP - 1] = vf[k, pl.ds(fs, DEEP - 1)]
        out[PLANES - DEEP : PLANES] = vm[pl.ds(s, DEEP)]
    strip1[...] = strip[pl.ds(s1, DEEP)]
    strip2[...] = strip[pl.ds(s2, DEEP)]


def pack_kernel(sc, u, f, m, x1, x2, strip, strip1, strip2, own_u, own_f, msg1, msg2, eu, ef, em, es):
    gz = sc[0]
    low_first = gz == 0
    p1 = jnp.where(low_first, 0, BX + DEEP)
    p2 = BX + DEEP - p1
    q1 = jnp.where(low_first, 1, BX + DEEP)
    q2 = BX + DEEP + 1 - q1
    for k in range(3):
        eu[k, DEEP : DEEP + BX] = u[k]
        ef[k, DEEP : DEEP + BX] = f[k]
        ef[k, 0] = jnp.zeros((BY, 128), F32)
        ef[k, 2 * DEEP + BX - 1] = jnp.zeros((BY, 128), F32)
        for msg, p, q in ((x1, p1, q1), (x2, p2, q2)):
            eu[k, pl.ds(p, DEEP)] = msg[k * DEEP : (k + 1) * DEEP]
            base = 3 * DEEP + k * (DEEP - 1)
            ef[k, pl.ds(q, DEEP - 1)] = msg[base : base + DEEP - 1]
    em[DEEP : DEEP + BX] = m[...]
    es[DEEP : DEEP + BX] = strip[...]
    em[pl.ds(p1, DEEP)] = x1[PLANES - DEEP : PLANES]
    em[pl.ds(p2, DEEP)] = x2[PLANES - DEEP : PLANES]
    es[pl.ds(p2, DEEP)] = strip1[...]
    es[pl.ds(p1, DEEP)] = strip2[...]

    lane = iota((BY, 128), 1)
    group = lax.shift_right_arithmetic(lane, 5)
    inner = lane & 31
    zoff = jnp.where(low_first, BZ, -DEEP)

    def window(relz):
        w0 = relz - (DEEP - 5)
        z = inner + w0
        main_ok = (z >= 0) & (z < BZ)
        strip_ok = (z >= zoff) & (z < zoff + DEEP)

        def take(x):
            side = es[x]
            values = []
            for sources in ((eu, 0), (ef, 3)):
                ref, first = sources
                main = jnp.zeros((BY, 128), F32)
                far = jnp.zeros((BY, 128), F32)
                for k in range(4 if first == 0 else 3):
                    source, c = (ref[k, x], first + k) if k < 3 else (em[x], 6)
                    main = jnp.where(group == k, lane_roll(source, 32 * k - w0), main)
                    far = jnp.where(group == k, lane_roll(side, 32 * k + zoff - w0 - DEEP * c), far)
                values.append(jnp.where(main_ok, main, jnp.where(strip_ok, far, 0.0)))
            return values

        return take

    take_own = window(sc[3])
    x0 = sc[1] + 5

    def own(i):
        field, force = take_own(x0 + i)
        own_u[i] = field
        own_f[i] = force

    loop(0, WIN, own, 6)

    sub = iota((8, 128), 0)
    for msg, base, upward in ((msg1, 4, low_first), (msg2, 7, gz != 0)):
        take = window(sc[base + 2])
        start = sc[base] + 5

        def pair(i, msg=msg, take=take, start=start, upward=upward):
            mixed = jnp.zeros((8, 128), F32)
            number = 0
            for step in range(2):
                for values in take(start + 2 * i + step):
                    top, bottom = values[0:8], values[8:16]
                    msg[i, 8 * number : 8 * number + 8] = jnp.where(upward, bottom, top)
                    edge = jnp.where(upward, row_roll(top, 2), bottom)
                    mixed = jnp.where((sub >= 2 * number) & (sub < 2 * number + 2), row_roll(edge, 2 * number), mixed)
                    number += 1
            msg[i, 32:40] = mixed

        loop(0, WIN // 2, pair, 3)


def side_kernel(sc, u, f, m, x1, x2, strip, strip1, strip2, side1, side2):
    low_first = sc[0] == 0
    sub = iota((8, 128), 0)

    def put(dest, values16):
        for side, upward in ((side1, low_first), (side2, sc[0] != 0)):
            every = [jnp.where(upward, row_roll(v[8:16], 4), v[0:8]) for v in values16]
            for j in range(4):
                side[dest, 8 * j : 8 * j + 8] = jnp.where(sub < 4, every[2 * j], row_roll(every[2 * j + 1], 4))

    def inner_plane(i):
        put(i + FSWEEPS, [u[k, i] for k in range(3)] + [f[k, i] for k in range(3)] + [m[i], strip[i]])

    loop(0, BX, inner_plane, 8)

    def outer_plane(i):
        for a, b, sa, sb, start, dest in (
            (x1, x2, strip2, strip1, DEEP - FSWEEPS, i), (x2, x1, strip1, strip2, 0, i + FSWEEPS + BX),
        ):
            j = i + start
            force = j - (1 if start else 0)

            def pick(index):
                return jnp.where(low_first, a[index], b[index])

            put(
                dest,
                [pick(k * DEEP + j) for k in range(3)]
                + [pick(3 * DEEP + k * (DEEP - 1) + force) for k in range(3)]
                + [pick(PLANES - DEEP + j), jnp.where(low_first, sa[j], sb[j])],
            )

    loop(0, FSWEEPS, outer_plane, 4)


def invert(chains):
    sub = iota((8, 128), 0)
    lane = iota((8, 128), 1)

    def row_of(values, j):
        return jnp.broadcast_to(values[j : j + 1, :], (8, 128))

    def column_of(values, j):
        return jnp.broadcast_to(values[:, j : j + 1], (8, 128))

    empty = jnp.zeros((8, 128), F32)

    def eliminate(b, tile):
        own = [column_of(tile, 8 * b + j) for j in range(8)]
        for j in range(0, 8, 2):
            here0, here1 = sub == j, sub == j + 1
            at0, at1 = lane == 8 * b + j, lane == 8 * b + j + 1
            p00, p01 = row_of(own[j], j), row_of(own[j + 1], j)
            p10, p11 = row_of(own[j], j + 1), row_of(own[j + 1], j + 1)
            scale = pl.reciprocal(p00 * p11 - p01 * p10, approx=True)
            side0 = jnp.where(here0, -1.0, jnp.where(here1, 0.0, own[j]))
            side1 = jnp.where(here0, 0.0, jnp.where(here1, -1.0, own[j + 1]))
            both = here0 | here1

            def step(values, line0, line1):
                first = p11 * line0 - p01 * line1
                second = p00 * line1 - p10 * line0
                return jnp.where(both, 0.0, values) - (side0 * first + side1 * second) * scale

            for n in range(j + 2, 8):
                own[n] = step(own[n], row_of(own[n], j), row_of(own[n], j + 1))
            line0 = jnp.where(at0, 1.0, jnp.where(at1, 0.0, row_of(tile, j)))
            line1 = jnp.where(at0, 0.0, jnp.where(at1, 1.0, row_of(tile, j + 1)))
            tile = step(jnp.where(at0 | at1, 0.0, tile), line0, line1)
        return tile

    def reduced(b, tile, pivot):
        terms = [column_of(tile, 8 * b + j) * row_of(pivot, j) for j in range(8)]
        while len(terms) > 1:
            terms = [p + q for p, q in zip(terms[0::2], terms[1::2])]
        return jnp.where((lane >= 8 * b) & (lane < 8 * b + 8), 0.0, tile) - terms[0]

    for first in range(0, TILES, 2):
        blocks = [b for b in (first, first + 1) if b < TILES]
        in_blocks = (lane >= 8 * first) & (lane < 8 * first + 8 * len(blocks))
        before = [list(chain) for chain in chains]
        for b in blocks:
            for chain in chains:
                chain[b] = eliminate(b, chain[b])
                for i in range(first, min(first + 4, TILES)):
                    if i != b:
                        chain[i] = reduced(b, chain[i], chain[b])
        for chain, old in zip(chains, before):
            spread = jnp.concatenate([chain[r] if r in blocks else empty for r in range(16)], axis=0)
            change = dot(jnp.concatenate(old, axis=0), spread)
            for i in range(TILES):
                if not first <= i < first + 4:
                    chain[i] = jnp.where(in_blocks, 0.0, old[i]) - change[8 * i : 8 * i + 8]
    return chains


OFFSETS = (0, PC, -PC, 1, -1)
BANDS = (0, 1, 2, 9, 10, 11, 20)


def zone_kernel(
    sizes, sc, own_u, own_f, r1, r2, out,
    ua, ub, fo, m3, cx, cy, cz, iv, rows, band, up, down, far, grad, hess, bl, br, yt, zs, dl, gs,
):
    nx, ny, nz = sizes
    low_first = sc[0] == 0
    rely = sc[2]
    lane32 = iota((WY, 128), 1)
    group = lax.shift_right_arithmetic(lane32, 5)
    inner = lane32 & 31
    row32 = iota((WY, 128), 0)
    shift = -(rely + 11)

    inside_y = sc[11] - 5 + row32
    inside_z = sc[12] - 5 + inner
    inside = (inside_y >= 0) & (inside_y < ny) & (inside_z >= 0) & (inside_z < nz)

    def unpack(i):
        for step in range(2):
            gx = sc[10] - 5 + 2 * i + step
            good = inside & (gx >= 0) & (gx < nx)
            for which in range(2):
                number = 2 * step + which
                first = r1[i, 8 * number : 8 * number + 8]
                second = r2[i, 8 * number : 8 * number + 8]
                mix1 = r1[i, 32:40]
                mix2 = r2[i, 32:40]
                low, high = jnp.where(low_first, first, second), jnp.where(low_first, second, first)
                low_mix, high_mix = jnp.where(low_first, mix1, mix2), jnp.where(low_first, mix2, mix1)
                middle = own_u[2 * i + step] if which == 0 else own_f[2 * i + step]
                tall = jnp.concatenate(
                    [row_roll(low_mix, 6 - 2 * number), low, middle, high, row_roll(high_mix, -2 * number)], axis=0
                )
                tall = row_roll(tall, shift)[0:WY]
                if which == 0:
                    tall = jnp.where(good, tall, 0.0)
                    ua[2 * i + step] = tall
                    moved = jnp.where(group == 0, lane_roll(tall, 32), 0.0)
                    moved = jnp.where(group == 1, lane_roll(tall, 64), moved)
                    m3[2 * i + step] = jnp.where(group == 2, lane_roll(tall, 96), moved)
                else:
                    fo[2 * i + step] = tall

    loop(0, WIN // 2, unpack, 3)

    def faces(i):
        here = m3[i]
        cx[i] = 0.5 * (here + m3[jnp.minimum(i + 1, WIN - 1)])
        cy[i] = 0.5 * (here + row_roll(here, -1))
        cz[i] = 0.5 * (here + lane_roll(here, -1))

    loop(0, WIN, faces, 15)

    def scale(i):
        total = MASS_TERM + cx[i] + cx[i - 1] + cy[i] + row_roll(cy[i], 1) + cz[i] + lane_roll(cz[i], 1)
        gx = sc[10] - 5 + i
        good = inside & (gx >= 0) & (gx < nx)
        iv[i] = jnp.where(good, 1.0 / total, 0.0)

    loop(1, WIN - 1, scale, 14)

    for sweep in range(FSWEEPS):
        src, dst = (ua, ub) if sweep % 2 == 0 else (ub, ua)

        def relax(i, src=src, dst=dst):
            here = src[i]
            total = fo[i] + cx[i] * src[i + 1] + cx[i - 1] * src[i - 1]
            total = total + cy[i] * row_roll(here, -1) + row_roll(cy[i] * here, 1)
            total = total + cz[i] * lane_roll(here, -1) + lane_roll(cz[i] * here, 1)
            dst[i] = total * iv[i]

        loop(sweep + 1, WIN - 1 - sweep, relax, WIN - 2 - 2 * sweep)

    line = iota((128, 384), 0)
    column = iota((128, 384), 1)
    part = lax.shift_right_arithmetic(column, 7)
    spot = column & 127
    spot_y = div10(spot)
    spot_z = spot - PC * spot_y
    inner_z = (line & 31) - 5
    hit = (lax.shift_right_arithmetic(line, 5) == part) & (inner_z >= 0) & (inner_z < SPAN) & (spot < PC * PC)
    hit = hit & (lax.shift_right_arithmetic(inner_z, 1) == spot_z)
    selector = jnp.where(hit, 1.0, 0.0).astype(BF16)
    zone_y = row32 - 5
    lane_y = div10(lane32)
    pick_y = (zone_y >= 0) & (zone_y < SPAN) & (lax.shift_right_arithmetic(zone_y, 1) == lane_y) & (lane32 < PC * PC)
    pick_y = jnp.where(pick_y, 1.0, 0.0)
    even_y = (zone_y & 1) == 0
    even_z = ((inner - 5) & 1) == 0
    rows[...] = jnp.zeros(rows.shape, F32)

    def layer(a):
        sums = None
        for odd in range(2):
            i = 5 + 2 * a + odd
            here, m_here = ua[i], m3[i]
            ch_x, ch_b = here - ua[i + 1], ua[i - 1] - here
            ch_y = here - row_roll(here, -1)
            ch_z = here - lane_roll(here, -1)
            flow_y, flow_z = cy[i] * ch_y, cz[i] * ch_z
            applied = MASS_TERM * here + cx[i] * ch_x - cx[i - 1] * ch_b
            applied = applied + flow_y - row_roll(flow_y, 1) + flow_z - lane_roll(flow_z, 1)
            resid = fo[i] - applied
            back_y, back_z = row_roll(ch_y, 1), lane_roll(ch_z, 1)
            laplace = ch_x - ch_b + ch_y - back_y + ch_z - back_z
            xp = -0.5 * m3[i + 1] * ch_x
            xm = 0.5 * m3[i - 1] * ch_b
            yp = -0.5 * row_roll(m_here, -1) * ch_y
            ym = 0.5 * row_roll(m_here, 1) * back_y
            zp = -0.5 * lane_roll(m_here, -1) * ch_z
            zm = 0.5 * lane_roll(m_here, 1) * back_z
            diag = -0.5 * m_here * laplace + jnp.where(even_y, yp, ym) + jnp.where(even_z, zp, zm)
            diag = diag + (xm if odd else xp)
            now = [
                diag, xp if odd else None, None if odd else xm,
                jnp.where(even_y, 0.0, yp), jnp.where(even_y, ym, 0.0),
                jnp.where(even_z, 0.0, zp), jnp.where(even_z, zm, 0.0), resid,
            ]
            if sums is None:
                sums = now
            else:
                sums = [p if q is None else (q if p is None else p + q) for p, q in zip(sums, now)]
        tall = dot_exact(jnp.concatenate(sums, axis=0), selector)
        for n in range(8):
            for k in range(3):
                piece = tall[n * WY : (n + 1) * WY, 128 * k : 128 * k + 128] * pick_y
                rows[n, k, pl.ds(a, 1), :] = jnp.sum(piece, axis=0, keepdims=True)

    loop(0, PC, layer, 5)

    lane16 = iota((16, 128), 1)
    row16 = iota((16, 128), 0)
    at_y = div10(lane16)
    at_z = lane16 - PC * at_y

    def masked(n, keep):
        return [jnp.where(keep, rows[n, k], 0.0) for k in range(3)]

    full = row16 < PC
    v = {
        0: masked(0, full),
        PC: masked(3, full & (at_y < PC - 1)),
        -PC: masked(4, full & (at_y > 0)),
        1: masked(5, full & (at_z < PC - 1)),
        -1: masked(6, full & (at_z > 0)),
    }
    vxp = masked(1, row16 < PC - 1)
    vxm = masked(2, full & (row16 > 0))
    res = masked(7, full)

    def mix(p, q):
        return p[0] * q[0] + p[1] * q[1] + p[2] * q[2]

    bands = {}
    for o1 in OFFSETS:
        for o2 in OFFSETS:
            key = o1 - o2
            if key >= 0:
                term = lane_roll(mix(v[o1], v[o2]), o2)
                bands[key] = bands[key] + term if key in bands else term
    bands[0] = bands[0] + row_roll(mix(vxp, vxp), 1) + row_roll(mix(vxm, vxm), -1)
    trace = jnp.sum(jnp.sum(bands[0], axis=1, keepdims=True), axis=0, keepdims=True)
    ridge = DAMPING * trace / PC**3 + EPSILON
    bands[0] = jnp.where(lane16 < PC * PC, bands[0] + ridge, jnp.where(lane16 < ROWS, 1.0, 0.0))
    slots = {}
    for n, key in enumerate(BANDS):
        band[n] = bands[key]
        slots[key] = n
    for n, key in enumerate(BANDS[1:]):
        band[len(BANDS) + n] = lane_roll(bands[key], key)
        slots[-key] = len(BANDS) + n
    for n, key in enumerate(OFFSETS):
        above = row_roll(mix(vxm, v[-key]), -1)
        below = row_roll(mix(vxp, v[-key]), 1)
        up[n] = mix(vxp, v[key]) + lane_roll(above, -key)
        down[n] = mix(vxm, v[key]) + lane_roll(below, -key)
    cross = mix(vxm, vxp)
    far[0] = row_roll(cross, -1)
    far[1] = row_roll(cross, 1)
    gradient = row_roll(mix(vxp, res), 1) + row_roll(mix(vxm, res), -1)
    for key in OFFSETS:
        gradient = gradient + lane_roll(mix(v[key], res), key)
    grad[...] = gradient

    sub = iota((8, 128), 0)
    lane8 = iota((8, 128), 1)

    def spread(ref, n, x):
        return jnp.broadcast_to(ref[n, pl.ds(x, 1), :], (8, 128))

    def fill(dst, lines, lead):
        for r in range(TILES):
            apart = sub + 8 * r - lane8
            tile = jnp.zeros((8, 128), F32)
            for key, values in lines:
                if 8 * r + 7 - key >= 0 and 8 * r - key < 128:
                    tile = jnp.where(apart == key, values, tile)
            dst[lead + (slice(8 * r, 8 * r + 8), slice(None))] = tile
        dst[lead + (slice(ROWS, 128), slice(None))] = jnp.zeros((128 - ROWS, 128), F32)

    def dense(x, carry):
        fill(hess, [(key, spread(band, n, x)) for key, n in slots.items()], (x,))
        gs[x] = jnp.broadcast_to(grad[pl.ds(x, 1), :], (8, 128))
        return carry

    lax.fori_loop(0, PC, dense, 0)

    def couple(t, carry):
        right = PC - 1 - t
        fill(bl, [(key, spread(up, n, t)) for n, key in enumerate(OFFSETS)], (t, 0))
        fill(bl, [(key, spread(down, n, t + 1)) for n, key in enumerate(OFFSETS)], (t, 1))

        @pl.when(t < 4)
        def _():
            fill(br, [(key, spread(down, n, right)) for n, key in enumerate(OFFSETS)], (t, 0))
            fill(br, [(key, spread(up, n, right - 1)) for n, key in enumerate(OFFSETS)], (t, 1))

        return carry

    lax.fori_loop(0, 5, couple, 0)
    br[4] = jnp.zeros((2, 128, 128), F32)

    on_diagonal = iota((128, 128), 0) == iota((128, 128), 1)
    ones = jnp.ones((128, 128), BF16)

    def tiles_of(x):
        return [hess[x, 8 * r : 8 * r + 8, :] for r in range(TILES)]

    def whole(chain):
        return jnp.concatenate(chain + [jnp.zeros((128 - ROWS, 128), F32)], axis=0)

    def eliminate(t, carry):
        right = PC - 1 - t
        left_tiles, right_tiles = invert([tiles_of(t), tiles_of(right)])
        for s, tiles, x, step, ref in ((0, left_tiles, t, 1, bl), (1, right_tiles, right, -1, br)):
            q = whole(tiles)
            row = jnp.broadcast_to(far[s, pl.ds(x, 1), :], (128, 128))
            column = dot_exact(jnp.where(on_diagonal, row, 0.0), ones)
            w, wt = ref[t, 0], ref[t, 1]
            y1, y2 = dot(q, w), q * row
            yt[s, t, 0:128] = dot(wt, q)
            yt[s, t, 128:256] = column * q
            s1 = dot(wt, jnp.concatenate([y1, y2], axis=1))
            g = gs[x]
            z = dot(g, q)
            zs[s, t] = z
            one, two_on = x + step, x + 2 * step
            hess[one] = hess[one] - s1[:, 0:128]
            hess[two_on] = hess[two_on] - column * y2
            ref[t + 1, 0] = ref[t + 1, 0] - s1[:, 128:256]
            ref[t + 1, 1] = ref[t + 1, 1] - column * y1
            gs[one] = gs[one] - dot(z, w)
            gs[two_on] = gs[two_on] - z * row[0:8]
        return carry

    lax.fori_loop(0, 4, eliminate, 0)

    def middle(t, carry):
        x = 4 + t
        (tiles,) = invert([tiles_of(x)])
        q = whole(tiles)
        g = gs[x]
        dl[x] = dot(g, q)

        @pl.when(t == 0)
        def _():
            w = bl[4, 0] + br[4, 1]
            wt = bl[4, 1] + br[4, 0]
            y = dot(q, w)
            yt[0, 4, 0:128] = dot(wt, q)
            hess[5] = hess[5] - dot(wt, y)
            gs[5] = gs[5] - dot(g, y)

        return carry

    lax.fori_loop(0, 2, middle, 0)
    dl[4] = dl[4] - dot(dl[5], yt[0, 4, 0:128])
    for t in (3, 2, 1, 0):
        right = PC - 1 - t
        dl[t] = zs[0, t] - dot(jnp.concatenate([dl[t + 1], dl[t + 2]], axis=1), yt[0, t])
        dl[right] = zs[1, t] - dot(jnp.concatenate([dl[right - 1], dl[right - 2]], axis=1), yt[1, t])
    for x in range(PC):
        out[x : x + 1, :] = -dl[x, 0:1, :]
    spare = iota((16 - PC, 128), 1)
    corner = jnp.zeros((16 - PC, 128), F32)
    for n in range(3):
        corner = jnp.where(spare == n, sc[10 + n].astype(F32), corner)
    out[PC:16, :] = corner


def field_kernel(
    sizes, sc, u, f, m, x1, x2, strip, strip1, strip2, s1, s2, out,
    ua, ub, fo, mo, cx, cy, zu, zd, ze, iv, ba, bb, bf, bm, bx, by, bz, bi,
):
    nx, ny, nz = sizes
    low_first = sc[0] == 0
    sub = iota((8, 128), 0)
    lane = iota((AX, 128), 1)
    group = lax.shift_right_arithmetic(lane, 5)
    inner = lane & 31
    lead = DEEP - FSWEEPS
    w0 = jnp.where(low_first, BZ - 8, -8)
    zoff = jnp.where(low_first, BZ, -DEEP)
    z = inner + w0
    main_ok = (z >= 0) & (z < BZ)
    far_ok = (z >= zoff) & (z < zoff + DEEP)
    edge_lane = jnp.where(low_first, BZ - 1, 0)
    edge_from = jnp.where(low_first, 8, 7)
    at_edge = lane == edge_lane
    row24 = iota((AX, 128), 0)
    gy = sc[14] - FSWEEPS + row24
    inside = (gy >= 0) & (gy < ny)

    def build(dest, values16):
        gx = sc[13] - FSWEEPS + dest
        good = inside & (gx >= 0) & (gx < nx)
        every = []
        for q in range(8):
            j = q // 2
            a = s1[dest, 8 * j : 8 * j + 8]
            b = s2[dest, 8 * j : 8 * j + 8]
            low, high = jnp.where(low_first, a, b), jnp.where(low_first, b, a)
            if q % 2 == 0:
                high = row_roll(high, 4)
            else:
                low = row_roll(low, 4)
            t0, t1 = row_roll(values16[q][0:8], 4), row_roll(values16[q][8:16], 4)
            tall = jnp.concatenate(
                [jnp.where(sub < 4, low, t0), jnp.where(sub < 4, t0, t1), jnp.where(sub < 4, t1, high)], axis=0
            )
            every.append(jnp.where(good, tall, 0.0))
        for k in range(3):
            ua[k, dest] = every[k]
            fo[k, dest] = every[3 + k]
        mo[dest] = every[6]
        side = []
        for channels in ((0, 1, 2), (3, 4, 5)):
            main, far = jnp.zeros((AX, 128), F32), jnp.zeros((AX, 128), F32)
            for k, c in enumerate(channels):
                main = jnp.where(group == k, lane_roll(every[c], 32 * k - w0), main)
                far = jnp.where(group == k, lane_roll(every[7], 32 * k + zoff - w0 - DEEP * c), far)
            side.append(jnp.where(main_ok, main, jnp.where(far_ok, far, 0.0)))
        ba[dest], bf[dest] = side
        main = jnp.where(main_ok, lane_roll(every[6], -w0), jnp.where(far_ok, lane_roll(every[7], zoff - w0 - DEEP * 6), 0.0))
        first = jnp.where(group == 0, main, 0.0)
        first = jnp.where(group == 1, lane_roll(main, 32), first)
        bm[dest] = jnp.where(group == 2, lane_roll(main, 64), first)

    def inner_plane(i):
        build(i + FSWEEPS, [u[k, i] for k in range(3)] + [f[k, i] for k in range(3)] + [m[i], strip[i]])

    loop(0, BX, inner_plane, 4)

    def outer_plane(i):
        for a, b, sa, sb, start, dest in (
            (x1, x2, strip2, strip1, lead, i), (x2, x1, strip1, strip2, 0, i + FSWEEPS + BX),
        ):
            j = i + start
            force = j - (1 if start else 0)

            def pick(index):
                return jnp.where(low_first, a[index], b[index])

            build(
                dest,
                [pick(k * DEEP + j) for k in range(3)]
                + [pick(3 * DEEP + k * (DEEP - 1) + force) for k in range(3)]
                + [pick(PLANES - DEEP + j), jnp.where(low_first, sa[j], sb[j])],
            )

    loop(0, FSWEEPS, outer_plane, 2)

    def edge(values, k):
        return jnp.where(at_edge, lane_roll(values, edge_lane - edge_from - 32 * k), 0.0)

    def faces(i):
        here, there = mo[i], bm[i]
        cx[i] = 0.5 * (here + mo[jnp.minimum(i + 1, AX - 1)])
        bx[i] = 0.5 * (there + bm[jnp.minimum(i + 1, AX - 1)])
        cy[i] = 0.5 * (here + row_roll(here, -1))
        by[i] = 0.5 * (there + row_roll(there, -1))
        bz[i] = 0.5 * (there + lane_roll(there, -1))
        zu[i] = jnp.where(lane == BZ - 1, 0.0, 0.5 * (here + lane_roll(here, -1)))
        zd[i] = jnp.where(lane == 0, 0.0, 0.5 * (here + lane_roll(here, 1)))
        ze[i] = jnp.where(at_edge, 0.5 * (here + edge(there, 0)), 0.0)

    loop(0, AX, faces, 12)
    side_inside = (sc[15] + z >= 0) & (sc[15] + z < nz)
    far_edge = BZ - 1 - edge_lane

    def scale(i):
        open_face = jnp.where(lane == far_edge, 0.5 * mo[i], 0.0)
        total = MASS_TERM + cx[i] + cx[i - 1] + cy[i] + row_roll(cy[i], 1) + zu[i] + zd[i] + ze[i] + open_face
        gx = sc[13] - FSWEEPS + i
        good = inside & (gx >= 0) & (gx < nx)
        iv[i] = jnp.where(good, 1.0 / total, 0.0)
        total = MASS_TERM + bx[i] + bx[i - 1] + by[i] + row_roll(by[i], 1) + bz[i] + lane_roll(bz[i], 1)
        bi[i] = jnp.where(good & side_inside, 1.0 / total, 0.0)

    loop(1, AX - 1, scale, 11)
    for sweep in range(FSWEEPS):
        src, dst = (ua, ub) if sweep % 2 == 0 else (ub, ua)
        bsrc, bdst = (ba, bb) if sweep % 2 == 0 else (bb, ba)

        def relax(i, src=src, dst=dst, bsrc=bsrc, bdst=bdst, last=sweep == FSWEEPS - 1):
            there = bsrc[i]
            for k in range(3):
                here = src[k, i]
                total = fo[k, i] + cx[i] * src[k, i + 1] + cx[i - 1] * src[k, i - 1]
                total = total + cy[i] * row_roll(here, -1) + row_roll(cy[i] * here, 1)
                total = total + zu[i] * lane_roll(here, -1) + zd[i] * lane_roll(here, 1) + ze[i] * edge(there, k)
                total = total * iv[i]
                if last:
                    out[k, i - FSWEEPS] = row_roll(total, -FSWEEPS)[0:BY]
                else:
                    dst[k, i] = total
            if not last:
                total = bf[i] + bx[i] * bsrc[i + 1] + bx[i - 1] * bsrc[i - 1]
                total = total + by[i] * row_roll(there, -1) + row_roll(by[i] * there, 1)
                total = total + bz[i] * lane_roll(there, -1) + lane_roll(bz[i] * there, 1)
                bdst[i] = total * bi[i]

        loop(sweep + 1, AX - 1 - sweep, relax, AX - 2 - 2 * sweep)


def taper(offset):
    folded = jnp.minimum(offset, SPAN - 1 - offset)
    total = jnp.zeros(offset.shape, F32)
    for n in range(PC):
        total = jnp.where(folded == float(n), math.sin(math.pi * (n + 0.5) / SPAN), total)
    return total


def contribution(sc, delta, start, planes):
    rows = 16 if planes > 8 else 8
    laneix = iota((rows, 128), 1)
    lane16i = iota((16, 128), 1)
    lane_y = div10(lane16i).astype(F32)
    rows128 = iota((128, 128), 0)
    rows_z = (rows128 - PC * div10(rows128)).astype(F32)

    def place(axis):
        return delta[PC : PC + 1, axis : axis + 1] - sc[13 + axis].astype(F32)

    off_x = (iota((rows, 128), 0) + start).astype(F32) - place(0)
    apart = off_x - 2.0 * laneix.astype(F32)
    choose = jnp.where((apart >= 0.0) & (apart < 2.0) & (laneix < PC), 1.0, 0.0).astype(BF16)[:, 0:16]
    picked = [lax.dot_general(choose, p, (((1,), (0,)), ((), ())), preferred_element_type=F32) for p in three_parts(delta)]
    lines = (picked[0] + picked[1] + picked[2]) * taper(off_x)
    off_y = iota((16, 128), 0).astype(F32) - place(1)
    apart = off_y - 2.0 * lane_y
    cover = jnp.where((apart >= 0.0) & (apart < 2.0) & (lane16i < PC * PC), taper(off_y), 0.0)
    off_z = iota((128, 128), 1).astype(F32) - place(2)
    apart = off_z - 2.0 * rows_z
    expand = jnp.where((apart >= 0.0) & (apart < 2.0) & (rows128 < PC * PC), 1.0, 0.0).astype(BF16)
    tall = jnp.concatenate([jnp.broadcast_to(lines[x : x + 1, :], (BY, 128)) * cover for x in range(planes)], axis=0)
    return dot_exact(tall, expand) * taper(off_z[0:1, :])


def near_kernel(sc, parts, acc):
    acc[...] = jnp.zeros(acc.shape, F32)

    def add(n):
        acc[...] += contribution(sc, parts[n], 0, BX)

    loop(0, parts.shape[0], add, 3)


def final_kernel(sc, m, near, parts1, parts2, out, acc):
    acc[...] = near[...]
    reach = HALO - 1
    start1 = jnp.where(sc[0] == 0, 0, BX - reach)
    start2 = BX - reach - start1

    def add(n):
        for parts, start in ((parts1, start1), (parts2, start2)):
            where = pl.ds(pl.multiple_of(start * BY, BY), reach * BY)
            acc[where, :] += contribution(sc, parts[n], start, reach)

    loop(0, parts1.shape[0], add, 3)
    for x in range(BX):
        out[x] = m[x] * (1.0 + acc[16 * x : 16 * x + 16, :])


def call(kernel, shapes, scratch, inputs, flops, space=pltpu.VMEM, limit=VMEM_LIMIT):
    specs = [pl.BlockSpec(memory_space=pltpu.SMEM)] + [pl.BlockSpec(memory_space=space)] * (len(inputs) - 1)
    single = not isinstance(shapes, list)
    outs = [jax.ShapeDtypeStruct(s, F32) for s in ([shapes] if single else shapes)]
    results = pl.pallas_call(
        kernel,
        out_shape=outs,
        in_specs=specs,
        out_specs=[pl.BlockSpec(memory_space=pltpu.VMEM)] * len(outs),
        scratch_shapes=[pltpu.VMEM(s, F32) if isinstance(s, tuple) else s for s in scratch],
        compiler_params=pltpu.CompilerParams(vmem_limit_bytes=limit),
        cost_estimate=pl.CostEstimate(flops=flops, bytes_accessed=1 << 20, transcendentals=0),
    )(*inputs)
    return results[0] if single else results


def body(forcing, start_field, modulus, corners):
    counts = tuple(lax.axis_size(axis) for axis in AXES)
    sizes = (counts[0] * BX, counts[1] * BY, counts[2] * BZ)
    place = tuple(lax.axis_index(axis) for axis in AXES)
    gz = place[2].astype(jnp.int32)
    lower = jnp.stack([place[0] * BX, place[1] * BY, place[2] * BZ]).astype(jnp.int32)

    def send(values, move):
        pairs = []
        for x in range(counts[0]):
            for y in range(counts[1]):
                for z in range(counts[2]):
                    to = [t % c for t, c in zip(move(x, y, z), counts)]
                    pairs.append(((x * counts[1] + y) * counts[2] + z, (to[0] * counts[1] + to[1]) * counts[2] + to[2]))
        return lax.ppermute(values, AXES, pairs)

    def turn(z):
        return 1 if z == 0 else -1

    relative = corners[0] - lower
    near = jnp.broadcast_to(relative[None, :], (1, 3))
    want1 = send(near, lambda x, y, z: (x, y - turn(z), z))
    want2 = send(near, lambda x, y, z: (x, y + turn(z), z))
    scalar = jnp.concatenate([gz[None], relative, want1[0], want2[0], corners[0], lower]).astype(jnp.int32)
    first = gz[None]

    msg1, msg2, strip, strip1, strip2 = call(
        edge_kernel,
        [(PLANES, BY, 128), (PLANES, BY, 128), (BX, BY, 128), (DEEP, BY, 128), (DEEP, BY, 128)],
        [(3, BX, BY, BZ), (3, BX, BY, BZ), (BX, BY, BZ), pltpu.SemaphoreType.DMA((3,))],
        [first, start_field, forcing, modulus],
        1 << 20,
        pltpu.HBM,
        LARGE_LIMIT,
    )
    x1 = send(msg1, lambda x, y, z: (x + turn(z), y, z))
    x2 = send(msg2, lambda x, y, z: (x - turn(z), y, z))
    far_strip = send(strip, lambda x, y, z: (x, y, 1 - z))
    far1 = send(strip1, lambda x, y, z: (x + turn(z), y, 1 - z))
    far2 = send(strip2, lambda x, y, z: (x - turn(z), y, 1 - z))
    spread = [scalar, start_field, forcing, modulus, x1, x2, far_strip, far1, far2]
    a1, a2 = call(side_kernel, [(AX, 32, 128)] * 2, [], spread, 1 << 20)
    b1 = send(a1, lambda x, y, z: (x, y + turn(z), z))
    b2 = send(a2, lambda x, y, z: (x, y - turn(z), z))
    own_u, own_f, y1, y2 = call(
        pack_kernel,
        [(WIN, BY, 128)] * 2 + [(WIN // 2, 40, 128)] * 2,
        [(3, 36, BY, 128), (3, 36, BY, 128), (36, BY, 128), (36, BY, 128)],
        spread,
        1 << 31,
    )
    r1 = send(y1, lambda x, y, z: (x, y + turn(z), z))
    r2 = send(y2, lambda x, y, z: (x, y - turn(z), z))
    wide = (AX, AX, 128)
    displacement = call(
        functools.partial(field_kernel, sizes),
        (3, BX, BY, BZ),
        [(3,) + wide] * 3 + [wide] * 15,
        spread + [b1, b2],
        1 << 32,
    )
    own_u, own_f, r1, r2, displacement = lax.optimization_barrier((own_u, own_f, r1, r2, displacement))
    window = (WIN, WY, 128)
    delta = call(
        functools.partial(zone_kernel, sizes),
        (16, 128),
        [window] * 8
        + [
            (8, 3, 16, 128), (13, 16, 128), (5, 16, 128), (5, 16, 128), (2, 16, 128), (16, 128),
            (PC, 128, 128), (5, 2, 128, 128), (5, 2, 128, 128), (2, 5, 256, 128), (2, 5, 8, 128), (PC, 8, 128), (PC, 8, 128),
        ],
        [scalar, own_u, own_f, r1, r2],
        1 << 33,
    )
    plane = jnp.stack([delta, send(delta, lambda x, y, z: (x, y, 1 - z))])
    right = send(plane, lambda x, y, z: (x, y + turn(z), z))
    left = send(plane, lambda x, y, z: (x, y - turn(z), z))
    plane = jnp.concatenate([plane, right, left])
    after = send(plane, lambda x, y, z: (x + turn(z), y, z))
    before = send(plane, lambda x, y, z: (x - turn(z), y, z))
    near = call(near_kernel, (BX * BY, 128), [], [scalar, plane], 1 << 29)
    near, after, before = lax.optimization_barrier((near, after, before))
    new_modulus = call(
        final_kernel, (BX, BY, BZ), [(BX * BY, 128)], [scalar, modulus, near, after, before], 1 << 24
    )
    return displacement, new_modulus


def solution(mesh):
    placed = (
        P(None, "gx", "gy", "gz"),
        P(None, "gx", "gy", "gz"),
        P("gx", "gy", "gz"),
        P(("gx", "gy", "gz"), None),
    )
    return jax.shard_map(
        body,
        mesh=mesh,
        in_specs=placed,
        out_specs=(P(None, "gx", "gy", "gz"), P("gx", "gy", "gz")),
        check_vma=False,
    )
```

```python
import functools
import math

import jax
import jax.numpy as jnp
from jax import lax
from jax.experimental import pallas as pl
from jax.experimental.pallas import tpu as pltpu
from jax.sharding import PartitionSpec as P

PC = 10
SPAN = 2 * PC
FSWEEPS = 4
MASS_TERM = 0.5
DAMPING = 0.1
EPSILON = 1e-06
BX, BY, BZ = 16, 16, 128
HALO = 6
DEEP = 10
WIN = 30
WY = 32
AX = 24
ROWS = 104
TILES = ROWS // 8
PLANES = 3 * DEEP + 3 * (DEEP - 1) + DEEP
AXES = ("gx", "gy", "gz")
F32 = jnp.float32
BF16 = jnp.bfloat16
HIGH = lax.Precision.HIGHEST
VMEM_LIMIT = 48 * 1024 * 1024
LARGE_LIMIT = 61 * 1024 * 1024


def iota(shape, dim):
    return lax.broadcasted_iota(jnp.int32, shape, dim)


def lane_roll(values, shift):
    if isinstance(shift, int):
        shift = shift % values.shape[-1]
        return values if shift == 0 else pltpu.roll(values, shift, values.ndim - 1)
    size = values.shape[-1]
    return pltpu.roll(values, lax.rem(shift + 8 * size, size), values.ndim - 1)


def row_roll(values, shift):
    if isinstance(shift, int):
        shift = shift % values.shape[-2]
        return values if shift == 0 else pltpu.roll(values, shift, values.ndim - 2)
    size = values.shape[-2]
    return pltpu.roll(values, lax.rem(shift + 8 * size, size), values.ndim - 2)


def loop(low, high, step, unroll):
    whole = (high - low) // unroll
    if whole == 1:
        for i in range(low, low + unroll):
            step(i)
    elif whole > 1:

        def chunk(t, carry):
            for n in range(unroll):
                step(low + t * unroll + n)
            return carry

        lax.fori_loop(0, whole, chunk, 0)
    for i in range(low + whole * unroll, high):
        step(i)


def three_parts(values):
    first = values.astype(BF16)
    rest = values - first.astype(F32)
    second = rest.astype(BF16)
    third = (rest - second.astype(F32)).astype(BF16)
    return first, second, third


def dot(a, b):
    return lax.dot_general(a, b, (((1,), (0,)), ((), ())), precision=HIGH, preferred_element_type=F32)


def dot_exact(values, selector):
    parts = [
        lax.dot_general(part, selector, (((1,), (0,)), ((), ())), preferred_element_type=F32)
        for part in three_parts(values)
    ]
    return parts[0] + parts[1] + parts[2]


def div10(value):
    return lax.shift_right_arithmetic(value * 205, 11)


def edge_kernel(sc, u, f, m, msg1, msg2, strip, strip1, strip2, vu, vf, vm, sems):
    gz = sc[0]
    low_first = gz == 0
    s1 = jnp.where(low_first, BX - DEEP, 0)
    s2 = BX - DEEP - s1
    f1 = jnp.where(low_first, BX - DEEP + 1, 0)
    f2 = BX - DEEP + 1 - f1
    loads = [pltpu.make_async_copy(u, vu, sems.at[0]), pltpu.make_async_copy(f, vf, sems.at[1])]
    loads.append(pltpu.make_async_copy(m, vm, sems.at[2]))
    for load in loads:
        load.start()
    for load in loads:
        load.wait()
    lane = iota((BY, 128), 1)
    extra = jnp.where(low_first, DEEP, 0)

    def one(x):
        total = jnp.zeros((BY, 128), F32)
        for c in range(7):
            source = vu[c, x] if c < 3 else (vf[c - 3, x] if c < 6 else vm[x])
            moved = lane_roll(source, extra + DEEP * c)
            total = jnp.where((lane >= DEEP * c) & (lane < DEEP * (c + 1)), moved, total)
        strip[x] = total

    loop(0, BX, one, 8)
    for out, s, fs in ((msg1, s1, f1), (msg2, s2, f2)):
        for k in range(3):
            out[k * DEEP : (k + 1) * DEEP] = vu[k, pl.ds(s, DEEP)]
            base = 3 * DEEP + k * (DEEP - 1)
            out[base : base + DEEP - 1] = vf[k, pl.ds(fs, DEEP - 1)]
        out[PLANES - DEEP : PLANES] = vm[pl.ds(s, DEEP)]
    strip1[...] = strip[pl.ds(s1, DEEP)]
    strip2[...] = strip[pl.ds(s2, DEEP)]


def pack_kernel(sc, u, f, m, x1, x2, strip, strip1, strip2, own_u, own_f, msg1, msg2, eu, ef, em, es):
    gz = sc[0]
    low_first = gz == 0
    p1 = jnp.where(low_first, 0, BX + DEEP)
    p2 = BX + DEEP - p1
    q1 = jnp.where(low_first, 1, BX + DEEP)
    q2 = BX + DEEP + 1 - q1
    for k in range(3):
        eu[k, DEEP : DEEP + BX] = u[k]
        ef[k, DEEP : DEEP + BX] = f[k]
        ef[k, 0] = jnp.zeros((BY, 128), F32)
        ef[k, 2 * DEEP + BX - 1] = jnp.zeros((BY, 128), F32)
        for msg, p, q in ((x1, p1, q1), (x2, p2, q2)):
            eu[k, pl.ds(p, DEEP)] = msg[k * DEEP : (k + 1) * DEEP]
            base = 3 * DEEP + k * (DEEP - 1)
            ef[k, pl.ds(q, DEEP - 1)] = msg[base : base + DEEP - 1]
    em[DEEP : DEEP + BX] = m[...]
    es[DEEP : DEEP + BX] = strip[...]
    em[pl.ds(p1, DEEP)] = x1[PLANES - DEEP : PLANES]
    em[pl.ds(p2, DEEP)] = x2[PLANES - DEEP : PLANES]
    es[pl.ds(p2, DEEP)] = strip1[...]
    es[pl.ds(p1, DEEP)] = strip2[...]

    lane = iota((BY, 128), 1)
    group = lax.shift_right_arithmetic(lane, 5)
    inner = lane & 31
    zoff = jnp.where(low_first, BZ, -DEEP)

    def window(relz):
        w0 = relz - (DEEP - 5)
        z = inner + w0
        main_ok = (z >= 0) & (z < BZ)
        strip_ok = (z >= zoff) & (z < zoff + DEEP)

        def take(x):
            side = es[x]
            values = []
            for sources in ((eu, 0), (ef, 3)):
                ref, first = sources
                main = jnp.zeros((BY, 128), F32)
                far = jnp.zeros((BY, 128), F32)
                for k in range(4 if first == 0 else 3):
                    source, c = (ref[k, x], first + k) if k < 3 else (em[x], 6)
                    main = jnp.where(group == k, lane_roll(source, 32 * k - w0), main)
                    far = jnp.where(group == k, lane_roll(side, 32 * k + zoff - w0 - DEEP * c), far)
                values.append(jnp.where(main_ok, main, jnp.where(strip_ok, far, 0.0)))
            return values

        return take

    take_own = window(sc[3])
    x0 = sc[1] + 5

    def own(i):
        field, force = take_own(x0 + i)
        own_u[i] = field
        own_f[i] = force

    loop(0, WIN, own, 10)

    sub = iota((8, 128), 0)
    for msg, base, upward in ((msg1, 4, low_first), (msg2, 7, gz != 0)):
        take = window(sc[base + 2])
        start = sc[base] + 5

        def pair(i, msg=msg, take=take, start=start, upward=upward):
            mixed = jnp.zeros((8, 128), F32)
            number = 0
            for step in range(2):
                for values in take(start + 2 * i + step):
                    top, bottom = values[0:8], values[8:16]
                    msg[i, 8 * number : 8 * number + 8] = jnp.where(upward, bottom, top)
                    edge = jnp.where(upward, row_roll(top, 2), bottom)
                    mixed = jnp.where((sub >= 2 * number) & (sub < 2 * number + 2), row_roll(edge, 2 * number), mixed)
                    number += 1
            msg[i, 32:40] = mixed

        loop(0, WIN // 2, pair, 5)


def side_kernel(sc, u, f, m, x1, x2, strip, strip1, strip2, side1, side2):
    low_first = sc[0] == 0
    sub = iota((8, 128), 0)

    def put(dest, values16):
        for side, upward in ((side1, low_first), (side2, sc[0] != 0)):
            every = [jnp.where(upward, row_roll(v[8:16], 4), v[0:8]) for v in values16]
            for j in range(4):
                side[dest, 8 * j : 8 * j + 8] = jnp.where(sub < 4, every[2 * j], row_roll(every[2 * j + 1], 4))

    def inner_plane(i):
        put(i + FSWEEPS, [u[k, i] for k in range(3)] + [f[k, i] for k in range(3)] + [m[i], strip[i]])

    loop(0, BX, inner_plane, 8)

    def outer_plane(i):
        for a, b, sa, sb, start, dest in (
            (x1, x2, strip2, strip1, DEEP - FSWEEPS, i), (x2, x1, strip1, strip2, 0, i + FSWEEPS + BX),
        ):
            j = i + start
            force = j - (1 if start else 0)

            def pick(index):
                return jnp.where(low_first, a[index], b[index])

            put(
                dest,
                [pick(k * DEEP + j) for k in range(3)]
                + [pick(3 * DEEP + k * (DEEP - 1) + force) for k in range(3)]
                + [pick(PLANES - DEEP + j), jnp.where(low_first, sa[j], sb[j])],
            )

    loop(0, FSWEEPS, outer_plane, 4)


def invert(chains):
    sub = iota((8, 128), 0)
    lane = iota((8, 128), 1)

    def row_of(values, j):
        return jnp.broadcast_to(values[j : j + 1, :], (8, 128))

    def column_of(values, j):
        return jnp.broadcast_to(values[:, j : j + 1], (8, 128))

    empty = jnp.zeros((8, 128), F32)

    def eliminate(b, tile):
        own = [column_of(tile, 8 * b + j) for j in range(8)]
        for j in range(0, 8, 2):
            here0, here1 = sub == j, sub == j + 1
            at0, at1 = lane == 8 * b + j, lane == 8 * b + j + 1
            p00, p01 = row_of(own[j], j), row_of(own[j + 1], j)
            p10, p11 = row_of(own[j], j + 1), row_of(own[j + 1], j + 1)
            scale = pl.reciprocal(p00 * p11 - p01 * p10, approx=True)
            side0 = jnp.where(here0, -1.0, jnp.where(here1, 0.0, own[j]))
            side1 = jnp.where(here0, 0.0, jnp.where(here1, -1.0, own[j + 1]))
            both = here0 | here1

            def step(values, line0, line1):
                first = p11 * line0 - p01 * line1
                second = p00 * line1 - p10 * line0
                return jnp.where(both, 0.0, values) - (side0 * first + side1 * second) * scale

            for n in range(j + 2, 8):
                own[n] = step(own[n], row_of(own[n], j), row_of(own[n], j + 1))
            line0 = jnp.where(at0, 1.0, jnp.where(at1, 0.0, row_of(tile, j)))
            line1 = jnp.where(at0, 0.0, jnp.where(at1, 1.0, row_of(tile, j + 1)))
            tile = step(jnp.where(at0 | at1, 0.0, tile), line0, line1)
        return tile

    def reduced(b, tile, pivot):
        terms = [column_of(tile, 8 * b + j) * row_of(pivot, j) for j in range(8)]
        while len(terms) > 1:
            terms = [p + q for p, q in zip(terms[0::2], terms[1::2])]
        return jnp.where((lane >= 8 * b) & (lane < 8 * b + 8), 0.0, tile) - terms[0]

    for first in range(0, TILES, 2):
        blocks = [b for b in (first, first + 1) if b < TILES]
        in_blocks = (lane >= 8 * first) & (lane < 8 * first + 8 * len(blocks))
        before = [list(chain) for chain in chains]
        for b in blocks:
            for chain in chains:
                chain[b] = eliminate(b, chain[b])
                for i in range(first, min(first + 4, TILES)):
                    if i != b:
                        chain[i] = reduced(b, chain[i], chain[b])
        for chain, old in zip(chains, before):
            spread = jnp.concatenate([chain[r] if r in blocks else empty for r in range(16)], axis=0)
            change = dot(jnp.concatenate(old, axis=0), spread)
            for i in range(TILES):
                if not first <= i < first + 4:
                    chain[i] = jnp.where(in_blocks, 0.0, old[i]) - change[8 * i : 8 * i + 8]
    return chains


OFFSETS = (0, PC, -PC, 1, -1)
BANDS = (0, 1, 2, 9, 10, 11, 20)


def zone_kernel(
    sizes, sc, own_u, own_f, r1, r2, out,
    ua, ub, fo, m3, cx, cy, cz, iv, rows, band, up, down, far, grad, hess, bl, br, yt, zs, dl, gs,
):
    nx, ny, nz = sizes
    low_first = sc[0] == 0
    rely = sc[2]
    lane32 = iota((WY, 128), 1)
    group = lax.shift_right_arithmetic(lane32, 5)
    inner = lane32 & 31
    row32 = iota((WY, 128), 0)
    shift = -(rely + 11)

    inside_y = sc[11] - 5 + row32
    inside_z = sc[12] - 5 + inner
    inside = (inside_y >= 0) & (inside_y < ny) & (inside_z >= 0) & (inside_z < nz)

    def unpack(i):
        for step in range(2):
            gx = sc[10] - 5 + 2 * i + step
            good = inside & (gx >= 0) & (gx < nx)
            for which in range(2):
                number = 2 * step + which
                first = r1[i, 8 * number : 8 * number + 8]
                second = r2[i, 8 * number : 8 * number + 8]
                mix1 = r1[i, 32:40]
                mix2 = r2[i, 32:40]
                low, high = jnp.where(low_first, first, second), jnp.where(low_first, second, first)
                low_mix, high_mix = jnp.where(low_first, mix1, mix2), jnp.where(low_first, mix2, mix1)
                middle = own_u[2 * i + step] if which == 0 else own_f[2 * i + step]
                tall = jnp.concatenate(
                    [row_roll(low_mix, 6 - 2 * number), low, middle, high, row_roll(high_mix, -2 * number)], axis=0
                )
                tall = row_roll(tall, shift)[0:WY]
                if which == 0:
                    tall = jnp.where(good, tall, 0.0)
                    ua[2 * i + step] = tall
                    moved = jnp.where(group == 0, lane_roll(tall, 32), 0.0)
                    moved = jnp.where(group == 1, lane_roll(tall, 64), moved)
                    m3[2 * i + step] = jnp.where(group == 2, lane_roll(tall, 96), moved)
                else:
                    fo[2 * i + step] = tall

    loop(0, WIN // 2, unpack, 5)

    def faces(i):
        here = m3[i]
        cx[i] = 0.5 * (here + m3[jnp.minimum(i + 1, WIN - 1)])
        cy[i] = 0.5 * (here + row_roll(here, -1))
        cz[i] = 0.5 * (here + lane_roll(here, -1))

    loop(0, WIN, faces, 15)

    def scale(i):
        total = MASS_TERM + cx[i] + cx[i - 1] + cy[i] + row_roll(cy[i], 1) + cz[i] + lane_roll(cz[i], 1)
        gx = sc[10] - 5 + i
        good = inside & (gx >= 0) & (gx < nx)
        iv[i] = jnp.where(good, 1.0 / total, 0.0)

    loop(1, WIN - 1, scale, 14)

    for sweep in range(FSWEEPS):
        src, dst = (ua, ub) if sweep % 2 == 0 else (ub, ua)

        def relax(i, src=src, dst=dst):
            here = src[i]
            total = fo[i] + cx[i] * src[i + 1] + cx[i - 1] * src[i - 1]
            total = total + cy[i] * row_roll(here, -1) + row_roll(cy[i] * here, 1)
            total = total + cz[i] * lane_roll(here, -1) + lane_roll(cz[i] * here, 1)
            dst[i] = total * iv[i]

        loop(sweep + 1, WIN - 1 - sweep, relax, WIN - 2 - 2 * sweep)

    line = iota((128, 384), 0)
    column = iota((128, 384), 1)
    part = lax.shift_right_arithmetic(column, 7)
    spot = column & 127
    spot_y = div10(spot)
    spot_z = spot - PC * spot_y
    inner_z = (line & 31) - 5
    hit = (lax.shift_right_arithmetic(line, 5) == part) & (inner_z >= 0) & (inner_z < SPAN) & (spot < PC * PC)
    hit = hit & (lax.shift_right_arithmetic(inner_z, 1) == spot_z)
    selector = jnp.where(hit, 1.0, 0.0).astype(BF16)
    zone_y = row32 - 5
    lane_y = div10(lane32)
    pick_y = (zone_y >= 0) & (zone_y < SPAN) & (lax.shift_right_arithmetic(zone_y, 1) == lane_y) & (lane32 < PC * PC)
    pick_y = jnp.where(pick_y, 1.0, 0.0)
    even_y = (zone_y & 1) == 0
    even_z = ((inner - 5) & 1) == 0
    rows[...] = jnp.zeros(rows.shape, F32)

    def layer(a):
        sums = None
        for odd in range(2):
            i = 5 + 2 * a + odd
            here, m_here = ua[i], m3[i]
            ch_x, ch_b = here - ua[i + 1], ua[i - 1] - here
            ch_y = here - row_roll(here, -1)
            ch_z = here - lane_roll(here, -1)
            flow_y, flow_z = cy[i] * ch_y, cz[i] * ch_z
            applied = MASS_TERM * here + cx[i] * ch_x - cx[i - 1] * ch_b
            applied = applied + flow_y - row_roll(flow_y, 1) + flow_z - lane_roll(flow_z, 1)
            resid = fo[i] - applied
            back_y, back_z = row_roll(ch_y, 1), lane_roll(ch_z, 1)
            laplace = ch_x - ch_b + ch_y - back_y + ch_z - back_z
            xp = -0.5 * m3[i + 1] * ch_x
            xm = 0.5 * m3[i - 1] * ch_b
            yp = -0.5 * row_roll(m_here, -1) * ch_y
            ym = 0.5 * row_roll(m_here, 1) * back_y
            zp = -0.5 * lane_roll(m_here, -1) * ch_z
            zm = 0.5 * lane_roll(m_here, 1) * back_z
            diag = -0.5 * m_here * laplace + jnp.where(even_y, yp, ym) + jnp.where(even_z, zp, zm)
            diag = diag + (xm if odd else xp)
            now = [
                diag, xp if odd else None, None if odd else xm,
                jnp.where(even_y, 0.0, yp), jnp.where(even_y, ym, 0.0),
                jnp.where(even_z, 0.0, zp), jnp.where(even_z, zm, 0.0), resid,
            ]
            if sums is None:
                sums = now
            else:
                sums = [p if q is None else (q if p is None else p + q) for p, q in zip(sums, now)]
        tall = dot_exact(jnp.concatenate(sums, axis=0), selector)
        for n in range(8):
            for k in range(3):
                piece = tall[n * WY : (n + 1) * WY, 128 * k : 128 * k + 128] * pick_y
                rows[n, k, pl.ds(a, 1), :] = jnp.sum(piece, axis=0, keepdims=True)

    loop(0, PC, layer, PC)

    lane16 = iota((16, 128), 1)
    row16 = iota((16, 128), 0)
    at_y = div10(lane16)
    at_z = lane16 - PC * at_y

    def masked(n, keep):
        return [jnp.where(keep, rows[n, k], 0.0) for k in range(3)]

    full = row16 < PC
    v = {
        0: masked(0, full),
        PC: masked(3, full & (at_y < PC - 1)),
        -PC: masked(4, full & (at_y > 0)),
        1: masked(5, full & (at_z < PC - 1)),
        -1: masked(6, full & (at_z > 0)),
    }
    vxp = masked(1, row16 < PC - 1)
    vxm = masked(2, full & (row16 > 0))
    res = masked(7, full)

    def mix(p, q):
        return p[0] * q[0] + p[1] * q[1] + p[2] * q[2]

    bands = {}
    for o1 in OFFSETS:
        for o2 in OFFSETS:
            key = o1 - o2
            if key >= 0:
                term = lane_roll(mix(v[o1], v[o2]), o2)
                bands[key] = bands[key] + term if key in bands else term
    bands[0] = bands[0] + row_roll(mix(vxp, vxp), 1) + row_roll(mix(vxm, vxm), -1)
    trace = jnp.sum(jnp.sum(bands[0], axis=1, keepdims=True), axis=0, keepdims=True)
    ridge = DAMPING * trace / PC**3 + EPSILON
    bands[0] = jnp.where(lane16 < PC * PC, bands[0] + ridge, jnp.where(lane16 < ROWS, 1.0, 0.0))
    slots = {}
    for n, key in enumerate(BANDS):
        band[n] = bands[key]
        slots[key] = n
    for n, key in enumerate(BANDS[1:]):
        band[len(BANDS) + n] = lane_roll(bands[key], key)
        slots[-key] = len(BANDS) + n
    for n, key in enumerate(OFFSETS):
        above = row_roll(mix(vxm, v[-key]), -1)
        below = row_roll(mix(vxp, v[-key]), 1)
        up[n] = mix(vxp, v[key]) + lane_roll(above, -key)
        down[n] = mix(vxm, v[key]) + lane_roll(below, -key)
    cross = mix(vxm, vxp)
    far[0] = row_roll(cross, -1)
    far[1] = row_roll(cross, 1)
    gradient = row_roll(mix(vxp, res), 1) + row_roll(mix(vxm, res), -1)
    for key in OFFSETS:
        gradient = gradient + lane_roll(mix(v[key], res), key)
    grad[...] = gradient

    sub = iota((8, 128), 0)
    lane8 = iota((8, 128), 1)

    def spread(ref, n, x):
        return jnp.broadcast_to(ref[n, pl.ds(x, 1), :], (8, 128))

    def fill(dst, lines, lead):
        for r in range(TILES):
            apart = sub + 8 * r - lane8
            tile = jnp.zeros((8, 128), F32)
            for key, values in lines:
                if 8 * r + 7 - key >= 0 and 8 * r - key < 128:
                    tile = jnp.where(apart == key, values, tile)
            dst[lead + (slice(8 * r, 8 * r + 8), slice(None))] = tile
        dst[lead + (slice(ROWS, 128), slice(None))] = jnp.zeros((128 - ROWS, 128), F32)

    def dense(x, carry):
        fill(hess, [(key, spread(band, n, x)) for key, n in slots.items()], (x,))
        gs[x] = jnp.broadcast_to(grad[pl.ds(x, 1), :], (8, 128))
        return carry

    lax.fori_loop(0, PC, dense, 0)

    def couple(t, carry):
        right = PC - 1 - t
        fill(bl, [(key, spread(up, n, t)) for n, key in enumerate(OFFSETS)], (t, 0))
        fill(bl, [(key, spread(down, n, t + 1)) for n, key in enumerate(OFFSETS)], (t, 1))

        @pl.when(t < 4)
        def _():
            fill(br, [(key, spread(down, n, right)) for n, key in enumerate(OFFSETS)], (t, 0))
            fill(br, [(key, spread(up, n, right - 1)) for n, key in enumerate(OFFSETS)], (t, 1))

        return carry

    lax.fori_loop(0, 5, couple, 0)
    br[4] = jnp.zeros((2, 128, 128), F32)

    on_diagonal = iota((128, 128), 0) == iota((128, 128), 1)
    ones = jnp.ones((128, 128), BF16)

    def tiles_of(x):
        return [hess[x, 8 * r : 8 * r + 8, :] for r in range(TILES)]

    def whole(chain):
        return jnp.concatenate(chain + [jnp.zeros((128 - ROWS, 128), F32)], axis=0)

    def eliminate(t, carry):
        right = PC - 1 - t
        left_tiles, right_tiles = invert([tiles_of(t), tiles_of(right)])
        for s, tiles, x, step, ref in ((0, left_tiles, t, 1, bl), (1, right_tiles, right, -1, br)):
            q = whole(tiles)
            row = jnp.broadcast_to(far[s, pl.ds(x, 1), :], (128, 128))
            column = dot_exact(jnp.where(on_diagonal, row, 0.0), ones)
            w, wt = ref[t, 0], ref[t, 1]
            y1, y2 = dot(q, w), q * row
            yt[s, t, 0:128] = dot(wt, q)
            yt[s, t, 128:256] = column * q
            s1 = dot(wt, jnp.concatenate([y1, y2], axis=1))
            g = gs[x]
            z = dot(g, q)
            zs[s, t] = z
            one, two_on = x + step, x + 2 * step
            hess[one] = hess[one] - s1[:, 0:128]
            hess[two_on] = hess[two_on] - column * y2
            ref[t + 1, 0] = ref[t + 1, 0] - s1[:, 128:256]
            ref[t + 1, 1] = ref[t + 1, 1] - column * y1
            gs[one] = gs[one] - dot(z, w)
            gs[two_on] = gs[two_on] - z * row[0:8]
        return carry

    lax.fori_loop(0, 4, eliminate, 0)

    def middle(t, carry):
        x = 4 + t
        (tiles,) = invert([tiles_of(x)])
        q = whole(tiles)
        g = gs[x]
        dl[x] = dot(g, q)

        @pl.when(t == 0)
        def _():
            w = bl[4, 0] + br[4, 1]
            wt = bl[4, 1] + br[4, 0]
            y = dot(q, w)
            yt[0, 4, 0:128] = dot(wt, q)
            hess[5] = hess[5] - dot(wt, y)
            gs[5] = gs[5] - dot(g, y)

        return carry

    lax.fori_loop(0, 2, middle, 0)
    dl[4] = dl[4] - dot(dl[5], yt[0, 4, 0:128])
    for t in (3, 2, 1, 0):
        right = PC - 1 - t
        dl[t] = zs[0, t] - dot(jnp.concatenate([dl[t + 1], dl[t + 2]], axis=1), yt[0, t])
        dl[right] = zs[1, t] - dot(jnp.concatenate([dl[right - 1], dl[right - 2]], axis=1), yt[1, t])
    for x in range(PC):
        out[x : x + 1, :] = -dl[x, 0:1, :]
    spare = iota((16 - PC, 128), 1)
    corner = jnp.zeros((16 - PC, 128), F32)
    for n in range(3):
        corner = jnp.where(spare == n, sc[10 + n].astype(F32), corner)
    out[PC:16, :] = corner


def field_kernel(
    sizes, sc, u, f, m, x1, x2, strip, strip1, strip2, s1, s2, out,
    ua, ub, fo, mo, cx, cy, zu, zd, ze, iv, ba, bb, bf, bm, bx, by, bz, bi,
):
    nx, ny, nz = sizes
    low_first = sc[0] == 0
    sub = iota((8, 128), 0)
    lane = iota((AX, 128), 1)
    group = lax.shift_right_arithmetic(lane, 5)
    inner = lane & 31
    lead = DEEP - FSWEEPS
    w0 = jnp.where(low_first, BZ - 8, -8)
    zoff = jnp.where(low_first, BZ, -DEEP)
    z = inner + w0
    main_ok = (z >= 0) & (z < BZ)
    far_ok = (z >= zoff) & (z < zoff + DEEP)
    edge_lane = jnp.where(low_first, BZ - 1, 0)
    edge_from = jnp.where(low_first, 8, 7)
    at_edge = lane == edge_lane
    row24 = iota((AX, 128), 0)
    gy = sc[14] - FSWEEPS + row24
    inside = (gy >= 0) & (gy < ny)

    def build(dest, values16):
        gx = sc[13] - FSWEEPS + dest
        good = inside & (gx >= 0) & (gx < nx)
        every = []
        for q in range(8):
            j = q // 2
            a = s1[dest, 8 * j : 8 * j + 8]
            b = s2[dest, 8 * j : 8 * j + 8]
            low, high = jnp.where(low_first, a, b), jnp.where(low_first, b, a)
            if q % 2 == 0:
                high = row_roll(high, 4)
            else:
                low = row_roll(low, 4)
            t0, t1 = row_roll(values16[q][0:8], 4), row_roll(values16[q][8:16], 4)
            tall = jnp.concatenate(
                [jnp.where(sub < 4, low, t0), jnp.where(sub < 4, t0, t1), jnp.where(sub < 4, t1, high)], axis=0
            )
            every.append(jnp.where(good, tall, 0.0))
        for k in range(3):
            ua[k, dest] = every[k]
            fo[k, dest] = every[3 + k]
        mo[dest] = every[6]
        side = []
        for channels in ((0, 1, 2), (3, 4, 5)):
            main, far = jnp.zeros((AX, 128), F32), jnp.zeros((AX, 128), F32)
            for k, c in enumerate(channels):
                main = jnp.where(group == k, lane_roll(every[c], 32 * k - w0), main)
                far = jnp.where(group == k, lane_roll(every[7], 32 * k + zoff - w0 - DEEP * c), far)
            side.append(jnp.where(main_ok, main, jnp.where(far_ok, far, 0.0)))
        ba[dest], bf[dest] = side
        main = jnp.where(main_ok, lane_roll(every[6], -w0), jnp.where(far_ok, lane_roll(every[7], zoff - w0 - DEEP * 6), 0.0))
        first = jnp.where(group == 0, main, 0.0)
        first = jnp.where(group == 1, lane_roll(main, 32), first)
        bm[dest] = jnp.where(group == 2, lane_roll(main, 64), first)

    def inner_plane(i):
        build(i + FSWEEPS, [u[k, i] for k in range(3)] + [f[k, i] for k in range(3)] + [m[i], strip[i]])

    loop(0, BX, inner_plane, 4)

    def outer_plane(i):
        for a, b, sa, sb, start, dest in (
            (x1, x2, strip2, strip1, lead, i), (x2, x1, strip1, strip2, 0, i + FSWEEPS + BX),
        ):
            j = i + start
            force = j - (1 if start else 0)

            def pick(index):
                return jnp.where(low_first, a[index], b[index])

            build(
                dest,
                [pick(k * DEEP + j) for k in range(3)]
                + [pick(3 * DEEP + k * (DEEP - 1) + force) for k in range(3)]
                + [pick(PLANES - DEEP + j), jnp.where(low_first, sa[j], sb[j])],
            )

    loop(0, FSWEEPS, outer_plane, 2)

    def edge(values, k):
        return jnp.where(at_edge, lane_roll(values, edge_lane - edge_from - 32 * k), 0.0)

    def faces(i):
        here, there = mo[i], bm[i]
        cx[i] = 0.5 * (here + mo[jnp.minimum(i + 1, AX - 1)])
        bx[i] = 0.5 * (there + bm[jnp.minimum(i + 1, AX - 1)])
        cy[i] = 0.5 * (here + row_roll(here, -1))
        by[i] = 0.5 * (there + row_roll(there, -1))
        bz[i] = 0.5 * (there + lane_roll(there, -1))
        zu[i] = jnp.where(lane == BZ - 1, 0.0, 0.5 * (here + lane_roll(here, -1)))
        zd[i] = jnp.where(lane == 0, 0.0, 0.5 * (here + lane_roll(here, 1)))
        ze[i] = jnp.where(at_edge, 0.5 * (here + edge(there, 0)), 0.0)

    loop(0, AX, faces, 12)
    side_inside = (sc[15] + z >= 0) & (sc[15] + z < nz)
    far_edge = BZ - 1 - edge_lane

    def scale(i):
        open_face = jnp.where(lane == far_edge, 0.5 * mo[i], 0.0)
        total = MASS_TERM + cx[i] + cx[i - 1] + cy[i] + row_roll(cy[i], 1) + zu[i] + zd[i] + ze[i] + open_face
        gx = sc[13] - FSWEEPS + i
        good = inside & (gx >= 0) & (gx < nx)
        iv[i] = jnp.where(good, 1.0 / total, 0.0)
        total = MASS_TERM + bx[i] + bx[i - 1] + by[i] + row_roll(by[i], 1) + bz[i] + lane_roll(bz[i], 1)
        bi[i] = jnp.where(good & side_inside, 1.0 / total, 0.0)

    loop(1, AX - 1, scale, 11)
    for sweep in range(FSWEEPS):
        src, dst = (ua, ub) if sweep % 2 == 0 else (ub, ua)
        bsrc, bdst = (ba, bb) if sweep % 2 == 0 else (bb, ba)

        def relax(i, src=src, dst=dst, bsrc=bsrc, bdst=bdst, last=sweep == FSWEEPS - 1):
            there = bsrc[i]
            for k in range(3):
                here = src[k, i]
                total = fo[k, i] + cx[i] * src[k, i + 1] + cx[i - 1] * src[k, i - 1]
                total = total + cy[i] * row_roll(here, -1) + row_roll(cy[i] * here, 1)
                total = total + zu[i] * lane_roll(here, -1) + zd[i] * lane_roll(here, 1) + ze[i] * edge(there, k)
                total = total * iv[i]
                if last:
                    out[k, i - FSWEEPS] = row_roll(total, -FSWEEPS)[0:BY]
                else:
                    dst[k, i] = total
            if not last:
                total = bf[i] + bx[i] * bsrc[i + 1] + bx[i - 1] * bsrc[i - 1]
                total = total + by[i] * row_roll(there, -1) + row_roll(by[i] * there, 1)
                total = total + bz[i] * lane_roll(there, -1) + lane_roll(bz[i] * there, 1)
                bdst[i] = total * bi[i]

        loop(sweep + 1, AX - 1 - sweep, relax, AX - 2 - 2 * sweep)


def taper(offset):
    folded = jnp.minimum(offset, SPAN - 1 - offset)
    total = jnp.zeros(offset.shape, F32)
    for n in range(PC):
        total = jnp.where(folded == float(n), math.sin(math.pi * (n + 0.5) / SPAN), total)
    return total


def contribution(sc, delta, start, planes):
    rows = 16 if planes > 8 else 8
    laneix = iota((rows, 128), 1)
    lane16i = iota((16, 128), 1)
    lane_y = div10(lane16i).astype(F32)
    rows128 = iota((128, 128), 0)
    rows_z = (rows128 - PC * div10(rows128)).astype(F32)

    def place(axis):
        return delta[PC : PC + 1, axis : axis + 1] - sc[13 + axis].astype(F32)

    off_x = (iota((rows, 128), 0) + start).astype(F32) - place(0)
    apart = off_x - 2.0 * laneix.astype(F32)
    choose = jnp.where((apart >= 0.0) & (apart < 2.0) & (laneix < PC), 1.0, 0.0).astype(BF16)[:, 0:16]
    picked = [lax.dot_general(choose, p, (((1,), (0,)), ((), ())), preferred_element_type=F32) for p in three_parts(delta)]
    lines = (picked[0] + picked[1] + picked[2]) * taper(off_x)
    off_y = iota((16, 128), 0).astype(F32) - place(1)
    apart = off_y - 2.0 * lane_y
    cover = jnp.where((apart >= 0.0) & (apart < 2.0) & (lane16i < PC * PC), taper(off_y), 0.0)
    off_z = iota((128, 128), 1).astype(F32) - place(2)
    apart = off_z - 2.0 * rows_z
    expand = jnp.where((apart >= 0.0) & (apart < 2.0) & (rows128 < PC * PC), 1.0, 0.0).astype(BF16)
    tall = jnp.concatenate([jnp.broadcast_to(lines[x : x + 1, :], (BY, 128)) * cover for x in range(planes)], axis=0)
    return dot_exact(tall, expand) * taper(off_z[0:1, :])


def near_kernel(sc, parts, acc):
    acc[...] = jnp.zeros(acc.shape, F32)

    def add(n):
        acc[...] += contribution(sc, parts[n], 0, BX)

    loop(0, parts.shape[0], add, 6)


def final_kernel(sc, m, near, parts1, parts2, out, acc):
    acc[...] = near[...]
    reach = HALO - 1
    start1 = jnp.where(sc[0] == 0, 0, BX - reach)
    start2 = BX - reach - start1

    def add(n):
        for parts, start in ((parts1, start1), (parts2, start2)):
            where = pl.ds(pl.multiple_of(start * BY, BY), reach * BY)
            acc[where, :] += contribution(sc, parts[n], start, reach)

    loop(0, parts1.shape[0], add, 6)
    for x in range(BX):
        out[x] = m[x] * (1.0 + acc[16 * x : 16 * x + 16, :])


def call(kernel, shapes, scratch, inputs, flops, space=pltpu.VMEM, limit=VMEM_LIMIT):
    specs = [pl.BlockSpec(memory_space=pltpu.SMEM)] + [pl.BlockSpec(memory_space=space)] * (len(inputs) - 1)
    single = not isinstance(shapes, list)
    outs = [jax.ShapeDtypeStruct(s, F32) for s in ([shapes] if single else shapes)]
    results = pl.pallas_call(
        kernel,
        out_shape=outs,
        in_specs=specs,
        out_specs=[pl.BlockSpec(memory_space=pltpu.VMEM)] * len(outs),
        scratch_shapes=[pltpu.VMEM(s, F32) if isinstance(s, tuple) else s for s in scratch],
        compiler_params=pltpu.CompilerParams(vmem_limit_bytes=limit),
        cost_estimate=pl.CostEstimate(flops=flops, bytes_accessed=1 << 20, transcendentals=0),
    )(*inputs)
    return results[0] if single else results


def body(forcing, start_field, modulus, corners):
    counts = tuple(lax.axis_size(axis) for axis in AXES)
    sizes = (counts[0] * BX, counts[1] * BY, counts[2] * BZ)
    place = tuple(lax.axis_index(axis) for axis in AXES)
    gz = place[2].astype(jnp.int32)
    lower = jnp.stack([place[0] * BX, place[1] * BY, place[2] * BZ]).astype(jnp.int32)

    def send(values, move):
        pairs = []
        for x in range(counts[0]):
            for y in range(counts[1]):
                for z in range(counts[2]):
                    to = [t % c for t, c in zip(move(x, y, z), counts)]
                    pairs.append(((x * counts[1] + y) * counts[2] + z, (to[0] * counts[1] + to[1]) * counts[2] + to[2]))
        return lax.ppermute(values, AXES, pairs)

    def turn(z):
        return 1 if z == 0 else -1

    relative = corners[0] - lower
    near = jnp.broadcast_to(relative[None, :], (1, 3))
    want1 = send(near, lambda x, y, z: (x, y - turn(z), z))
    want2 = send(near, lambda x, y, z: (x, y + turn(z), z))
    scalar = jnp.concatenate([gz[None], relative, want1[0], want2[0], corners[0], lower]).astype(jnp.int32)
    first = gz[None]

    msg1, msg2, strip, strip1, strip2 = call(
        edge_kernel,
        [(PLANES, BY, 128), (PLANES, BY, 128), (BX, BY, 128), (DEEP, BY, 128), (DEEP, BY, 128)],
        [(3, BX, BY, BZ), (3, BX, BY, BZ), (BX, BY, BZ), pltpu.SemaphoreType.DMA((3,))],
        [first, start_field, forcing, modulus],
        1 << 20,
        pltpu.HBM,
        LARGE_LIMIT,
    )
    x1 = send(msg1, lambda x, y, z: (x + turn(z), y, z))
    x2 = send(msg2, lambda x, y, z: (x - turn(z), y, z))
    far_strip = send(strip, lambda x, y, z: (x, y, 1 - z))
    far1 = send(strip1, lambda x, y, z: (x + turn(z), y, 1 - z))
    far2 = send(strip2, lambda x, y, z: (x - turn(z), y, 1 - z))
    spread = [scalar, start_field, forcing, modulus, x1, x2, far_strip, far1, far2]
    a1, a2 = call(side_kernel, [(AX, 32, 128)] * 2, [], spread, 1 << 20)
    b1 = send(a1, lambda x, y, z: (x, y + turn(z), z))
    b2 = send(a2, lambda x, y, z: (x, y - turn(z), z))
    own_u, own_f, y1, y2 = call(
        pack_kernel,
        [(WIN, BY, 128)] * 2 + [(WIN // 2, 40, 128)] * 2,
        [(3, 36, BY, 128), (3, 36, BY, 128), (36, BY, 128), (36, BY, 128)],
        spread,
        1 << 31,
    )
    r1 = send(y1, lambda x, y, z: (x, y + turn(z), z))
    r2 = send(y2, lambda x, y, z: (x, y - turn(z), z))
    wide = (AX, AX, 128)
    displacement = call(
        functools.partial(field_kernel, sizes),
        (3, BX, BY, BZ),
        [(3,) + wide] * 3 + [wide] * 15,
        spread + [b1, b2],
        1 << 32,
    )
    own_u, own_f, r1, r2, displacement = lax.optimization_barrier((own_u, own_f, r1, r2, displacement))
    window = (WIN, WY, 128)
    delta = call(
        functools.partial(zone_kernel, sizes),
        (16, 128),
        [window] * 8
        + [
            (8, 3, 16, 128), (13, 16, 128), (5, 16, 128), (5, 16, 128), (2, 16, 128), (16, 128),
            (PC, 128, 128), (5, 2, 128, 128), (5, 2, 128, 128), (2, 5, 256, 128), (2, 5, 8, 128), (PC, 8, 128), (PC, 8, 128),
        ],
        [scalar, own_u, own_f, r1, r2],
        1 << 33,
    )
    plane = jnp.stack([delta, send(delta, lambda x, y, z: (x, y, 1 - z))])
    right = send(plane, lambda x, y, z: (x, y + turn(z), z))
    left = send(plane, lambda x, y, z: (x, y - turn(z), z))
    plane = jnp.concatenate([plane, right, left])
    after = send(plane, lambda x, y, z: (x + turn(z), y, z))
    before = send(plane, lambda x, y, z: (x - turn(z), y, z))
    near = call(near_kernel, (BX * BY, 128), [], [scalar, plane], 1 << 29)
    near, after, before = lax.optimization_barrier((near, after, before))
    new_modulus = call(
        final_kernel, (BX, BY, BZ), [(BX * BY, 128)], [scalar, modulus, near, after, before], 1 << 24
    )
    return displacement, new_modulus


def solution(mesh):
    placed = (
        P(None, "gx", "gy", "gz"),
        P(None, "gx", "gy", "gz"),
        P("gx", "gy", "gz"),
        P(("gx", "gy", "gz"), None),
    )
    return jax.shard_map(
        body,
        mesh=mesh,
        in_specs=placed,
        out_specs=(P(None, "gx", "gy", "gz"), P("gx", "gy", "gz")),
        check_vma=False,
    )
```

```python
import functools
import math

import jax
import jax.numpy as jnp
from jax import lax
from jax.experimental import pallas as pl
from jax.experimental.pallas import tpu as pltpu
from jax.sharding import PartitionSpec as P

PC = 10
SPAN = 2 * PC
FSWEEPS = 4
MASS_TERM = 0.5
DAMPING = 0.1
EPSILON = 1e-06
BX, BY, BZ = 16, 16, 128
HALO = 6
DEEP = 10
WIN = 30
WY = 32
AX = 24
ROWS = 104
TILES = ROWS // 8
PLANES = 3 * DEEP + 3 * (DEEP - 1) + DEEP
AXES = ("gx", "gy", "gz")
F32 = jnp.float32
BF16 = jnp.bfloat16
HIGH = lax.Precision.HIGHEST
VMEM_LIMIT = 48 * 1024 * 1024
LARGE_LIMIT = 61 * 1024 * 1024


def iota(shape, dim):
    return lax.broadcasted_iota(jnp.int32, shape, dim)


def lane_roll(values, shift):
    if isinstance(shift, int):
        shift = shift % values.shape[-1]
        return values if shift == 0 else pltpu.roll(values, shift, values.ndim - 1)
    size = values.shape[-1]
    return pltpu.roll(values, lax.rem(shift + 8 * size, size), values.ndim - 1)


def row_roll(values, shift):
    if isinstance(shift, int):
        shift = shift % values.shape[-2]
        return values if shift == 0 else pltpu.roll(values, shift, values.ndim - 2)
    size = values.shape[-2]
    return pltpu.roll(values, lax.rem(shift + 8 * size, size), values.ndim - 2)


def loop(low, high, step, unroll):
    whole = (high - low) // unroll
    if whole == 1:
        for i in range(low, low + unroll):
            step(i)
    elif whole > 1:

        def chunk(t, carry):
            for n in range(unroll):
                step(low + t * unroll + n)
            return carry

        lax.fori_loop(0, whole, chunk, 0)
    for i in range(low + whole * unroll, high):
        step(i)


def three_parts(values):
    first = values.astype(BF16)
    rest = values - first.astype(F32)
    second = rest.astype(BF16)
    third = (rest - second.astype(F32)).astype(BF16)
    return first, second, third


def dot(a, b):
    return lax.dot_general(a, b, (((1,), (0,)), ((), ())), precision=HIGH, preferred_element_type=F32)


def dot_exact(values, selector):
    parts = [
        lax.dot_general(part, selector, (((1,), (0,)), ((), ())), preferred_element_type=F32)
        for part in three_parts(values)
    ]
    return parts[0] + parts[1] + parts[2]


def div10(value):
    return lax.shift_right_arithmetic(value * 205, 11)


def edge_kernel(sc, u, f, m, msg1, msg2, strip, strip1, strip2, vu, vf, vm, sems):
    gz = sc[0]
    low_first = gz == 0
    s1 = jnp.where(low_first, BX - DEEP, 0)
    s2 = BX - DEEP - s1
    f1 = jnp.where(low_first, BX - DEEP + 1, 0)
    f2 = BX - DEEP + 1 - f1
    loads = [pltpu.make_async_copy(u, vu, sems.at[0]), pltpu.make_async_copy(f, vf, sems.at[1])]
    loads.append(pltpu.make_async_copy(m, vm, sems.at[2]))
    for load in loads:
        load.start()
    for load in loads:
        load.wait()
    lane = iota((BY, 128), 1)
    extra = jnp.where(low_first, DEEP, 0)

    def one(x):
        total = jnp.zeros((BY, 128), F32)
        for c in range(7):
            source = vu[c, x] if c < 3 else (vf[c - 3, x] if c < 6 else vm[x])
            moved = lane_roll(source, extra + DEEP * c)
            total = jnp.where((lane >= DEEP * c) & (lane < DEEP * (c + 1)), moved, total)
        strip[x] = total

    loop(0, BX, one, 8)
    for out, s, fs in ((msg1, s1, f1), (msg2, s2, f2)):
        for k in range(3):
            out[k * DEEP : (k + 1) * DEEP] = vu[k, pl.ds(s, DEEP)]
            base = 3 * DEEP + k * (DEEP - 1)
            out[base : base + DEEP - 1] = vf[k, pl.ds(fs, DEEP - 1)]
        out[PLANES - DEEP : PLANES] = vm[pl.ds(s, DEEP)]
    strip1[...] = strip[pl.ds(s1, DEEP)]
    strip2[...] = strip[pl.ds(s2, DEEP)]


def pack_kernel(sc, u, f, m, x1, x2, strip, strip1, strip2, own_u, own_f, msg1, msg2, eu, ef, em, es):
    gz = sc[0]
    low_first = gz == 0
    p1 = jnp.where(low_first, 0, BX + DEEP)
    p2 = BX + DEEP - p1
    q1 = jnp.where(low_first, 1, BX + DEEP)
    q2 = BX + DEEP + 1 - q1
    for k in range(3):
        eu[k, DEEP : DEEP + BX] = u[k]
        ef[k, DEEP : DEEP + BX] = f[k]
        ef[k, 0] = jnp.zeros((BY, 128), F32)
        ef[k, 2 * DEEP + BX - 1] = jnp.zeros((BY, 128), F32)
        for msg, p, q in ((x1, p1, q1), (x2, p2, q2)):
            eu[k, pl.ds(p, DEEP)] = msg[k * DEEP : (k + 1) * DEEP]
            base = 3 * DEEP + k * (DEEP - 1)
            ef[k, pl.ds(q, DEEP - 1)] = msg[base : base + DEEP - 1]
    em[DEEP : DEEP + BX] = m[...]
    es[DEEP : DEEP + BX] = strip[...]
    em[pl.ds(p1, DEEP)] = x1[PLANES - DEEP : PLANES]
    em[pl.ds(p2, DEEP)] = x2[PLANES - DEEP : PLANES]
    es[pl.ds(p2, DEEP)] = strip1[...]
    es[pl.ds(p1, DEEP)] = strip2[...]

    lane = iota((BY, 128), 1)
    group = lax.shift_right_arithmetic(lane, 5)
    inner = lane & 31
    zoff = jnp.where(low_first, BZ, -DEEP)

    def window(relz):
        w0 = relz - (DEEP - 5)
        z = inner + w0
        main_ok = (z >= 0) & (z < BZ)
        strip_ok = (z >= zoff) & (z < zoff + DEEP)

        def take(x):
            side = es[x]
            values = []
            for sources in ((eu, 0), (ef, 3)):
                ref, first = sources
                main = jnp.zeros((BY, 128), F32)
                far = jnp.zeros((BY, 128), F32)
                for k in range(4 if first == 0 else 3):
                    source, c = (ref[k, x], first + k) if k < 3 else (em[x], 6)
                    main = jnp.where(group == k, lane_roll(source, 32 * k - w0), main)
                    far = jnp.where(group == k, lane_roll(side, 32 * k + zoff - w0 - DEEP * c), far)
                values.append(jnp.where(main_ok, main, jnp.where(strip_ok, far, 0.0)))
            return values

        return take

    take_own = window(sc[3])
    x0 = sc[1] + 5

    def own(i):
        field, force = take_own(x0 + i)
        own_u[i] = field
        own_f[i] = force

    loop(0, WIN, own, 10)

    sub = iota((8, 128), 0)
    for msg, base, upward in ((msg1, 4, low_first), (msg2, 7, gz != 0)):
        take = window(sc[base + 2])
        start = sc[base] + 5

        def pair(i, msg=msg, take=take, start=start, upward=upward):
            mixed = jnp.zeros((8, 128), F32)
            number = 0
            for step in range(2):
                for values in take(start + 2 * i + step):
                    top, bottom = values[0:8], values[8:16]
                    msg[i, 8 * number : 8 * number + 8] = jnp.where(upward, bottom, top)
                    edge = jnp.where(upward, row_roll(top, 2), bottom)
                    mixed = jnp.where((sub >= 2 * number) & (sub < 2 * number + 2), row_roll(edge, 2 * number), mixed)
                    number += 1
            msg[i, 32:40] = mixed

        loop(0, WIN // 2, pair, 5)


def side_kernel(sc, u, f, m, x1, x2, strip, strip1, strip2, side1, side2):
    low_first = sc[0] == 0
    sub = iota((8, 128), 0)

    def put(dest, values16):
        for side, upward in ((side1, low_first), (side2, sc[0] != 0)):
            every = [jnp.where(upward, row_roll(v[8:16], 4), v[0:8]) for v in values16]
            for j in range(4):
                side[dest, 8 * j : 8 * j + 8] = jnp.where(sub < 4, every[2 * j], row_roll(every[2 * j + 1], 4))

    def inner_plane(i):
        put(i + FSWEEPS, [u[k, i] for k in range(3)] + [f[k, i] for k in range(3)] + [m[i], strip[i]])

    loop(0, BX, inner_plane, 8)

    def outer_plane(i):
        for a, b, sa, sb, start, dest in (
            (x1, x2, strip2, strip1, DEEP - FSWEEPS, i), (x2, x1, strip1, strip2, 0, i + FSWEEPS + BX),
        ):
            j = i + start
            force = j - (1 if start else 0)

            def pick(index):
                return jnp.where(low_first, a[index], b[index])

            put(
                dest,
                [pick(k * DEEP + j) for k in range(3)]
                + [pick(3 * DEEP + k * (DEEP - 1) + force) for k in range(3)]
                + [pick(PLANES - DEEP + j), jnp.where(low_first, sa[j], sb[j])],
            )

    loop(0, FSWEEPS, outer_plane, 4)


def invert(chains):
    sub = iota((8, 128), 0)
    lane = iota((8, 128), 1)

    def row_of(values, j):
        return jnp.broadcast_to(values[j : j + 1, :], (8, 128))

    def column_of(values, j):
        return jnp.broadcast_to(values[:, j : j + 1], (8, 128))

    empty = jnp.zeros((8, 128), F32)

    def eliminate(b, tile):
        own = [column_of(tile, 8 * b + j) for j in range(8)]
        for j in range(0, 8, 2):
            here0, here1 = sub == j, sub == j + 1
            at0, at1 = lane == 8 * b + j, lane == 8 * b + j + 1
            p00, p01 = row_of(own[j], j), row_of(own[j + 1], j)
            p10, p11 = row_of(own[j], j + 1), row_of(own[j + 1], j + 1)
            scale = pl.reciprocal(p00 * p11 - p01 * p10, approx=True)
            side0 = jnp.where(here0, -1.0, jnp.where(here1, 0.0, own[j]))
            side1 = jnp.where(here0, 0.0, jnp.where(here1, -1.0, own[j + 1]))
            both = here0 | here1

            def step(values, line0, line1):
                first = p11 * line0 - p01 * line1
                second = p00 * line1 - p10 * line0
                return jnp.where(both, 0.0, values) - (side0 * first + side1 * second) * scale

            for n in range(j + 2, 8):
                own[n] = step(own[n], row_of(own[n], j), row_of(own[n], j + 1))
            line0 = jnp.where(at0, 1.0, jnp.where(at1, 0.0, row_of(tile, j)))
            line1 = jnp.where(at0, 0.0, jnp.where(at1, 1.0, row_of(tile, j + 1)))
            tile = step(jnp.where(at0 | at1, 0.0, tile), line0, line1)
        return tile

    def reduced(b, tile, pivot):
        terms = [column_of(tile, 8 * b + j) * row_of(pivot, j) for j in range(8)]
        while len(terms) > 1:
            terms = [p + q for p, q in zip(terms[0::2], terms[1::2])]
        return jnp.where((lane >= 8 * b) & (lane < 8 * b + 8), 0.0, tile) - terms[0]

    for first in range(0, TILES, 2):
        blocks = [b for b in (first, first + 1) if b < TILES]
        in_blocks = (lane >= 8 * first) & (lane < 8 * first + 8 * len(blocks))
        before = [list(chain) for chain in chains]
        for b in blocks:
            for chain in chains:
                chain[b] = eliminate(b, chain[b])
                for i in range(first, min(first + 4, TILES)):
                    if i != b:
                        chain[i] = reduced(b, chain[i], chain[b])
        for chain, old in zip(chains, before):
            spread = jnp.concatenate([chain[r] if r in blocks else empty for r in range(16)], axis=0)
            change = dot(jnp.concatenate(old, axis=0), spread)
            for i in range(TILES):
                if not first <= i < first + 4:
                    chain[i] = jnp.where(in_blocks, 0.0, old[i]) - change[8 * i : 8 * i + 8]
    return chains


OFFSETS = (0, PC, -PC, 1, -1)
BANDS = (0, 1, 2, 9, 10, 11, 20)


def zone_kernel(
    sizes, sc, own_u, own_f, r1, r2, out,
    ua, ub, fo, m3, cx, cy, cz, iv, rows, band, up, down, far, grad, hess, bl, br, yt, zs, dl, gs,
):
    nx, ny, nz = sizes
    low_first = sc[0] == 0
    rely = sc[2]
    lane32 = iota((WY, 128), 1)
    group = lax.shift_right_arithmetic(lane32, 5)
    inner = lane32 & 31
    row32 = iota((WY, 128), 0)
    shift = -(rely + 11)

    inside_y = sc[11] - 5 + row32
    inside_z = sc[12] - 5 + inner
    inside = (inside_y >= 0) & (inside_y < ny) & (inside_z >= 0) & (inside_z < nz)

    def unpack(i):
        for step in range(2):
            gx = sc[10] - 5 + 2 * i + step
            good = inside & (gx >= 0) & (gx < nx)
            for which in range(2):
                number = 2 * step + which
                first = r1[i, 8 * number : 8 * number + 8]
                second = r2[i, 8 * number : 8 * number + 8]
                mix1 = r1[i, 32:40]
                mix2 = r2[i, 32:40]
                low, high = jnp.where(low_first, first, second), jnp.where(low_first, second, first)
                low_mix, high_mix = jnp.where(low_first, mix1, mix2), jnp.where(low_first, mix2, mix1)
                middle = own_u[2 * i + step] if which == 0 else own_f[2 * i + step]
                tall = jnp.concatenate(
                    [row_roll(low_mix, 6 - 2 * number), low, middle, high, row_roll(high_mix, -2 * number)], axis=0
                )
                tall = row_roll(tall, shift)[0:WY]
                if which == 0:
                    tall = jnp.where(good, tall, 0.0)
                    ua[2 * i + step] = tall
                    moved = jnp.where(group == 0, lane_roll(tall, 32), 0.0)
                    moved = jnp.where(group == 1, lane_roll(tall, 64), moved)
                    m3[2 * i + step] = jnp.where(group == 2, lane_roll(tall, 96), moved)
                else:
                    fo[2 * i + step] = tall

    loop(0, WIN // 2, unpack, 5)

    def faces(i):
        here = m3[i]
        cx[i] = 0.5 * (here + m3[jnp.minimum(i + 1, WIN - 1)])
        cy[i] = 0.5 * (here + row_roll(here, -1))
        cz[i] = 0.5 * (here + lane_roll(here, -1))

    loop(0, WIN, faces, 15)

    def scale(i):
        total = MASS_TERM + cx[i] + cx[i - 1] + cy[i] + row_roll(cy[i], 1) + cz[i] + lane_roll(cz[i], 1)
        gx = sc[10] - 5 + i
        good = inside & (gx >= 0) & (gx < nx)
        iv[i] = jnp.where(good, 1.0 / total, 0.0)

    loop(1, WIN - 1, scale, 14)

    for sweep in range(FSWEEPS):
        src, dst = (ua, ub) if sweep % 2 == 0 else (ub, ua)

        def relax(i, src=src, dst=dst):
            here = src[i]
            total = fo[i] + cx[i] * src[i + 1] + cx[i - 1] * src[i - 1]
            total = total + cy[i] * row_roll(here, -1) + row_roll(cy[i] * here, 1)
            total = total + cz[i] * lane_roll(here, -1) + lane_roll(cz[i] * here, 1)
            dst[i] = total * iv[i]

        loop(sweep + 1, WIN - 1 - sweep, relax, WIN - 2 - 2 * sweep)

    line = iota((128, 384), 0)
    column = iota((128, 384), 1)
    part = lax.shift_right_arithmetic(column, 7)
    spot = column & 127
    spot_y = div10(spot)
    spot_z = spot - PC * spot_y
    inner_z = (line & 31) - 5
    hit = (lax.shift_right_arithmetic(line, 5) == part) & (inner_z >= 0) & (inner_z < SPAN) & (spot < PC * PC)
    hit = hit & (lax.shift_right_arithmetic(inner_z, 1) == spot_z)
    selector = jnp.where(hit, 1.0, 0.0).astype(BF16)
    zone_y = row32 - 5
    lane_y = div10(lane32)
    pick_y = (zone_y >= 0) & (zone_y < SPAN) & (lax.shift_right_arithmetic(zone_y, 1) == lane_y) & (lane32 < PC * PC)
    pick_y = jnp.where(pick_y, 1.0, 0.0)
    even_y = (zone_y & 1) == 0
    even_z = ((inner - 5) & 1) == 0
    rows[...] = jnp.zeros(rows.shape, F32)

    def layer(a):
        sums = None
        for odd in range(2):
            i = 5 + 2 * a + odd
            here, m_here = ua[i], m3[i]
            ch_x, ch_b = here - ua[i + 1], ua[i - 1] - here
            ch_y = here - row_roll(here, -1)
            ch_z = here - lane_roll(here, -1)
            flow_y, flow_z = cy[i] * ch_y, cz[i] * ch_z
            applied = MASS_TERM * here + cx[i] * ch_x - cx[i - 1] * ch_b
            applied = applied + flow_y - row_roll(flow_y, 1) + flow_z - lane_roll(flow_z, 1)
            resid = fo[i] - applied
            back_y, back_z = row_roll(ch_y, 1), lane_roll(ch_z, 1)
            laplace = ch_x - ch_b + ch_y - back_y + ch_z - back_z
            xp = -0.5 * m3[i + 1] * ch_x
            xm = 0.5 * m3[i - 1] * ch_b
            yp = -0.5 * row_roll(m_here, -1) * ch_y
            ym = 0.5 * row_roll(m_here, 1) * back_y
            zp = -0.5 * lane_roll(m_here, -1) * ch_z
            zm = 0.5 * lane_roll(m_here, 1) * back_z
            diag = -0.5 * m_here * laplace + jnp.where(even_y, yp, ym) + jnp.where(even_z, zp, zm)
            diag = diag + (xm if odd else xp)
            now = [
                diag, xp if odd else None, None if odd else xm,
                jnp.where(even_y, 0.0, yp), jnp.where(even_y, ym, 0.0),
                jnp.where(even_z, 0.0, zp), jnp.where(even_z, zm, 0.0), resid,
            ]
            if sums is None:
                sums = now
            else:
                sums = [p if q is None else (q if p is None else p + q) for p, q in zip(sums, now)]
        tall = dot_exact(jnp.concatenate(sums, axis=0), selector)
        for n in range(8):
            for k in range(3):
                piece = tall[n * WY : (n + 1) * WY, 128 * k : 128 * k + 128] * pick_y
                rows[n, k, pl.ds(a, 1), :] = jnp.sum(piece, axis=0, keepdims=True)

    loop(0, PC, layer, PC)

    lane16 = iota((16, 128), 1)
    row16 = iota((16, 128), 0)
    at_y = div10(lane16)
    at_z = lane16 - PC * at_y

    def masked(n, keep):
        return [jnp.where(keep, rows[n, k], 0.0) for k in range(3)]

    full = row16 < PC
    v = {
        0: masked(0, full),
        PC: masked(3, full & (at_y < PC - 1)),
        -PC: masked(4, full & (at_y > 0)),
        1: masked(5, full & (at_z < PC - 1)),
        -1: masked(6, full & (at_z > 0)),
    }
    vxp = masked(1, row16 < PC - 1)
    vxm = masked(2, full & (row16 > 0))
    res = masked(7, full)

    def mix(p, q):
        return p[0] * q[0] + p[1] * q[1] + p[2] * q[2]

    bands = {}
    for o1 in OFFSETS:
        for o2 in OFFSETS:
            key = o1 - o2
            if key >= 0:
                term = lane_roll(mix(v[o1], v[o2]), o2)
                bands[key] = bands[key] + term if key in bands else term
    bands[0] = bands[0] + row_roll(mix(vxp, vxp), 1) + row_roll(mix(vxm, vxm), -1)
    trace = jnp.sum(jnp.sum(bands[0], axis=1, keepdims=True), axis=0, keepdims=True)
    ridge = DAMPING * trace / PC**3 + EPSILON
    bands[0] = jnp.where(lane16 < PC * PC, bands[0] + ridge, jnp.where(lane16 < ROWS, 1.0, 0.0))
    slots = {}
    for n, key in enumerate(BANDS):
        band[n] = bands[key]
        slots[key] = n
    for n, key in enumerate(BANDS[1:]):
        band[len(BANDS) + n] = lane_roll(bands[key], key)
        slots[-key] = len(BANDS) + n
    for n, key in enumerate(OFFSETS):
        above = row_roll(mix(vxm, v[-key]), -1)
        below = row_roll(mix(vxp, v[-key]), 1)
        up[n] = mix(vxp, v[key]) + lane_roll(above, -key)
        down[n] = mix(vxm, v[key]) + lane_roll(below, -key)
    cross = mix(vxm, vxp)
    far[0] = row_roll(cross, -1)
    far[1] = row_roll(cross, 1)
    gradient = row_roll(mix(vxp, res), 1) + row_roll(mix(vxm, res), -1)
    for key in OFFSETS:
        gradient = gradient + lane_roll(mix(v[key], res), key)
    grad[...] = gradient

    sub = iota((8, 128), 0)
    lane8 = iota((8, 128), 1)

    def spread(ref, n, x):
        return jnp.broadcast_to(ref[n, pl.ds(x, 1), :], (8, 128))

    def fill(dst, lines, lead):
        for r in range(TILES):
            apart = sub + 8 * r - lane8
            tile = jnp.zeros((8, 128), F32)
            for key, values in lines:
                if 8 * r + 7 - key >= 0 and 8 * r - key < 128:
                    tile = jnp.where(apart == key, values, tile)
            dst[lead + (slice(8 * r, 8 * r + 8), slice(None))] = tile
        dst[lead + (slice(ROWS, 128), slice(None))] = jnp.zeros((128 - ROWS, 128), F32)

    def dense(x, carry):
        fill(hess, [(key, spread(band, n, x)) for key, n in slots.items()], (x,))
        gs[x] = jnp.broadcast_to(grad[pl.ds(x, 1), :], (8, 128))
        return carry

    lax.fori_loop(0, PC, dense, 0)

    def couple(t, carry):
        right = PC - 1 - t
        fill(bl, [(key, spread(up, n, t)) for n, key in enumerate(OFFSETS)], (t, 0))
        fill(bl, [(key, spread(down, n, t + 1)) for n, key in enumerate(OFFSETS)], (t, 1))

        @pl.when(t < 4)
        def _():
            fill(br, [(key, spread(down, n, right)) for n, key in enumerate(OFFSETS)], (t, 0))
            fill(br, [(key, spread(up, n, right - 1)) for n, key in enumerate(OFFSETS)], (t, 1))

        return carry

    lax.fori_loop(0, 5, couple, 0)
    br[4] = jnp.zeros((2, 128, 128), F32)

    on_diagonal = iota((128, 128), 0) == iota((128, 128), 1)
    ones = jnp.ones((128, 128), BF16)

    def tiles_of(x):
        return [hess[x, 8 * r : 8 * r + 8, :] for r in range(TILES)]

    def whole(chain):
        return jnp.concatenate(chain + [jnp.zeros((128 - ROWS, 128), F32)], axis=0)

    def eliminate(t, carry):
        right = PC - 1 - t
        left_tiles, right_tiles = invert([tiles_of(t), tiles_of(right)])
        for s, tiles, x, step, ref in ((0, left_tiles, t, 1, bl), (1, right_tiles, right, -1, br)):
            q = whole(tiles)
            row = jnp.broadcast_to(far[s, pl.ds(x, 1), :], (128, 128))
            column = dot_exact(jnp.where(on_diagonal, row, 0.0), ones)
            w, wt = ref[t, 0], ref[t, 1]
            y1, y2 = dot(q, w), q * row
            yt[s, t, 0:128] = dot(wt, q)
            yt[s, t, 128:256] = column * q
            s1 = dot(wt, jnp.concatenate([y1, y2], axis=1))
            g = gs[x]
            z = dot(g, q)
            zs[s, t] = z
            one, two_on = x + step, x + 2 * step
            hess[one] = hess[one] - s1[:, 0:128]
            hess[two_on] = hess[two_on] - column * y2
            ref[t + 1, 0] = ref[t + 1, 0] - s1[:, 128:256]
            ref[t + 1, 1] = ref[t + 1, 1] - column * y1
            gs[one] = gs[one] - dot(z, w)
            gs[two_on] = gs[two_on] - z * row[0:8]
        return carry

    lax.fori_loop(0, 4, eliminate, 0)

    def middle(t, carry):
        x = 4 + t
        (tiles,) = invert([tiles_of(x)])
        q = whole(tiles)
        g = gs[x]
        dl[x] = dot(g, q)

        @pl.when(t == 0)
        def _():
            w = bl[4, 0] + br[4, 1]
            wt = bl[4, 1] + br[4, 0]
            y = dot(q, w)
            yt[0, 4, 0:128] = dot(wt, q)
            hess[5] = hess[5] - dot(wt, y)
            gs[5] = gs[5] - dot(g, y)

        return carry

    lax.fori_loop(0, 2, middle, 0)
    dl[4] = dl[4] - dot(dl[5], yt[0, 4, 0:128])
    for t in (3, 2, 1, 0):
        right = PC - 1 - t
        dl[t] = zs[0, t] - dot(jnp.concatenate([dl[t + 1], dl[t + 2]], axis=1), yt[0, t])
        dl[right] = zs[1, t] - dot(jnp.concatenate([dl[right - 1], dl[right - 2]], axis=1), yt[1, t])
    for x in range(PC):
        out[x : x + 1, :] = -dl[x, 0:1, :]
    spare = iota((16 - PC, 128), 1)
    corner = jnp.zeros((16 - PC, 128), F32)
    for n in range(3):
        corner = jnp.where(spare == n, sc[10 + n].astype(F32), corner)
    out[PC:16, :] = corner


def field_kernel(
    sizes, sc, u, f, m, x1, x2, strip, strip1, strip2, s1, s2, out,
    ua, ub, fo, mo, cx, cy, zu, zd, ze, iv, ba, bb, bf, bm, bx, by, bz, bi,
):
    nx, ny, nz = sizes
    low_first = sc[0] == 0
    sub = iota((8, 128), 0)
    lane = iota((AX, 128), 1)
    group = lax.shift_right_arithmetic(lane, 5)
    inner = lane & 31
    lead = DEEP - FSWEEPS
    w0 = jnp.where(low_first, BZ - 8, -8)
    zoff = jnp.where(low_first, BZ, -DEEP)
    z = inner + w0
    main_ok = (z >= 0) & (z < BZ)
    far_ok = (z >= zoff) & (z < zoff + DEEP)
    edge_lane = jnp.where(low_first, BZ - 1, 0)
    edge_from = jnp.where(low_first, 8, 7)
    at_edge = lane == edge_lane
    row24 = iota((AX, 128), 0)
    gy = sc[14] - FSWEEPS + row24
    inside = (gy >= 0) & (gy < ny)

    def build(dest, values16):
        gx = sc[13] - FSWEEPS + dest
        good = inside & (gx >= 0) & (gx < nx)
        every = []
        for q in range(8):
            j = q // 2
            a = s1[dest, 8 * j : 8 * j + 8]
            b = s2[dest, 8 * j : 8 * j + 8]
            low, high = jnp.where(low_first, a, b), jnp.where(low_first, b, a)
            if q % 2 == 0:
                high = row_roll(high, 4)
            else:
                low = row_roll(low, 4)
            t0, t1 = row_roll(values16[q][0:8], 4), row_roll(values16[q][8:16], 4)
            tall = jnp.concatenate(
                [jnp.where(sub < 4, low, t0), jnp.where(sub < 4, t0, t1), jnp.where(sub < 4, t1, high)], axis=0
            )
            every.append(jnp.where(good, tall, 0.0))
        for k in range(3):
            ua[k, dest] = every[k]
            fo[k, dest] = every[3 + k]
        mo[dest] = every[6]
        side = []
        for channels in ((0, 1, 2), (3, 4, 5)):
            main, far = jnp.zeros((AX, 128), F32), jnp.zeros((AX, 128), F32)
            for k, c in enumerate(channels):
                main = jnp.where(group == k, lane_roll(every[c], 32 * k - w0), main)
                far = jnp.where(group == k, lane_roll(every[7], 32 * k + zoff - w0 - DEEP * c), far)
            side.append(jnp.where(main_ok, main, jnp.where(far_ok, far, 0.0)))
        ba[dest], bf[dest] = side
        main = jnp.where(main_ok, lane_roll(every[6], -w0), jnp.where(far_ok, lane_roll(every[7], zoff - w0 - DEEP * 6), 0.0))
        first = jnp.where(group == 0, main, 0.0)
        first = jnp.where(group == 1, lane_roll(main, 32), first)
        bm[dest] = jnp.where(group == 2, lane_roll(main, 64), first)

    def inner_plane(i):
        build(i + FSWEEPS, [u[k, i] for k in range(3)] + [f[k, i] for k in range(3)] + [m[i], strip[i]])

    loop(0, BX, inner_plane, 4)

    def outer_plane(i):
        for a, b, sa, sb, start, dest in (
            (x1, x2, strip2, strip1, lead, i), (x2, x1, strip1, strip2, 0, i + FSWEEPS + BX),
        ):
            j = i + start
            force = j - (1 if start else 0)

            def pick(index):
                return jnp.where(low_first, a[index], b[index])

            build(
                dest,
                [pick(k * DEEP + j) for k in range(3)]
                + [pick(3 * DEEP + k * (DEEP - 1) + force) for k in range(3)]
                + [pick(PLANES - DEEP + j), jnp.where(low_first, sa[j], sb[j])],
            )

    loop(0, FSWEEPS, outer_plane, 2)

    def edge(values, k):
        return jnp.where(at_edge, lane_roll(values, edge_lane - edge_from - 32 * k), 0.0)

    def faces(i):
        here, there = mo[i], bm[i]
        cx[i] = 0.5 * (here + mo[jnp.minimum(i + 1, AX - 1)])
        bx[i] = 0.5 * (there + bm[jnp.minimum(i + 1, AX - 1)])
        cy[i] = 0.5 * (here + row_roll(here, -1))
        by[i] = 0.5 * (there + row_roll(there, -1))
        bz[i] = 0.5 * (there + lane_roll(there, -1))
        zu[i] = jnp.where(lane == BZ - 1, 0.0, 0.5 * (here + lane_roll(here, -1)))
        zd[i] = jnp.where(lane == 0, 0.0, 0.5 * (here + lane_roll(here, 1)))
        ze[i] = jnp.where(at_edge, 0.5 * (here + edge(there, 0)), 0.0)

    loop(0, AX, faces, 12)
    side_inside = (sc[15] + z >= 0) & (sc[15] + z < nz)
    far_edge = BZ - 1 - edge_lane

    def scale(i):
        open_face = jnp.where(lane == far_edge, 0.5 * mo[i], 0.0)
        total = MASS_TERM + cx[i] + cx[i - 1] + cy[i] + row_roll(cy[i], 1) + zu[i] + zd[i] + ze[i] + open_face
        gx = sc[13] - FSWEEPS + i
        good = inside & (gx >= 0) & (gx < nx)
        iv[i] = jnp.where(good, 1.0 / total, 0.0)
        total = MASS_TERM + bx[i] + bx[i - 1] + by[i] + row_roll(by[i], 1) + bz[i] + lane_roll(bz[i], 1)
        bi[i] = jnp.where(good & side_inside, 1.0 / total, 0.0)

    loop(1, AX - 1, scale, 11)
    for sweep in range(FSWEEPS):
        src, dst = (ua, ub) if sweep % 2 == 0 else (ub, ua)
        bsrc, bdst = (ba, bb) if sweep % 2 == 0 else (bb, ba)

        def relax(i, src=src, dst=dst, bsrc=bsrc, bdst=bdst, last=sweep == FSWEEPS - 1):
            there = bsrc[i]
            for k in range(3):
                here = src[k, i]
                total = fo[k, i] + cx[i] * src[k, i + 1] + cx[i - 1] * src[k, i - 1]
                total = total + cy[i] * row_roll(here, -1) + row_roll(cy[i] * here, 1)
                total = total + zu[i] * lane_roll(here, -1) + zd[i] * lane_roll(here, 1) + ze[i] * edge(there, k)
                total = total * iv[i]
                if last:
                    out[k, i - FSWEEPS] = row_roll(total, -FSWEEPS)[0:BY]
                else:
                    dst[k, i] = total
            if not last:
                total = bf[i] + bx[i] * bsrc[i + 1] + bx[i - 1] * bsrc[i - 1]
                total = total + by[i] * row_roll(there, -1) + row_roll(by[i] * there, 1)
                total = total + bz[i] * lane_roll(there, -1) + lane_roll(bz[i] * there, 1)
                bdst[i] = total * bi[i]

        loop(sweep + 1, AX - 1 - sweep, relax, AX - 2 - 2 * sweep)


def taper(offset):
    folded = jnp.minimum(offset, SPAN - 1 - offset)
    total = jnp.zeros(offset.shape, F32)
    for n in range(PC):
        total = jnp.where(folded == float(n), math.sin(math.pi * (n + 0.5) / SPAN), total)
    return total


def contribution(sc, delta, start, planes):
    rows = 16 if planes > 8 else 8
    laneix = iota((rows, 128), 1)
    lane16i = iota((16, 128), 1)
    lane_y = div10(lane16i).astype(F32)
    rows128 = iota((128, 128), 0)
    rows_z = (rows128 - PC * div10(rows128)).astype(F32)

    def place(axis):
        return delta[PC : PC + 1, axis : axis + 1] - sc[13 + axis].astype(F32)

    off_x = (iota((rows, 128), 0) + start).astype(F32) - place(0)
    apart = off_x - 2.0 * laneix.astype(F32)
    choose = jnp.where((apart >= 0.0) & (apart < 2.0) & (laneix < PC), 1.0, 0.0).astype(BF16)[:, 0:16]
    picked = [lax.dot_general(choose, p, (((1,), (0,)), ((), ())), preferred_element_type=F32) for p in three_parts(delta)]
    lines = (picked[0] + picked[1] + picked[2]) * taper(off_x)
    off_y = iota((16, 128), 0).astype(F32) - place(1)
    apart = off_y - 2.0 * lane_y
    cover = jnp.where((apart >= 0.0) & (apart < 2.0) & (lane16i < PC * PC), taper(off_y), 0.0)
    off_z = iota((128, 128), 1).astype(F32) - place(2)
    apart = off_z - 2.0 * rows_z
    expand = jnp.where((apart >= 0.0) & (apart < 2.0) & (rows128 < PC * PC), 1.0, 0.0).astype(BF16)
    tall = jnp.concatenate([jnp.broadcast_to(lines[x : x + 1, :], (BY, 128)) * cover for x in range(planes)], axis=0)
    return dot_exact(tall, expand) * taper(off_z[0:1, :])


def near_kernel(sc, parts, acc):
    acc[...] = jnp.zeros(acc.shape, F32)

    def add(n):
        acc[...] += contribution(sc, parts[n], 0, BX)

    loop(0, parts.shape[0], add, 6)


def final_kernel(sc, m, near, parts1, parts2, out, acc):
    acc[...] = near[...]
    reach = HALO - 1
    start1 = jnp.where(sc[0] == 0, 0, BX - reach)
    start2 = BX - reach - start1

    def add(n):
        for parts, start in ((parts1, start1), (parts2, start2)):
            where = pl.ds(pl.multiple_of(start * BY, BY), reach * BY)
            acc[where, :] += contribution(sc, parts[n], start, reach)

    loop(0, parts1.shape[0], add, 6)
    for x in range(BX):
        out[x] = m[x] * (1.0 + acc[16 * x : 16 * x + 16, :])


def call(kernel, shapes, scratch, inputs, flops, space=pltpu.VMEM, limit=VMEM_LIMIT):
    specs = [pl.BlockSpec(memory_space=pltpu.SMEM)] + [pl.BlockSpec(memory_space=space)] * (len(inputs) - 1)
    single = not isinstance(shapes, list)
    outs = [jax.ShapeDtypeStruct(s, F32) for s in ([shapes] if single else shapes)]
    results = pl.pallas_call(
        kernel,
        out_shape=outs,
        in_specs=specs,
        out_specs=[pl.BlockSpec(memory_space=pltpu.VMEM)] * len(outs),
        scratch_shapes=[pltpu.VMEM(s, F32) if isinstance(s, tuple) else s for s in scratch],
        compiler_params=pltpu.CompilerParams(vmem_limit_bytes=limit),
        cost_estimate=pl.CostEstimate(flops=flops, bytes_accessed=1 << 20, transcendentals=0),
    )(*inputs)
    return results[0] if single else results


def body(forcing, start_field, modulus, corners):
    counts = tuple(lax.axis_size(axis) for axis in AXES)
    sizes = (counts[0] * BX, counts[1] * BY, counts[2] * BZ)
    place = tuple(lax.axis_index(axis) for axis in AXES)
    gz = place[2].astype(jnp.int32)
    lower = jnp.stack([place[0] * BX, place[1] * BY, place[2] * BZ]).astype(jnp.int32)

    def send(values, move):
        pairs = []
        for x in range(counts[0]):
            for y in range(counts[1]):
                for z in range(counts[2]):
                    to = [t % c for t, c in zip(move(x, y, z), counts)]
                    pairs.append(((x * counts[1] + y) * counts[2] + z, (to[0] * counts[1] + to[1]) * counts[2] + to[2]))
        return lax.ppermute(values, AXES, pairs)

    def turn(z):
        return 1 if z == 0 else -1

    relative = corners[0] - lower
    near = jnp.broadcast_to(relative[None, :], (1, 3))
    want1 = send(near, lambda x, y, z: (x, y - turn(z), z))
    want2 = send(near, lambda x, y, z: (x, y + turn(z), z))
    scalar = jnp.concatenate([gz[None], relative, want1[0], want2[0], corners[0], lower]).astype(jnp.int32)
    first = gz[None]

    msg1, msg2, strip, strip1, strip2 = call(
        edge_kernel,
        [(PLANES, BY, 128), (PLANES, BY, 128), (BX, BY, 128), (DEEP, BY, 128), (DEEP, BY, 128)],
        [(3, BX, BY, BZ), (3, BX, BY, BZ), (BX, BY, BZ), pltpu.SemaphoreType.DMA((3,))],
        [first, start_field, forcing, modulus],
        1 << 20,
        pltpu.HBM,
        LARGE_LIMIT,
    )
    x1 = send(msg1, lambda x, y, z: (x + turn(z), y, z))
    x2 = send(msg2, lambda x, y, z: (x - turn(z), y, z))
    far_strip = send(strip, lambda x, y, z: (x, y, 1 - z))
    far1 = send(strip1, lambda x, y, z: (x + turn(z), y, 1 - z))
    far2 = send(strip2, lambda x, y, z: (x - turn(z), y, 1 - z))
    spread = [scalar, start_field, forcing, modulus, x1, x2, far_strip, far1, far2]
    a1, a2 = call(side_kernel, [(AX, 32, 128)] * 2, [], spread, 1 << 20)
    b1 = send(a1, lambda x, y, z: (x, y + turn(z), z))
    b2 = send(a2, lambda x, y, z: (x, y - turn(z), z))
    own_u, own_f, y1, y2 = call(
        pack_kernel,
        [(WIN, BY, 128)] * 2 + [(WIN // 2, 40, 128)] * 2,
        [(3, 36, BY, 128), (3, 36, BY, 128), (36, BY, 128), (36, BY, 128)],
        spread,
        1 << 31,
    )
    r1 = send(y1, lambda x, y, z: (x, y + turn(z), z))
    r2 = send(y2, lambda x, y, z: (x, y - turn(z), z))
    wide = (AX, AX, 128)
    displacement = call(
        functools.partial(field_kernel, sizes),
        (3, BX, BY, BZ),
        [(3,) + wide] * 3 + [wide] * 15,
        spread + [b1, b2],
        1 << 32,
    )
    own_u, own_f, r1, r2, displacement = lax.optimization_barrier((own_u, own_f, r1, r2, displacement))
    window = (WIN, WY, 128)
    delta = call(
        functools.partial(zone_kernel, sizes),
        (16, 128),
        [window] * 8
        + [
            (8, 3, 16, 128), (13, 16, 128), (5, 16, 128), (5, 16, 128), (2, 16, 128), (16, 128),
            (PC, 128, 128), (5, 2, 128, 128), (5, 2, 128, 128), (2, 5, 256, 128), (2, 5, 8, 128), (PC, 8, 128), (PC, 8, 128),
        ],
        [scalar, own_u, own_f, r1, r2],
        1 << 33,
    )
    beside = [delta, send(delta, lambda x, y, z: (x, y, 1 - z))]
    for step in (1, -1):
        beside.append(send(delta, lambda x, y, z, step=step: (x, y + step * turn(z), z)))
        beside.append(send(delta, lambda x, y, z, step=step: (x, y + step * turn(z), 1 - z)))
    plane = jnp.stack(beside)
    after = send(plane, lambda x, y, z: (x + turn(z), y, z))
    before = send(plane, lambda x, y, z: (x - turn(z), y, z))
    near = call(near_kernel, (BX * BY, 128), [], [scalar, plane], 1 << 29)
    near, after, before = lax.optimization_barrier((near, after, before))
    new_modulus = call(
        final_kernel, (BX, BY, BZ), [(BX * BY, 128)], [scalar, modulus, near, after, before], 1 << 24
    )
    return displacement, new_modulus


def solution(mesh):
    placed = (
        P(None, "gx", "gy", "gz"),
        P(None, "gx", "gy", "gz"),
        P("gx", "gy", "gz"),
        P(("gx", "gy", "gz"), None),
    )
    return jax.shard_map(
        body,
        mesh=mesh,
        in_specs=placed,
        out_specs=(P(None, "gx", "gy", "gz"), P("gx", "gy", "gz")),
        check_vma=False,
    )
```
